128 devices in a mesh: gx: 8 (over z, core), gy: 16 (over x, y).
Axes of the slice: x: 4, y: 4, z: 4, core: 2. Of those that a mesh axis runs over, the one named last changes fastest.
Arguments:
- ensemble: bfloat16 [10, 90, 128, 4096], P(None, None, 'gx', 'gy'), may hold values from -6 to 6
- vertical_weights: float32 [90, 90], replicated, may hold values from 0 to 1
- dual_vector: float32 [262144], P(('gx', 'gy')), may hold values from -48 to 48
- observed_column: int32 [262144], P(('gx', 'gy')), may hold values from 0 to 524287, as said below
- observed_level: int32 [262144], P(('gx', 'gy')), may hold values from 0 to 89
- active_count: int32 [128], P(('gx', 'gy')), may hold values from 1024 to 2048, as said below
Outputs:
- increment: float32 [90, 128, 4096], P(None, 'gx', 'gy')
- obs_product: float32 [262144], P(('gx', 'gy'))
The draws below stay inside these ranges and needn't reach their ends.
Inputs may be any that keep to these rules, and one draw needn't show every extreme that they name: `active_count`: some device has all 2048 slots active. `observed_column`: over the active slots of one device, at most 48 columns lie in any one device's tile (16 rows by 256 columns); in every draw one tile receives exactly 48 from every device.
All inputs are finite; a program needn't handle non-finite values.
Results may differ from the reference program's by a relative error of at most 0.0003.
Values sent between devices are 32-bit elements; how exact they have to be, the bound alone decides.
No kernel may reach another device: no remote copies, remote signals or barrier semaphores. Data moves between devices by JAX's collectives and lax.ppermute only.
A program may use at most 640 MiB of HBM per device.

```python
import jax
import jax.numpy as jnp
from jax import lax

MEM = 10
LEV = 90
DIFF_STEPS = 3
CX_DEV = 16
CY_DEV = 256
OBS_DEV = 2048
NX = 128
NY = 4096
OBS_ALL = 262144
N_GX = 8
N_GY = 16


def counts_helper(key):
    devices = N_GX * N_GY
    key = jax.random.fold_in(key, 11)
    first, second = jax.random.split(key)
    counts = jax.random.randint(first, (devices,), OBS_DEV // 2, OBS_DEV + 1)
    fullest = jax.random.randint(second, (), 0, devices)
    return jnp.where(jnp.arange(devices) == fullest, OBS_DEV, counts).astype(jnp.int32)


def draw_active_count(key, part):
    return counts_helper(key)


def draw_observed_column(key, part):
    devices = N_GX * N_GY
    capacity = 3 * OBS_DEV // devices
    counts = counts_helper(key)
    key = jax.random.fold_in(key, 23)
    key_hot, key_shift, key_perm, key_row, key_col = jax.random.split(key, 5)
    hottest = jax.random.randint(key_hot, (), 0, devices)
    shifts = jax.random.randint(key_shift, (devices,), 0, devices - 1)
    position = jnp.arange(OBS_DEV, dtype=jnp.int32)

    def one_source(count, shift, subkey):
        others = (position - capacity + shift) % (devices - 1)
        listed = jnp.where(position < capacity, hottest, (hottest + 1 + others) % devices)
        scores = jnp.where(position < count, jax.random.permutation(subkey, OBS_DEV).astype(jnp.int32), OBS_DEV + position)
        ordering = jnp.argsort(scores, stable=True)
        return jnp.zeros((OBS_DEV,), jnp.int32).at[ordering].set(listed.astype(jnp.int32))
    subkeys = jax.random.split(key_perm, devices)
    target = jax.vmap(one_source)(counts, shifts, subkeys)
    local_row = jax.random.randint(key_row, (devices, OBS_DEV), 0, CX_DEV)
    local_col = jax.random.randint(key_col, (devices, OBS_DEV), 0, CY_DEV)
    global_row = target // N_GY * CX_DEV + local_row
    global_col = target % N_GY * CY_DEV + local_col
    return (global_row * (CY_DEV * N_GY) + global_col).reshape(-1).astype(jnp.int32)


def draw_vertical_weights(key, part):
    key = jax.random.fold_in(key, 37)
    level = jnp.arange(LEV)
    spacing = jnp.abs(level[:, None] - level[None, :]).astype(jnp.float32)
    factor = jax.random.uniform(key, (LEV, LEV), jnp.float32, 0.5, 1.5)
    return jnp.where(spacing == 0.0, 1.0, factor * jnp.exp(-spacing / 6.0) / 4.0).astype(jnp.float32)


def set_ends(entries, own_key, least, top_value):
    longest = entries.shape.index(max(entries.shape))
    spots = []
    for shift in (0, 1):
        where = [jax.random.randint(jax.random.fold_in(own_key, axis), (), 0, length) for axis, length in enumerate(entries.shape)]
        where[longest] = (where[longest] + shift) % entries.shape[longest]
        spots.append(tuple(where))
    return entries.at[spots[0]].set(least).at[spots[1]].set(top_value)


def level_of(stream_key, dims, pieces, least, top_value):
    factor_of, own = 1.0, jax.random.fold_in(stream_key, 6)
    for dim, parts in pieces:
        heights = jnp.exp(jax.random.uniform(jax.random.fold_in(own, dim), (parts,), jnp.float32, least / len(pieces), top_value / len(pieces)))
        factor_of = factor_of * jnp.repeat(heights, dims[dim] // parts).reshape([-1 if axis == dim else 1 for axis in range(len(dims))])
    return factor_of


def scatter_about(key, dims, scale, bound, cuts=(), held_as=jnp.bfloat16):
    entries = jax.random.normal(key, dims, jnp.float32) * scale
    if len(cuts) > 0:
        entries = level_of(key, dims, cuts, -0.22, 0.18) * entries
    return jnp.clip(entries, min=-bound, max=bound).astype(held_as)


def setup_inputs(seed: int = 0) -> dict:
    splits = jax.random.split(jax.random.key(seed), 7)
    ensemble = scatter_about(splits[0], (MEM, LEV, NX, NY), 1.0, 6.0, ((2, 8), (3, 16)))
    vertical_weights = draw_vertical_weights(jax.random.fold_in(splits[6], 71), 0)
    dual_vector = scatter_about(splits[2], (OBS_ALL,), 8.0, 48.0, ((0, 128),), jnp.float32)
    observed_column = draw_observed_column(jax.random.fold_in(splits[6], 71), 0)
    observed_level = set_ends(jax.random.randint(splits[4], (OBS_ALL,), 0, LEV), jax.random.fold_in(splits[4], 1), 0, LEV - 1).astype(jnp.int32)
    active_count = draw_active_count(jax.random.fold_in(splits[6], 71), 0)
    return {"ensemble": ensemble, "vertical_weights": vertical_weights, "dual_vector": dual_vector, "observed_column": observed_column, "observed_level": observed_level, "active_count": active_count}


diffusivity = 0.24


def diffuse_once(padded):
    centre = padded[:, 1:-1, 1:-1]
    beside_all = padded[:, 2:, 1:-1] + padded[:, :-2, 1:-1] + padded[:, 1:-1, 2:] + padded[:, 1:-1, :-2]
    return centre + diffusivity * (beside_all - 4.0 * centre)


def reference(ensemble, vertical_weights, dual_vector, observed_column, observed_level, active_count):
    slot_number = jnp.arange(OBS_DEV * N_GX * N_GY, dtype=jnp.int32)
    active = (slot_number % OBS_DEV) < active_count[slot_number // OBS_DEV]
    flat_index = (observed_level * (NX * NY) + observed_column).astype(jnp.int32)
    amount = jnp.where(active, dual_vector, 0.0)
    adjoint = jnp.zeros((LEV * NX * NY,), jnp.float32).at[flat_index].add(amount).reshape(LEV, NX * NY)

    def member_term(running, member):
        wide = member.astype(jnp.float32)
        spread = wide.reshape(LEV, NX * NY) * adjoint
        smoothed = jnp.dot(vertical_weights, spread, preferred_element_type=jnp.float32, precision=lax.Precision.HIGHEST).reshape(LEV, NX, NY)
        for repeat in range(DIFF_STEPS):
            smoothed = diffuse_once(jnp.pad(smoothed, ((0, 0), (1, 1), (1, 1))))
        return running + wide * smoothed, None

    summed, unused = lax.scan(member_term, jnp.zeros((LEV, NX, NY), jnp.float32), ensemble)
    increment = summed / (MEM - 1)
    picked = increment.reshape(-1)[flat_index]
    obs_product = jnp.where(active, picked, 0.0)
    return increment, obs_product
```

```python
import jax
import jax.numpy as jnp
import numpy as np
from jax import lax
from jax.experimental import pallas as pl
from jax.experimental.pallas import tpu as pltpu
from jax.sharding import PartitionSpec as P

F32 = jnp.float32
BF16 = jnp.bfloat16
I32 = jnp.int32

MEM, LEV, ROWS, COLS = 10, 90, 16, 256
PAD = 96
DEV = 128
CAP = 48
SLOTS = 2048
HALF = 128
EDGE = 3
STRIP = 18
PER_HALF = 5
SELF = 1.0 / 6.0
SCALE = 0.24**3 / (MEM - 1)
VMEM = 56 * 1024 * 1024


def split(value, count):
    parts = []
    for _ in range(count - 1):
        top = value.astype(BF16)
        parts.append(top)
        value = value - top.astype(F32)
    parts.append(value.astype(BF16))
    return parts


def dot(a, b):
    return lax.dot_general(a, b, (((1,), (0,)), ((), ())), preferred_element_type=F32)


def dot_nt(a, b):
    return lax.dot_general(a, b, (((1,), (1,)), ((), ())), preferred_element_type=F32)


def iota(shape, dim):
    return lax.broadcasted_iota(I32, shape, dim)


def one_hot(test):
    return jnp.where(test, 1.0, 0.0).astype(BF16)


def params(**kw):
    return pltpu.CompilerParams(vmem_limit_bytes=VMEM, **kw)


def cost(flops, moved):
    return pl.CostEstimate(flops=flops, bytes_accessed=moved, transcendentals=0)


def pack_kernel(count, dual, col, lev, upper, out, tgt_out, rank_out, left_v, left_c, right_v, right_c):
    number = count[0]
    rows = iota((DEV, HALF), 0)
    lane = iota((1, HALF), 1)
    carry = jnp.zeros((DEV, HALF), F32)
    for i in range(SLOTS // HALF):
        at = slice(i * HALF, (i + 1) * HALF)
        column = col[i : i + 1, :]
        row = column >> 12
        gcol = column & 4095
        y = gcol & 255
        y = ((y & 1) << 7) + (y >> 1)
        target = ((row >> 4) << 4) + (gcol >> 8)
        target = jnp.where(i * HALF + lane < number, target, -1)
        hit = rows == target
        both = dot(one_hot(hit), upper[...])
        rank = jnp.sum(jnp.where(hit, both[:, :HALF] + carry, 0.0), axis=0, keepdims=True)
        carry = carry + both[:, HALF:]
        tgt_out[i : i + 1, :] = target
        rank = rank.astype(I32)
        rank_out[i : i + 1, :] = rank
        right_v[:, at] = one_hot(rows == rank)
        right_c[:, at] = one_hot(rows == rank + CAP)
        values = dual[i : i + 1, :]
        for p, piece in enumerate(split(values, 3)):
            left_v[p * DEV : (p + 1) * DEV, at] = jnp.where(hit, piece.astype(F32), 0.0).astype(BF16)
        cells = (lev[i : i + 1, :] << 12, (row & 15) << 8, y)
        for p, piece in enumerate(cells):
            left_c[p * DEV : (p + 1) * DEV, at] = jnp.where(hit, piece.astype(F32), 0.0).astype(BF16)
    a = dot_nt(left_v[...], right_v[...])
    b = dot_nt(left_c[...], right_c[...])
    out[...] = ((a[:DEV] + a[DEV : 2 * DEV]) + a[2 * DEV :]) + ((b[:DEV] + b[DEV : 2 * DEV]) + b[2 * DEV :])


def pack(count, dual, col, lev):
    upper = np.concatenate([np.triu(np.ones((HALF, HALF)), 1), np.ones((HALF, HALF))], 1)
    spec = pl.BlockSpec(memory_space=pltpu.VMEM)
    return pl.pallas_call(
        pack_kernel,
        name="pack",
        out_shape=(
            jax.ShapeDtypeStruct((DEV, HALF), F32),
            jax.ShapeDtypeStruct((SLOTS // HALF, HALF), I32),
            jax.ShapeDtypeStruct((SLOTS // HALF, HALF), I32),
        ),
        in_specs=[pl.BlockSpec(memory_space=pltpu.SMEM)] + [spec] * 4,
        out_specs=(spec,) * 3,
        scratch_shapes=[pltpu.VMEM((3 * DEV, SLOTS), BF16)] * 2 + [pltpu.VMEM((DEV, SLOTS), BF16)] * 2,
        compiler_params=params(),
        cost_estimate=cost(10**9, 10**6),
    )(count, dual.reshape(-1, HALF), col.reshape(-1, HALF), lev.reshape(-1, HALF), jnp.asarray(upper, BF16))


def unpack_kernel(back, tgt, rank, out):
    rows = iota((DEV, HALF), 0)
    table = jnp.concatenate(split(back[...], 3), axis=0)
    for i in range(SLOTS // HALF):
        found = dot(table, one_hot(rows == rank[i : i + 1, :]))
        found = (found[:DEV] + found[DEV : 2 * DEV]) + found[2 * DEV :]
        out[i : i + 1, :] = jnp.sum(jnp.where(rows == tgt[i : i + 1, :], found, 0.0), axis=0, keepdims=True)


def unpack(back, tgt, rank):
    spec = pl.BlockSpec(memory_space=pltpu.VMEM)
    return pl.pallas_call(
        unpack_kernel,
        name="unpack",
        out_shape=jax.ShapeDtypeStruct((SLOTS // HALF, HALF), F32),
        in_specs=[spec] * 3,
        out_specs=spec,
        compiler_params=params(),
        cost_estimate=cost(10**8, 10**5),
    )(back, tgt, rank).reshape(SLOTS)


def strip_lane(member):
    return member // PER_HALF * HALF + member % PER_HALF * STRIP


def natural(permuted):
    return ((permuted & 127) << 1) + (permuted >> 7)


def arrange_kernel(ens, perm_y, perm_r, out, up, down, strip, side, strip_acc, side_acc):
    k = pl.program_id(0)

    @pl.when(k == 0)
    def _():
        strip_acc[...] = jnp.zeros_like(strip_acc)
        side_acc[...] = jnp.zeros_like(side_acc)

    base = k // PER_HALF * HALF + k % PER_HALF * STRIP
    y = natural(iota((COLS, COLS), 0))
    lane = iota((COLS, COLS), 1)
    want = jnp.where(y < 6, base + 3 + y, jnp.where(y >= 250, base + y - 241, -1))
    select = one_hot(lane == want)
    want = jnp.where(y < 3, 3 * k + y, jnp.where(y >= 253, HALF + 3 * k + y - 253, -1))
    select = jnp.concatenate([select, one_hot(lane == want)], axis=1)
    for b in range(6):
        if b < 5:
            block = ens[0, b * 256 : (b + 1) * 256, :]
        else:
            block = jnp.concatenate([ens[0, 1280:1440, :], jnp.zeros((96, COLS), BF16)], axis=0)
        block = dot(block, perm_y[...]).astype(BF16)
        turned = dot(perm_r[...], block)
        edges = dot(turned.astype(BF16), select)
        at = slice(b * 16, (b + 1) * 16)
        for x in range(ROWS):
            part = turned[x * 16 : (x + 1) * 16, :]
            out[0, x, at, :] = part.astype(BF16)
            if x < EDGE:
                up[0, x, at, :] = part
            if x >= ROWS - EDGE:
                down[0, x - (ROWS - EDGE), at, :] = part
            strip_acc[x, at, :] += edges[x * 16 : (x + 1) * 16, :COLS]
            side_acc[x, at, :] += edges[x * 16 : (x + 1) * 16, COLS:]

    @pl.when(k == MEM - 1)
    def _():
        strip[...] = strip_acc[...].astype(BF16)
        side[0] = side_acc[:, :, :HALF]
        side[1] = side_acc[:, :, HALF:]


def arrange(ensemble):
    y = np.arange(COLS)
    perm_y = np.zeros((COLS, COLS))
    perm_y[y, (y % 2) * HALF + y // 2] = 1
    perm_r = np.zeros((256, 256))
    i = np.arange(256)
    perm_r[i % 16 * 16 + i // 16, i] = 1
    whole = pl.BlockSpec((256, 256), lambda k: (0, 0))
    return pl.pallas_call(
        arrange_kernel,
        name="arrange",
        grid=(MEM,),
        out_shape=(
            jax.ShapeDtypeStruct((MEM, ROWS, PAD, COLS), BF16),
            jax.ShapeDtypeStruct((MEM, EDGE, PAD, COLS), F32),
            jax.ShapeDtypeStruct((MEM, EDGE, PAD, COLS), F32),
            jax.ShapeDtypeStruct((ROWS, PAD, COLS), BF16),
            jax.ShapeDtypeStruct((2, ROWS, PAD, HALF), F32),
        ),
        in_specs=[pl.BlockSpec((1, LEV * ROWS, COLS), lambda k: (k, 0, 0)), whole, whole],
        out_specs=(
            pl.BlockSpec((1, ROWS, PAD, COLS), lambda k: (k, 0, 0, 0)),
            pl.BlockSpec((1, EDGE, PAD, COLS), lambda k: (k, 0, 0, 0)),
            pl.BlockSpec((1, EDGE, PAD, COLS), lambda k: (k, 0, 0, 0)),
            pl.BlockSpec((ROWS, PAD, COLS), lambda k: (0, 0, 0)),
            pl.BlockSpec((2, ROWS, PAD, HALF), lambda k: (0, 0, 0, 0)),
        ),
        scratch_shapes=[pltpu.VMEM((ROWS, PAD, COLS), F32)] * 2,
        compiler_params=params(),
        cost_estimate=cost(10**10, 25 * 10**6),
    )(ensemble.reshape(MEM, LEV * ROWS, COLS), jnp.asarray(perm_y, BF16), jnp.asarray(perm_r, BF16))


def strip_kernel(strip, left, right, out, up, down):
    from_lane = iota((HALF, COLS), 0)
    k, c = from_lane // 3, from_lane % 3
    base = k // PER_HALF * HALF + k % PER_HALF * STRIP
    lane = iota((HALF, COLS), 1)
    good = from_lane < 3 * MEM
    place_l = one_hot((lane == base + c) & good)
    place_r = one_hot((lane == base + 15 + c) & good)
    for x in range(ROWS):
        value = strip[x].astype(F32) + dot(left[0, x].astype(BF16), place_l) + dot(right[0, x].astype(BF16), place_r)
        out[x] = value.astype(BF16)
        if x < EDGE:
            up[x] = value
        if x >= ROWS - EDGE:
            down[x - (ROWS - EDGE)] = value


def complete_strip(strip, left, right):
    spec = pl.BlockSpec(memory_space=pltpu.VMEM)
    return pl.pallas_call(
        strip_kernel,
        name="complete_strip",
        out_shape=(
            jax.ShapeDtypeStruct((ROWS, PAD, COLS), BF16),
            jax.ShapeDtypeStruct((EDGE, PAD, COLS), F32),
            jax.ShapeDtypeStruct((EDGE, PAD, COLS), F32),
        ),
        in_specs=[spec] * 3,
        out_specs=(spec,) * 3,
        compiler_params=params(),
        cost_estimate=cost(10**9, 4 * 10**6),
    )(strip, left, right)


KTILE = 1024


def scatter_kernel(incoming, out, sides, turned, hot1, hot2, acc):
    turned[...] = incoming[...].T
    acc[...] = jnp.zeros_like(acc)
    rows1 = iota((4 * PAD, HALF), 0)
    rows2 = iota((4 * COLS, HALF), 0)

    @pl.loop(0, CAP // 8)
    def _(j):
        first = pl.multiple_of(j * 8, 8)
        values = turned[pl.ds(first, 8), :]
        cells = turned[pl.ds(CAP + first, 8), :].astype(I32)
        for q in range(8):
            at = slice(q * HALF, (q + 1) * HALF)
            cell = cells[q : q + 1, :]
            key1 = ((cell >> 10) & 3) * PAD + (cell >> 12)
            hit = rows1 == key1
            for p, piece in enumerate(split(values[q : q + 1, :], 2)):
                hot1[p * 4 * PAD : (p + 1) * 4 * PAD, at] = jnp.where(hit, piece.astype(F32), 0.0).astype(BF16)
            hot2[:, at] = one_hot(rows2 == (cell & 1023))
        for n in range(4):
            cols = slice(n * COLS, (n + 1) * COLS)
            acc[:, cols] += dot_nt(hot1[...], hot2[cols, :])

    y = natural(iota((COLS, COLS), 0))
    lane = iota((COLS, COLS), 1)
    place = jnp.where(y < 3, y, jnp.where(y >= 253, HALF + y - 253, -1000))
    packed = jnp.zeros((PAD, COLS), F32)
    for x in range(ROWS):
        cols = slice(x % 4 * COLS, (x % 4 + 1) * COLS)
        level = x // 4 * PAD
        value = acc[level : level + PAD, cols] + acc[4 * PAD + level : 4 * PAD + level + PAD, cols]
        out[x] = value
        select = one_hot(lane == place + 3 * x)
        for piece in split(value, 2):
            packed = packed + dot(piece, select)
    sides[0] = packed[:, :HALF]
    sides[1] = packed[:, HALF:]


def scatter(incoming):
    spec = pl.BlockSpec(memory_space=pltpu.VMEM)
    return pl.pallas_call(
        scatter_kernel,
        name="scatter",
        out_shape=(
            jax.ShapeDtypeStruct((ROWS, PAD, COLS), F32),
            jax.ShapeDtypeStruct((2, PAD, HALF), F32),
        ),
        in_specs=[spec],
        out_specs=(spec,) * 2,
        scratch_shapes=[
            pltpu.VMEM((HALF, DEV), F32),
            pltpu.VMEM((8 * PAD, KTILE), BF16),
            pltpu.VMEM((4 * COLS, KTILE), BF16),
            pltpu.VMEM((8 * PAD, 4 * COLS), F32),
        ],
        compiler_params=params(),
        cost_estimate=cost(10**10, 2 * 10**6),
    )(incoming)


def adjoint_strip_kernel(adjoint, left, right, out, up, down):
    lane = iota((COLS, COLS), 1)
    member_c = jnp.where(lane % HALF < PER_HALF * STRIP, lane % HALF % STRIP, -1)
    y = natural(iota((COLS, COLS), 0))
    own = one_hot(member_c == jnp.where(y < 6, 3 + y, jnp.where(y >= 250, y - 241, -2)))
    from_lane = iota((HALF, COLS), 0)
    member_c = member_c[:HALF]
    for x in range(ROWS):
        c = from_lane - 3 * x
        good = (c >= 0) & (c < 3)
        place_l = one_hot(good & (member_c == c))
        place_r = one_hot(good & (member_c == c + 15))
        value = jnp.zeros((PAD, COLS), F32)
        for source, place in ((adjoint[x], own), (left[0], place_l), (right[0], place_r)):
            for piece in split(source, 2):
                value = value + dot(piece, place)
        out[x] = value
        if x < EDGE:
            up[x] = adjoint[x]
            up[EDGE + x] = value
        if x >= ROWS - EDGE:
            down[x - (ROWS - EDGE)] = adjoint[x]
            down[x - (ROWS - EDGE) + EDGE] = value


def adjoint_strip(adjoint, left, right):
    spec = pl.BlockSpec(memory_space=pltpu.VMEM)
    return pl.pallas_call(
        adjoint_strip_kernel,
        name="adjoint_strip",
        out_shape=(
            jax.ShapeDtypeStruct((ROWS, PAD, COLS), F32),
            jax.ShapeDtypeStruct((2 * EDGE, PAD, COLS), F32),
            jax.ShapeDtypeStruct((2 * EDGE, PAD, COLS), F32),
        ),
        in_specs=[spec] * 3,
        out_specs=(spec,) * 3,
        compiler_params=params(),
        cost_estimate=cost(10**9, 4 * 10**6),
    )(adjoint, left, right)


def beside_permuted(value):
    even, odd = value[:, :HALF], value[:, HALF:]
    return jnp.concatenate([odd + pltpu.roll(odd, 1, 1), even + pltpu.roll(even, HALF - 1, 1)], axis=1)


def beside_natural(value):
    halves = []
    for half in (value[:, :HALF], value[:, HALF:]):
        halves.append(pltpu.roll(half, 1, 1) + pltpu.roll(half, HALF - 1, 1))
    return jnp.concatenate(halves, axis=1)


def total(terms):
    result = None
    for term in terms:
        if term is not None:
            result = term if result is None else result + term
    return result


def diffuse(first, wanted, beside, mask=None):
    rows = first
    for step in range(1, EDGE + 1):
        reach = EDGE - step
        later = {}
        for x in range(min(wanted) - reach, max(wanted) + reach + 1):
            here = rows.get(x)
            terms = [rows.get(x - 1), rows.get(x + 1)]
            if here is not None:
                terms += [beside(here), here * SELF]
            value = total(terms)
            if value is not None:
                later[x] = value if mask is None or step == EDGE else mask(x, value)
        rows = later
    return {x: rows[x] for x in wanted}


def put_split(ref, index, at, value):
    top = value.astype(BF16)
    ref[index, at, :] = top
    ref[index, pl.ds(at.start + PAD, 16), :] = (value - top.astype(F32)).astype(BF16)


def mix(weights, field):
    both = dot(weights, field)
    return both[:PAD] + both[PAD:]


INNER = ROWS - 2 * EDGE


def inner_kernel(ens, adj, weights, ends, before, border, out, field):
    k = pl.program_id(0)

    @pl.when(k == 0)
    def _():
        out[...] = before[...]

    top_open, bottom_open = ends[0], ends[1]

    def mask(x, value):
        if x < 0:
            return value * top_open
        if x >= ROWS:
            return value * bottom_open
        return value

    @pl.loop(0, PAD // 16)
    def _(group):
        at = pl.ds(pl.multiple_of(group * 16, 16), 16)
        spread = {x: ens[0, x, at, :].astype(F32) * adj[x, at, :] for x in range(ROWS)}
        result = diffuse(spread, range(ROWS), beside_permuted, mask)
        for x in range(ROWS):
            if EDGE <= x < ROWS - EDGE:
                put_split(field, x - EDGE, at, result[x])
            else:
                border[0, x if x < EDGE else x - INNER, at, :] = result[x]

    @pl.loop(0, INNER)
    def _(x):
        out[x] += ens[0, x + EDGE].astype(F32) * mix(weights[...], field[x])


def inner(ens, adj, weights, ends, before, first, count):
    resident = lambda *shape: pl.BlockSpec(shape, lambda k: (0,) * len(shape))
    return pl.pallas_call(
        inner_kernel,
        name="inner",
        grid=(count,),
        out_shape=(
            jax.ShapeDtypeStruct((count, 2 * EDGE, PAD, COLS), F32),
            jax.ShapeDtypeStruct((INNER, PAD, COLS), F32),
        ),
        in_specs=[
            pl.BlockSpec((1, ROWS, PAD, COLS), lambda k: (k + first, 0, 0, 0)),
            resident(ROWS, PAD, COLS),
            resident(2 * PAD, 2 * PAD),
            pl.BlockSpec(memory_space=pltpu.SMEM),
            resident(INNER, PAD, COLS),
        ],
        out_specs=(
            pl.BlockSpec((1, 2 * EDGE, PAD, COLS), lambda k: (k, 0, 0, 0)),
            resident(INNER, PAD, COLS),
        ),
        scratch_shapes=[pltpu.VMEM((INNER, 2 * PAD, COLS), BF16)],
        compiler_params=params(),
        cost_estimate=cost(count * 2 * 10**9, count * 2 * 10**6),
    )(ens, adj, weights, ends, before)


def outer_kernel(ens_t, ens_b, halo_t, halo_b, adj_t, adj_b, border, weights, before, out, field):
    k = pl.program_id(0)

    @pl.when(k == 0)
    def _():
        out[...] = before[...]

    @pl.loop(0, PAD // 16)
    def _(group):
        at = pl.ds(pl.multiple_of(group * 16, 16), 16)
        above = {x - EDGE: halo_t[0, x, at, :] * adj_t[x, at, :] for x in range(EDGE)}
        result = diffuse(above, range(EDGE), beside_permuted)
        for x in range(EDGE):
            put_split(field, x, at, result[x] + border[0, x, at, :])
        below = {EDGE + x: halo_b[0, x, at, :] * adj_b[x, at, :] for x in range(EDGE)}
        result = diffuse(below, range(EDGE), beside_permuted)
        for x in range(EDGE):
            put_split(field, EDGE + x, at, result[x] + border[0, EDGE + x, at, :])

    for x in range(EDGE):
        out[x] += ens_t[0, x].astype(F32) * mix(weights[...], field[x])
    for x in range(EDGE):
        out[EDGE + x] += ens_b[0, x + 1].astype(F32) * mix(weights[...], field[EDGE + x])


def outer(ens, halo_t, halo_b, adj_t, adj_b, border, weights, before, first, count):
    resident = lambda *shape: pl.BlockSpec(shape, lambda k: (0,) * len(shape))
    member = lambda rows, at=0, off=0: pl.BlockSpec((1, rows, PAD, COLS), lambda k: (k + off, at, 0, 0))
    return pl.pallas_call(
        outer_kernel,
        name="outer",
        grid=(count,),
        out_shape=jax.ShapeDtypeStruct((2 * EDGE, PAD, COLS), F32),
        in_specs=[
            member(4, 0, first),
            member(4, 3, first),
            member(EDGE),
            member(EDGE),
            resident(EDGE, PAD, COLS),
            resident(EDGE, PAD, COLS),
            member(2 * EDGE),
            resident(2 * PAD, 2 * PAD),
            resident(2 * EDGE, PAD, COLS),
        ],
        out_specs=resident(2 * EDGE, PAD, COLS),
        scratch_shapes=[pltpu.VMEM((2 * EDGE, 2 * PAD, COLS), BF16)],
        compiler_params=params(),
        cost_estimate=cost(count * 10**9, count * 3 * 10**6),
    )(ens, ens, halo_t, halo_b, adj_t, adj_b, border, weights, before)


def edge_kernel(strip, halo_t, halo_b, adj, adj_t, adj_b, weights, ends, open_lanes, inside, border, out, field):
    top_open, bottom_open = ends[0], ends[1]

    @pl.loop(0, PAD // 16)
    def _(group):
        at = pl.ds(pl.multiple_of(group * 16, 16), 16)
        lanes = open_lanes[...]

        def mask(x, value):
            value = value * lanes
            if x < 0:
                return value * top_open
            if x >= ROWS:
                return value * bottom_open
            return value

        spread = {x: strip[x, at, :].astype(F32) * adj[x, at, :] for x in range(ROWS)}
        for x in range(EDGE):
            spread[x - EDGE] = halo_t[x, at, :] * adj_t[x, at, :]
            spread[ROWS + x] = halo_b[x, at, :] * adj_b[x, at, :]
        result = diffuse(spread, range(ROWS), beside_natural, mask)
        for x in range(ROWS):
            put_split(field, x, at, result[x])

    from_lane = iota((COLS, COLS), 0)
    c = jnp.where(from_lane % HALF < PER_HALF * STRIP, from_lane % HALF % STRIP, -1)
    place = jnp.where((c >= 3) & (c < 6), c - 3, jnp.where((c >= 12) & (c < 15), 241 + c, -1))
    y = natural(iota((COLS, COLS), 1))
    collect = one_hot(place == y)
    y = natural(iota((PAD, COLS), 1))
    middle = (y >= EDGE) & (y < COLS - EDGE)
    for x in range(ROWS):
        if EDGE <= x < ROWS - EDGE:
            value = inside[x - EDGE]
        else:
            value = border[x if x < EDGE else x - INNER]
        value = jnp.where(middle, value, 0.0)
        product = strip[x].astype(F32) * mix(weights[...], field[x])
        for piece in split(product, 2):
            value = value + dot(piece, collect)
        out[x] = value * SCALE


def edge(strip, halo_t, halo_b, adj, adj_t, adj_b, weights, ends, open_lanes, inside, border):
    spec = pl.BlockSpec(memory_space=pltpu.VMEM)
    return pl.pallas_call(
        edge_kernel,
        name="edge",
        out_shape=jax.ShapeDtypeStruct((ROWS, PAD, COLS), F32),
        in_specs=[spec] * 7 + [pl.BlockSpec(memory_space=pltpu.SMEM)] + [spec] * 3,
        out_specs=spec,
        scratch_shapes=[pltpu.VMEM((ROWS, 2 * PAD, COLS), BF16)],
        compiler_params=params(),
        cost_estimate=cost(4 * 10**9, 8 * 10**6),
    )(strip, halo_t, halo_b, adj, adj_t, adj_b, weights, ends, open_lanes, inside, border)


def gather_kernel(field, incoming, out, turned, table, hot, picked):
    turned[...] = incoming[...].T
    picked[...] = jnp.zeros_like(picked)
    for x in range(ROWS):
        cols = slice(x % 4 * COLS, (x % 4 + 1) * COLS)
        for p, piece in enumerate(split(field[x], 2)):
            first = (p * 4 + x // 4) * PAD
            table[first : first + PAD, cols] = piece
    rows1 = iota((4 * PAD, COLS), 0)
    rows2 = iota((4 * COLS, COLS), 0)

    @pl.loop(0, CAP // 8)
    def _(j):
        first = pl.multiple_of(j * 8, 8)
        cells = turned[pl.ds(CAP + first, 8), :].astype(I32)
        lines = []
        for q in range(0, 8, 2):
            cell = jnp.concatenate([cells[q : q + 1, :], cells[q + 1 : q + 2, :]], axis=1)
            hot[...] = one_hot(rows2 == (cell & 1023))
            found = dot(table[...], hot[...])
            key1 = ((cell >> 10) & 3) * PAD + (cell >> 12)
            found = jnp.where(rows1 == key1, found[: 4 * PAD] + found[4 * PAD :], 0.0)
            found = jnp.sum(found, axis=0, keepdims=True)
            lines += [found[:, :HALF], found[:, HALF:]]
        picked[pl.ds(first, 8), :] = jnp.concatenate(lines, axis=0)

    out[...] = picked[...].T


def gather(field, incoming):
    spec = pl.BlockSpec(memory_space=pltpu.VMEM)
    return pl.pallas_call(
        gather_kernel,
        name="gather",
        out_shape=jax.ShapeDtypeStruct((DEV, HALF), F32),
        in_specs=[spec] * 2,
        out_specs=spec,
        scratch_shapes=[
            pltpu.VMEM((HALF, DEV), F32),
            pltpu.VMEM((8 * PAD, 4 * COLS), BF16),
            pltpu.VMEM((4 * COLS, COLS), BF16),
            pltpu.VMEM((HALF, DEV), F32),
        ],
        compiler_params=params(),
        cost_estimate=cost(10**10, 2 * 10**6),
    )(field, incoming)


def restore_kernel(field, perm_y, perm_r, out, rows):
    for x in range(ROWS):
        value = field[x]
        high, low = split(value, 2)
        rows[x] = dot(high, perm_y[...]) + dot(low, perm_y[...])
    for b in range(6):
        block = jnp.concatenate([rows[x, b * 16 : (b + 1) * 16, :] for x in range(ROWS)], axis=0)
        high, low = split(block, 2)
        value = dot(perm_r[...], high) + dot(perm_r[...], low)
        if b < 5:
            out[b * 256 : (b + 1) * 256, :] = value
        else:
            out[1280:1440, :] = value[:160]


def restore(field):
    y = np.arange(COLS)
    perm_y = np.zeros((COLS, COLS))
    perm_y[(y % 2) * HALF + y // 2, y] = 1
    i = np.arange(256)
    perm_r = np.zeros((256, 256))
    perm_r[i, i % 16 * 16 + i // 16] = 1
    spec = pl.BlockSpec(memory_space=pltpu.VMEM)
    return pl.pallas_call(
        restore_kernel,
        name="restore",
        out_shape=jax.ShapeDtypeStruct((LEV * ROWS, COLS), F32),
        in_specs=[spec] * 3,
        out_specs=spec,
        scratch_shapes=[pltpu.VMEM((ROWS, PAD, COLS), F32)],
        compiler_params=params(),
        cost_estimate=cost(10**9, 3 * 10**6),
    )(field, jnp.asarray(perm_y, BF16), jnp.asarray(perm_r, BF16)).reshape(LEV, ROWS, COLS)


def forward(value, axis):
    size = lax.axis_size(axis)
    return lax.ppermute(value, axis, [(i, i + 1) for i in range(size - 1)])


def backward(value, axis):
    size = lax.axis_size(axis)
    return lax.ppermute(value, axis, [(i + 1, i) for i in range(size - 1)])


FIRST = 5


def body(ensemble, vertical_weights, dual_vector, observed_column, observed_level, active_count):
    gx, gy = lax.axis_index("gx"), lax.axis_index("gy")
    last_x, last_y = lax.axis_size("gx") - 1, lax.axis_size("gy") - 1
    ends = jnp.stack([gx != 0, gx != last_x]).astype(F32)
    lane = jnp.arange(COLS) % HALF % STRIP
    closed = ((lane < 3) & (gy == 0)) | ((lane >= 15) & (gy == last_y))
    open_lanes = jnp.where(closed, 0.0, 1.0).astype(F32)[None, :]
    wide = jnp.pad(vertical_weights, ((0, PAD - LEV), (0, PAD - LEV)))
    high = lax.reduce_precision(wide, 8, 7)
    low = (wide - high).astype(BF16)
    high = high.astype(BF16)
    weights = jnp.concatenate(
        [jnp.concatenate([high, high], 1), jnp.concatenate([low, jnp.zeros_like(low)], 1)], 0
    )

    outgoing, target, rank = pack(active_count, dual_vector, observed_column, observed_level)
    incoming = lax.all_to_all(outgoing, ("gx", "gy"), split_axis=0, concat_axis=0, tiled=True)

    ens, ens_up, ens_down, strip, side = arrange(ensemble)
    halo_t = forward(ens_down, "gx")
    halo_b = backward(ens_up, "gx")
    from_left = forward(side[1:], "gy")
    from_right = backward(side[:1], "gy")
    strip, strip_up, strip_down = complete_strip(strip, from_left, from_right)
    strip_t = forward(strip_down, "gx")
    strip_b = backward(strip_up, "gx")

    adj, sides = scatter(incoming)
    adj_left = forward(sides[1:], "gy")
    adj_right = backward(sides[:1], "gy")
    zero = jnp.zeros((INNER, PAD, COLS), F32)
    border0, inside = inner(ens, adj, weights, ends, zero, 0, FIRST)
    adj_strip, adj_up, adj_down = adjoint_strip(adj, adj_left, adj_right)
    adj_t = forward(adj_down, "gx")
    adj_b = backward(adj_up, "gx")
    border1, inside = inner(ens, adj, weights, ends, inside, FIRST, MEM - FIRST)

    zero = jnp.zeros((2 * EDGE, PAD, COLS), F32)
    border = jnp.concatenate([border0, border1], axis=0)
    outside = outer(ens, halo_t, halo_b, adj_t[:EDGE], adj_b[:EDGE], border, weights, zero, 0, MEM)
    field = edge(
        strip, strip_t, strip_b, adj_strip, adj_t[EDGE:], adj_b[EDGE:], weights, ends, open_lanes, inside, outside
    )
    picked = gather(field, incoming)
    back = lax.all_to_all(picked, ("gx", "gy"), split_axis=0, concat_axis=0, tiled=True)
    increment = restore(field)
    obs_product = unpack(back, target, rank)
    return (increment, obs_product)


def solution(mesh):
    placed = (
        P(None, None, "gx", "gy"),
        P(),
        P(("gx", "gy")),
        P(("gx", "gy")),
        P(("gx", "gy")),
        P(("gx", "gy")),
    )
    return jax.shard_map(
        body,
        mesh=mesh,
        in_specs=placed,
        out_specs=(P(None, "gx", "gy"), P(("gx", "gy"))),
        check_vma=False,
    )
```

```python
import jax
import jax.numpy as jnp
import numpy as np
from jax import lax
from jax.experimental import pallas as pl
from jax.experimental.pallas import tpu as pltpu
from jax.sharding import PartitionSpec as P

F32 = jnp.float32
BF16 = jnp.bfloat16
I32 = jnp.int32

MEM, LEV, ROWS, COLS = 10, 90, 16, 256
PAD = 96
DEV = 128
CAP = 48
SLOTS = 2048
HALF = 128
QUARTER = 64
DUO = 2 * COLS
DUOS = MEM // 2
EDGE = 3
STRIP = 18
PAIRS = STRIP // 2
SELF = 1.0 / 6.0
SCALE = 0.24**3 / (MEM - 1)
VMEM = 20 * 1024 * 1024


def split(value, count):
    parts = []
    for _ in range(count - 1):
        top = value.astype(BF16)
        parts.append(top)
        value = value - top.astype(F32)
    parts.append(value.astype(BF16))
    return parts


def dot(a, b):
    return lax.dot_general(a, b, (((1,), (0,)), ((), ())), preferred_element_type=F32)


def dot_nt(a, b):
    return lax.dot_general(a, b, (((1,), (1,)), ((), ())), preferred_element_type=F32)


def iota(shape, dim):
    return lax.broadcasted_iota(I32, shape, dim)


def one_hot(test):
    return jnp.where(test, 1.0, 0.0).astype(BF16)


def params(**kw):
    return pltpu.CompilerParams(vmem_limit_bytes=VMEM, **kw)


def cost(flops, moved):
    return pl.CostEstimate(flops=flops, bytes_accessed=moved, transcendentals=0)


def pack_kernel(count, dual, col, lev, upper, vertical, out, tgt_out, rank_out, weights, left_v, left_c, right_v, right_c):
    wide = jnp.concatenate([vertical[...], jnp.zeros((LEV, PAD - LEV), F32)], axis=1)
    high, low = split(jnp.concatenate([wide, jnp.zeros((PAD - LEV, PAD), F32)], axis=0), 2)
    both = jnp.concatenate([low, jnp.zeros_like(low)], axis=1)
    weights[...] = jnp.concatenate([jnp.concatenate([high, high], axis=1), both], axis=0)
    number = count[0]
    rows = iota((DEV, HALF), 0)
    lane = iota((1, HALF), 1)
    carry = jnp.zeros((DEV, HALF), F32)
    for i in range(SLOTS // HALF):
        at = slice(i * HALF, (i + 1) * HALF)
        column = col[i : i + 1, :]
        row = column >> 12
        gcol = column & 4095
        y = gcol & 255
        y = ((y & 3) << 6) + (y >> 2)
        target = ((row >> 4) << 4) + (gcol >> 8)
        target = jnp.where(i * HALF + lane < number, target, -1)
        hit = rows == target
        both = dot(one_hot(hit), upper[...])
        rank = jnp.sum(jnp.where(hit, both[:, :HALF] + carry, 0.0), axis=0, keepdims=True)
        carry = carry + both[:, HALF:]
        tgt_out[i : i + 1, :] = target
        rank = rank.astype(I32)
        rank_out[i : i + 1, :] = rank
        right_v[:, at] = one_hot(rows == rank)
        right_c[:, at] = one_hot(rows == rank + CAP)
        values = dual[i : i + 1, :]
        for p, piece in enumerate(split(values, 3)):
            left_v[p * DEV : (p + 1) * DEV, at] = jnp.where(hit, piece.astype(F32), 0.0).astype(BF16)
        cells = (lev[i : i + 1, :] << 12, (row & 15) << 8, y)
        for p, piece in enumerate(cells):
            left_c[p * DEV : (p + 1) * DEV, at] = jnp.where(hit, piece.astype(F32), 0.0).astype(BF16)
    a = dot_nt(left_v[...], right_v[...])
    b = dot_nt(left_c[...], right_c[...])
    out[...] = ((a[:DEV] + a[DEV : 2 * DEV]) + a[2 * DEV :]) + ((b[:DEV] + b[DEV : 2 * DEV]) + b[2 * DEV :])


def pack(count, dual, col, lev, vertical):
    upper = np.concatenate([np.triu(np.ones((HALF, HALF)), 1), np.ones((HALF, HALF))], 1)
    spec = pl.BlockSpec(memory_space=pltpu.VMEM)
    return pl.pallas_call(
        pack_kernel,
        name="pack",
        out_shape=(
            jax.ShapeDtypeStruct((DEV, HALF), F32),
            jax.ShapeDtypeStruct((SLOTS // HALF, HALF), I32),
            jax.ShapeDtypeStruct((SLOTS // HALF, HALF), I32),
            jax.ShapeDtypeStruct((2 * PAD, 2 * PAD), BF16),
        ),
        in_specs=[pl.BlockSpec(memory_space=pltpu.SMEM)] + [spec] * 5,
        out_specs=(spec,) * 4,
        scratch_shapes=[pltpu.VMEM((3 * DEV, SLOTS), BF16)] * 2 + [pltpu.VMEM((DEV, SLOTS), BF16)] * 2,
        compiler_params=params(),
        cost_estimate=cost(10**9, 10**6),
    )(count, dual.reshape(-1, HALF), col.reshape(-1, HALF), lev.reshape(-1, HALF), jnp.asarray(upper, BF16), vertical)


def unpack_kernel(back, tgt, rank, out):
    rows = iota((DEV, HALF), 0)
    table = jnp.concatenate(split(back[...], 3), axis=0)
    for i in range(SLOTS // HALF):
        found = dot(table, one_hot(rows == rank[i : i + 1, :]))
        found = (found[:DEV] + found[DEV : 2 * DEV]) + found[2 * DEV :]
        out[i : i + 1, :] = jnp.sum(jnp.where(rows == tgt[i : i + 1, :], found, 0.0), axis=0, keepdims=True)


def unpack(back, tgt, rank):
    spec = pl.BlockSpec(memory_space=pltpu.VMEM)
    return pl.pallas_call(
        unpack_kernel,
        name="unpack",
        out_shape=jax.ShapeDtypeStruct((SLOTS // HALF, HALF), F32),
        in_specs=[spec] * 3,
        out_specs=spec,
        compiler_params=params(),
        cost_estimate=cost(10**8, 10**5),
    )(back, tgt, rank).reshape(SLOTS)


def strip_place(lane):
    j = lane % HALF
    return j // PAIRS, jnp.where(j < MEM * PAIRS, j % PAIRS * 2 + lane // HALF, -1)


def natural(place):
    return ((place & 63) << 2) + (place >> 6)


def duo_place(place):
    return ((place & 63) << 2) + (place >> 7), (place >> 6) & 1


def widen(value):
    low = iota((value.shape[0], HALF), 1) < QUARTER
    phases = []
    for half in (value[:, :HALF], value[:, HALF:]):
        turned = pltpu.roll(half, QUARTER, 1)
        phases += [jnp.where(low, half, turned), jnp.where(low, turned, half)]
    return jnp.concatenate(phases, axis=1)


def fold(value):
    low = iota((value.shape[0], HALF), 1) < QUARTER
    p = [value[:, i * HALF : (i + 1) * HALF] for i in range(4)]
    return jnp.concatenate(
        [jnp.where(low, p[i], p[i + 1]) + pltpu.roll(jnp.where(low, p[i + 1], p[i]), QUARTER, 1) for i in (0, 2)],
        axis=1,
    )


def arrange_kernel(ens, perm_y, perm_r, out, up, down, strip, side_l, side_r, buffer, rows, select, sem):
    def fetch(k):
        return pltpu.make_async_copy(ens.at[k], buffer.at[k % 4], sem.at[k % 4])

    fetch(0).start()
    fetch(1).start()
    rows[LEV * ROWS :, :] = jnp.zeros((rows.shape[0] - LEV * ROWS, DUO), BF16)

    @pl.loop(0, DUOS)
    def _(duo):
        @pl.when(duo < DUOS - 1)
        def _():
            fetch(2 * duo + 2).start()
            fetch(2 * duo + 3).start()

        fetch(2 * duo).wait()
        fetch(2 * duo + 1).wait()
        here, there = 2 * duo % 4, (2 * duo + 1) % 4
        y, which = duo_place(iota((DUO, COLS), 0))
        member, c = strip_place(iota((DUO, COLS), 1))
        want = jnp.where(y < 6, 3 + y, jnp.where(y >= 250, y - 241, -2))
        select[pl.ds(pl.multiple_of(duo * DUO, DUO), DUO), :] = one_hot((member == 2 * duo + which) & (c == want))
        for b in range(6):
            at = slice(b * 240, (b + 1) * 240)
            block = jnp.concatenate([buffer[here, at, :], buffer[there, at, :]], axis=1)
            rows[at, :] = dot(block, perm_y[...]).astype(BF16)
        for b in range(6):
            turned = dot(perm_r[...], rows[b * 256 : (b + 1) * 256, :])
            at = slice(b * 16, (b + 1) * 16)
            for x in range(ROWS):
                part = turned[x * 16 : (x + 1) * 16, :]
                out[duo, x, at, :] = part.astype(BF16)
                if x < EDGE:
                    up[duo, x, at, :] = part
                if x >= ROWS - EDGE:
                    down[duo, x - (ROWS - EDGE), at, :] = part

    @pl.loop(0, ROWS)
    def _(x):
        every = jnp.concatenate([out[duo, x] for duo in range(DUOS)], axis=1)
        strip[x] = dot(every, select[...]).astype(BF16)

    member, c = strip_place(iota((COLS, COLS), 0))
    left, right = (c >= 3) & (c < 6), (c >= 12) & (c < 15)
    spot = jnp.where(left, 3 * member + c - 3, jnp.where(right, HALF + 3 * member + c - 12, -1000))
    for group in range(4):
        sides = jnp.zeros((PAD, COLS), F32)
        for j in range(4):
            sides = sides + dot(strip[group * 4 + j], one_hot(iota((COLS, COLS), 1) == spot + 30 * j))
        side_l[group] = sides[:, :HALF]
        side_r[group] = sides[:, HALF:]


def arrange(ensemble):
    y = np.arange(COLS)
    perm_y = np.zeros((DUO, DUO))
    for which in range(2):
        perm_y[which * COLS + y, y % 4 * HALF + which * QUARTER + y // 4] = 1
    i = np.arange(256)
    perm_r = np.zeros((256, 256))
    perm_r[i % 16 * 16 + i // 16, i] = 1
    spec = pl.BlockSpec(memory_space=pltpu.VMEM)
    return pl.pallas_call(
        arrange_kernel,
        name="arrange",
        out_shape=(
            jax.ShapeDtypeStruct((DUOS, ROWS, PAD, DUO), BF16),
            jax.ShapeDtypeStruct((DUOS, EDGE, PAD, DUO), F32),
            jax.ShapeDtypeStruct((DUOS, EDGE, PAD, DUO), F32),
            jax.ShapeDtypeStruct((ROWS, PAD, COLS), BF16),
            jax.ShapeDtypeStruct((4, PAD, HALF), F32),
            jax.ShapeDtypeStruct((4, PAD, HALF), F32),
        ),
        in_specs=[pl.BlockSpec(memory_space=pl.ANY), spec, spec],
        out_specs=(spec,) * 6,
        scratch_shapes=[
            pltpu.VMEM((4, LEV * ROWS, COLS), BF16),
            pltpu.VMEM((PAD * ROWS, DUO), BF16),
            pltpu.VMEM((DUOS * DUO, COLS), BF16),
            pltpu.SemaphoreType.DMA((4,)),
        ],
        compiler_params=params(),
        cost_estimate=cost(10**10, 25 * 10**6),
    )(ensemble.reshape(MEM, LEV * ROWS, COLS), jnp.asarray(perm_y, BF16), jnp.asarray(perm_r, BF16))


KTILE = 1024


def scatter_kernel(incoming, ens_l, ens_r, out, wide, side_l, side_r, turned, hot1, hot2, acc):
    turned[...] = incoming[...].T
    acc[...] = jnp.zeros_like(acc)
    rows1 = iota((4 * PAD, HALF), 0)
    rows2 = iota((4 * COLS, HALF), 0)

    @pl.loop(0, CAP // 8)
    def _(j):
        first = pl.multiple_of(j * 8, 8)
        values = turned[pl.ds(first, 8), :]
        cells = turned[pl.ds(CAP + first, 8), :].astype(I32)
        for q in range(8):
            at = slice(q * HALF, (q + 1) * HALF)
            cell = cells[q : q + 1, :]
            key1 = ((cell >> 10) & 3) * PAD + (cell >> 12)
            hit = rows1 == key1
            for p, piece in enumerate(split(values[q : q + 1, :], 2)):
                hot1[p * 4 * PAD : (p + 1) * 4 * PAD, at] = jnp.where(hit, piece.astype(F32), 0.0).astype(BF16)
            hot2[:, at] = one_hot(rows2 == (cell & 1023))
        for n in range(4):
            cols = slice(n * COLS, (n + 1) * COLS)
            acc[:, cols] += dot_nt(hot1[...], hot2[cols, :])

    y = natural(iota((COLS, COLS), 0))
    lane = iota((COLS, COLS), 1)
    place = jnp.where(y < 3, y, jnp.where(y >= 253, HALF + y - 253, -1000))
    packed = jnp.zeros((PAD, COLS), F32)
    for x in range(ROWS):
        cols = slice(x % 4 * COLS, (x % 4 + 1) * COLS)
        level = x // 4 * PAD
        value = acc[level : level + PAD, cols] + acc[4 * PAD + level : 4 * PAD + level + PAD, cols]
        out[x] = value
        wide[x] = widen(value)
        select = one_hot(lane == place + 3 * x)
        for piece in split(value, 2):
            packed = packed + dot(piece, select)
    side_l[:4] = ens_l[...]
    side_r[:4] = ens_r[...]
    side_l[4] = packed[:, :HALF]
    side_r[4] = packed[:, HALF:]


def scatter(incoming, ens_l, ens_r):
    spec = pl.BlockSpec(memory_space=pltpu.VMEM)
    return pl.pallas_call(
        scatter_kernel,
        name="scatter",
        out_shape=(
            jax.ShapeDtypeStruct((ROWS, PAD, COLS), F32),
            jax.ShapeDtypeStruct((ROWS, PAD, DUO), F32),
            jax.ShapeDtypeStruct((5, PAD, HALF), F32),
            jax.ShapeDtypeStruct((5, PAD, HALF), F32),
        ),
        in_specs=[spec] * 3,
        out_specs=(spec,) * 4,
        scratch_shapes=[
            pltpu.VMEM((HALF, DEV), F32),
            pltpu.VMEM((8 * PAD, KTILE), BF16),
            pltpu.VMEM((4 * COLS, KTILE), BF16),
            pltpu.VMEM((8 * PAD, 4 * COLS), F32),
        ],
        compiler_params=params(),
        cost_estimate=cost(10**10, 2 * 10**6),
    )(incoming, ens_l, ens_r)


def strips_kernel(strip, adjoint, left, right, ens_out, out, up, down):
    member, member_c = strip_place(iota((COLS, COLS), 1))
    y = natural(iota((COLS, COLS), 0))
    own = one_hot(member_c == jnp.where(y < 6, 3 + y, jnp.where(y >= 250, y - 241, -2)))
    from_lane = iota((HALF, COLS), 0)
    member_c, member = member_c[:HALF], member[:HALF]
    pieces = [split(side[4], 2) for side in (left, right)]
    for x in range(ROWS):
        value = strip[x].astype(F32)
        first = x % 4 * 30 + 3 * member
        for side, shift in ((left, 0), (right, 15)):
            inside = (member_c >= shift) & (member_c < shift + 3)
            spot = one_hot(inside & (from_lane == first + member_c - shift))
            value = value + dot(side[x // 4].astype(BF16), spot)
        ens_out[x] = value.astype(BF16)
        if x < EDGE:
            up[2, x] = value
        if x >= ROWS - EDGE:
            down[2, x - (ROWS - EDGE)] = value
        value = jnp.zeros((PAD, COLS), F32)
        for piece in split(adjoint[x], 2):
            value = value + dot(piece, own)
        for side, shift in ((pieces[0], 0), (pieces[1], 15)):
            inside = (member_c >= shift) & (member_c < shift + 3)
            spot = one_hot(inside & (from_lane == 3 * x + member_c - shift))
            for piece in side:
                value = value + dot(piece, spot)
        out[x] = value
        if x < EDGE:
            up[0, x] = adjoint[x]
            up[1, x] = value
        if x >= ROWS - EDGE:
            down[0, x - (ROWS - EDGE)] = adjoint[x]
            down[1, x - (ROWS - EDGE)] = value


def strips(strip, adjoint, left, right):
    spec = pl.BlockSpec(memory_space=pltpu.VMEM)
    return pl.pallas_call(
        strips_kernel,
        name="strips",
        out_shape=(
            jax.ShapeDtypeStruct((ROWS, PAD, COLS), BF16),
            jax.ShapeDtypeStruct((ROWS, PAD, COLS), F32),
            jax.ShapeDtypeStruct((3, EDGE, PAD, COLS), F32),
            jax.ShapeDtypeStruct((3, EDGE, PAD, COLS), F32),
        ),
        in_specs=[spec] * 4,
        out_specs=(spec,) * 4,
        compiler_params=params(),
        cost_estimate=cost(10**9, 4 * 10**6),
    )(strip, adjoint, left, right)


def beside_permuted(value):
    even, odd = value[:, :HALF], value[:, HALF:]
    return jnp.concatenate([odd + pltpu.roll(odd, 1, 1), even + pltpu.roll(even, HALF - 1, 1)], axis=1)


def beside_duo(value):
    p = [value[:, i * HALF : (i + 1) * HALF] for i in range(4)]
    return jnp.concatenate(
        [pltpu.roll(p[3], 1, 1) + p[1], p[0] + p[2], p[1] + p[3], p[2] + pltpu.roll(p[0], HALF - 1, 1)], axis=1
    )


def total(terms):
    result = None
    for term in terms:
        if term is not None:
            result = term if result is None else result + term
    return result


def diffuse(get, given, wanted, beside, emit, mask=None):
    rows = [{} for _ in range(EDGE + 1)]
    for x in range(min(wanted) - EDGE, max(wanted) + EDGE + 1):
        if x in given:
            rows[0][x] = get(x)
        for step in range(1, EDGE + 1):
            at, reach, older = x - step, EDGE - step, rows[step - 1]
            if not min(wanted) - reach <= at <= max(wanted) + reach:
                continue
            terms = [older.get(at - 1), older.get(at + 1)]
            if at in older:
                terms += [beside(older[at]), older[at] * SELF]
            value = total(terms)
            if value is None:
                continue
            if step == EDGE:
                emit(at, value)
            else:
                rows[step][at] = value if mask is None else mask(at, value)


def put_split(ref, index, at, value):
    top = value.astype(BF16)
    ref[index, at, :] = top
    ref[index, pl.ds(at.start + PAD, 16), :] = (value - top.astype(F32)).astype(BF16)


def mix(weights, field):
    both = dot(weights, field)
    return both[:PAD] + both[PAD:]


INNER = ROWS - 2 * EDGE


def inner_kernel(start, count, ens, adj, weights, place, *refs):
    border, out, field, first = refs[-4:]
    out[...] = refs[0][...] if start else jnp.zeros_like(out)
    top_open = jnp.where(place[0] == 0, 0.0, 1.0)
    bottom_open = jnp.where(place[0] == place[2], 0.0, 1.0)

    def mask(x, value):
        if x < 0:
            return value * top_open
        if x >= ROWS:
            return value * bottom_open
        return value

    @pl.loop(0, count)
    def _(step):
        k = start + step

        @pl.loop(0, PAD // 16)
        def _(group):
            at = pl.ds(pl.multiple_of(group * 16, 16), 16)

            for part in range(2):
                eight = pl.ds(pl.multiple_of(group * 16 + part * 8, 8), 8)

                def get(x):
                    return ens[k, x, at, :].astype(F32)[part * 8 : part * 8 + 8, :] * adj[x, eight, :]

                def emit(x, value):
                    if not EDGE <= x < ROWS - EDGE:
                        border[step, x if x < EDGE else x - INNER, eight, :] = value
                    elif part == 0:
                        first[x - EDGE] = value
                    else:
                        put_split(field, x - EDGE, at, jnp.concatenate([first[x - EDGE], value], axis=0))

                diffuse(get, range(ROWS), range(ROWS), beside_duo, emit, mask)

        for x in range(INNER):
            out[x] += ens[k, x + EDGE].astype(F32) * mix(weights[...], field[x])


def inner(ens, adj, weights, place, start, count, before=()):
    spec = pl.BlockSpec(memory_space=pltpu.VMEM)
    return pl.pallas_call(
        lambda *refs: inner_kernel(start, count, *refs),
        name="inner",
        out_shape=(
            jax.ShapeDtypeStruct((count, 2 * EDGE, PAD, DUO), F32),
            jax.ShapeDtypeStruct((INNER, PAD, DUO), F32),
        ),
        in_specs=[spec] * 3 + [pl.BlockSpec(memory_space=pltpu.SMEM)] + [spec] * len(before),
        out_specs=(spec,) * 2,
        scratch_shapes=[pltpu.VMEM((INNER, 2 * PAD, DUO), BF16), pltpu.VMEM((INNER, 8, DUO), F32)],
        compiler_params=params(),
        cost_estimate=cost(count * 2 * 10**9, count * 2 * 10**6),
    )(ens, adj, weights, place, *before)


def outer_kernel(ens, halo_t, halo_b, adj_t, adj_b, border0, border1, weights, out, field, first, wide):
    out[...] = jnp.zeros_like(out)
    for x in range(EDGE):
        wide[x] = widen(adj_t[0, x])
        wide[EDGE + x] = widen(adj_b[0, x])

    for border, start in ((border0, 0), (border1, FIRST)):

        @pl.loop(0, border.shape[0])
        def _(step):
            k = start + step

            @pl.loop(0, PAD // 16)
            def _(group):
                at = pl.ds(pl.multiple_of(group * 16, 16), 16)

                for part in range(2):
                    eight = pl.ds(pl.multiple_of(group * 16 + part * 8, 8), 8)

                    def emit(x, value):
                        value = value + border[step, x, eight, :]
                        if part == 0:
                            first[x] = value
                        else:
                            put_split(field, x, at, jnp.concatenate([first[x], value], axis=0))

                    def get_t(x):
                        return halo_t[k, x + EDGE, eight, :] * wide[x + EDGE, eight, :]

                    def get_b(x):
                        return halo_b[k, x - 2 * EDGE, eight, :] * wide[x - EDGE, eight, :]

                    diffuse(get_t, range(-EDGE, 0), range(EDGE), beside_duo, emit)
                    diffuse(get_b, range(2 * EDGE, 3 * EDGE), range(EDGE, 2 * EDGE), beside_duo, emit)

            for x in range(2 * EDGE):
                row = x if x < EDGE else x + INNER
                out[x] += ens[k, row].astype(F32) * mix(weights[...], field[x])


def outer(ens, halo_t, halo_b, adj_t, adj_b, border0, border1, weights):
    spec = pl.BlockSpec(memory_space=pltpu.VMEM)
    return pl.pallas_call(
        outer_kernel,
        name="outer",
        out_shape=jax.ShapeDtypeStruct((2 * EDGE, PAD, DUO), F32),
        in_specs=[spec] * 8,
        out_specs=spec,
        scratch_shapes=[
            pltpu.VMEM((2 * EDGE, 2 * PAD, DUO), BF16),
            pltpu.VMEM((2 * EDGE, 8, DUO), F32),
            pltpu.VMEM((2 * EDGE, PAD, DUO), F32),
        ],
        compiler_params=params(),
        cost_estimate=cost(MEM * 10**9, MEM * 3 * 10**6),
    )(ens, halo_t, halo_b, adj_t, adj_b, border0, border1, weights)


def edge_kernel(strip, adj, halo_t, halo_b, weights, place, inside, border, out, field):
    top_open = jnp.where(place[0] == 0, 0.0, 1.0)
    bottom_open = jnp.where(place[0] == place[2], 0.0, 1.0)
    left_open = jnp.where(place[1] == 0, 0.0, 1.0)
    right_open = jnp.where(place[1] == place[3], 0.0, 1.0)

    @pl.loop(0, PAD // 16)
    def _(group):
        at = pl.ds(pl.multiple_of(group * 16, 16), 16)
        c = strip_place(iota((16, COLS), 1))[1]
        lanes = jnp.where(c < 3, left_open, jnp.where(c >= 15, right_open, 1.0))

        def mask(x, value):
            value = value * lanes
            if x < 0:
                return value * top_open
            if x >= ROWS:
                return value * bottom_open
            return value

        def get(x):
            if x < 0:
                return halo_t[2, x + EDGE, at, :] * halo_t[1, x + EDGE, at, :]
            if x >= ROWS:
                return halo_b[2, x - ROWS, at, :] * halo_b[1, x - ROWS, at, :]
            return strip[x, at, :].astype(F32) * adj[x, at, :]

        def emit(x, value):
            put_split(field, x, at, value)

        diffuse(get, range(-EDGE, ROWS + EDGE), range(ROWS), beside_permuted, emit, mask)

    c = strip_place(iota((COLS, COLS), 0))[1]
    spot = jnp.where((c >= 3) & (c < 6), c - 3, jnp.where((c >= 12) & (c < 15), 241 + c, -1))
    collect = one_hot(spot == natural(iota((COLS, COLS), 1)))
    y = natural(iota((PAD, COLS), 1))
    middle = (y >= EDGE) & (y < COLS - EDGE)
    for x in range(ROWS):
        if EDGE <= x < ROWS - EDGE:
            value = inside[x - EDGE]
        else:
            value = border[x if x < EDGE else x - INNER]
        value = jnp.where(middle, fold(value), 0.0)
        product = strip[x].astype(F32) * mix(weights[...], field[x])
        for piece in split(product, 2):
            value = value + dot(piece, collect)
        out[x] = value * SCALE


def edge(strip, adj, halo_t, halo_b, weights, place, inside, border):
    spec = pl.BlockSpec(memory_space=pltpu.VMEM)
    return pl.pallas_call(
        edge_kernel,
        name="edge",
        out_shape=jax.ShapeDtypeStruct((ROWS, PAD, COLS), F32),
        in_specs=[spec] * 5 + [pl.BlockSpec(memory_space=pltpu.SMEM)] + [spec] * 2,
        out_specs=spec,
        scratch_shapes=[pltpu.VMEM((ROWS, 2 * PAD, COLS), BF16)],
        compiler_params=params(),
        cost_estimate=cost(4 * 10**9, 8 * 10**6),
    )(strip, adj, halo_t, halo_b, weights, place, inside, border)


def gather_kernel(field, incoming, out, turned, table, hot, picked):
    turned[...] = incoming[...].T
    picked[...] = jnp.zeros_like(picked)
    for x in range(ROWS):
        cols = slice(x % 4 * COLS, (x % 4 + 1) * COLS)
        for p, piece in enumerate(split(field[x], 2)):
            first = (p * 4 + x // 4) * PAD
            table[first : first + PAD, cols] = piece
    rows1 = iota((4 * PAD, COLS), 0)
    rows2 = iota((4 * COLS, COLS), 0)

    @pl.loop(0, CAP // 8)
    def _(j):
        first = pl.multiple_of(j * 8, 8)
        cells = turned[pl.ds(CAP + first, 8), :].astype(I32)
        lines = []
        for q in range(0, 8, 2):
            cell = jnp.concatenate([cells[q : q + 1, :], cells[q + 1 : q + 2, :]], axis=1)
            hot[...] = one_hot(rows2 == (cell & 1023))
            found = dot(table[...], hot[...])
            key1 = ((cell >> 10) & 3) * PAD + (cell >> 12)
            found = jnp.where(rows1 == key1, found[: 4 * PAD] + found[4 * PAD :], 0.0)
            found = jnp.sum(found, axis=0, keepdims=True)
            lines += [found[:, :HALF], found[:, HALF:]]
        picked[pl.ds(first, 8), :] = jnp.concatenate(lines, axis=0)

    out[...] = picked[...].T


def gather(field, incoming):
    spec = pl.BlockSpec(memory_space=pltpu.VMEM)
    return pl.pallas_call(
        gather_kernel,
        name="gather",
        out_shape=jax.ShapeDtypeStruct((DEV, HALF), F32),
        in_specs=[spec] * 2,
        out_specs=spec,
        scratch_shapes=[
            pltpu.VMEM((HALF, DEV), F32),
            pltpu.VMEM((8 * PAD, 4 * COLS), BF16),
            pltpu.VMEM((4 * COLS, COLS), BF16),
            pltpu.VMEM((HALF, DEV), F32),
        ],
        compiler_params=params(),
        cost_estimate=cost(10**10, 2 * 10**6),
    )(field, incoming)


def restore_kernel(field, perm_y, perm_r, out, rows):
    for x in range(ROWS):
        value = field[x]
        high, low = split(value, 2)
        rows[x] = dot(high, perm_y[...]) + dot(low, perm_y[...])
    for b in range(6):
        block = jnp.concatenate([rows[x, b * 16 : (b + 1) * 16, :] for x in range(ROWS)], axis=0)
        high, low = split(block, 2)
        value = dot(perm_r[...], high) + dot(perm_r[...], low)
        if b < 5:
            out[b * 256 : (b + 1) * 256, :] = value
        else:
            out[1280:1440, :] = value[:160]


def restore(field):
    y = np.arange(COLS)
    perm_y = np.zeros((COLS, COLS))
    perm_y[y % 4 * QUARTER + y // 4, y] = 1
    i = np.arange(256)
    perm_r = np.zeros((256, 256))
    perm_r[i, i % 16 * 16 + i // 16] = 1
    spec = pl.BlockSpec(memory_space=pltpu.VMEM)
    return pl.pallas_call(
        restore_kernel,
        name="restore",
        out_shape=jax.ShapeDtypeStruct((LEV * ROWS, COLS), F32),
        in_specs=[spec] * 3,
        out_specs=spec,
        scratch_shapes=[pltpu.VMEM((ROWS, PAD, COLS), F32)],
        compiler_params=params(),
        cost_estimate=cost(10**9, 3 * 10**6),
    )(field, jnp.asarray(perm_y, BF16), jnp.asarray(perm_r, BF16)).reshape(LEV, ROWS, COLS)


def forward(value, axis):
    size = lax.axis_size(axis)
    return lax.ppermute(value, axis, [(i, i + 1) for i in range(size - 1)])


def backward(value, axis):
    size = lax.axis_size(axis)
    return lax.ppermute(value, axis, [(i + 1, i) for i in range(size - 1)])


FIRST = 2


def body(ensemble, vertical_weights, dual_vector, observed_column, observed_level, active_count):
    place = jnp.stack(
        [lax.axis_index("gx"), lax.axis_index("gy"), lax.axis_size("gx") - 1, lax.axis_size("gy") - 1]
    ).astype(I32)
    outgoing, target, rank, weights = pack(
        active_count, dual_vector, observed_column, observed_level, vertical_weights
    )
    incoming = lax.all_to_all(outgoing, ("gx", "gy"), split_axis=0, concat_axis=0, tiled=True)

    ens, ens_up, ens_down, strip, ens_l, ens_r = arrange(ensemble)
    halo_t = forward(ens_down, "gx")
    halo_b = backward(ens_up, "gx")

    adj, wide, side_l, side_r = scatter(incoming, ens_l, ens_r)
    from_left = forward(side_r, "gy")
    from_right = backward(side_l, "gy")
    border0, inside = inner(ens, wide, weights, place, 0, FIRST)
    strip, adj_strip, up, down = strips(strip, adj, from_left, from_right)
    top = forward(down, "gx")
    bottom = backward(up, "gx")
    border1, inside = inner(ens, wide, weights, place, FIRST, DUOS - FIRST, (inside,))

    outside = outer(ens, halo_t, halo_b, top, bottom, border0, border1, weights)
    field = edge(strip, adj_strip, top, bottom, weights, place, inside, outside)
    picked = gather(field, incoming)
    back = lax.all_to_all(picked, ("gx", "gy"), split_axis=0, concat_axis=0, tiled=True)
    increment = restore(field)
    obs_product = unpack(back, target, rank)
    return (increment, obs_product)


def solution(mesh):
    placed = (
        P(None, None, "gx", "gy"),
        P(),
        P(("gx", "gy")),
        P(("gx", "gy")),
        P(("gx", "gy")),
        P(("gx", "gy")),
    )
    return jax.shard_map(
        body,
        mesh=mesh,
        in_specs=placed,
        out_specs=(P(None, "gx", "gy"), P(("gx", "gy"))),
        check_vma=False,
    )
```

```python
import jax
import jax.numpy as jnp
from jax import lax
from jax.experimental import pallas as pl
from jax.experimental.pallas import tpu as pltpu
from jax.sharding import PartitionSpec as P

F32 = jnp.float32
BF16 = jnp.bfloat16
I32 = jnp.int32

MEM, LEV, ROWS, COLS = 10, 90, 16, 256
PAD = 96
DEV = 128
CAP = 48
SLOTS = 2048
HALF = 128
QUARTER = 64
DUO = 2 * COLS
DUOS = MEM // 2
EDGE = 3
STRIP = 18
PAIRS = STRIP // 2
SELF = 1.0 / 6.0
SCALE = 0.24**3 / (MEM - 1)
VMEM = 20 * 1024 * 1024
MOST = 58 * 1024 * 1024


def split(value, count):
    parts = []
    for _ in range(count - 1):
        top = value.astype(BF16)
        parts.append(top)
        value = value - top.astype(F32)
    parts.append(value.astype(BF16))
    return parts


def dot(a, b):
    return lax.dot_general(a, b, (((1,), (0,)), ((), ())), preferred_element_type=F32)


def dot_nt(a, b):
    return lax.dot_general(a, b, (((1,), (1,)), ((), ())), preferred_element_type=F32)


def iota(shape, dim):
    return lax.broadcasted_iota(I32, shape, dim)


def one_hot(test):
    return jnp.where(test, 1.0, 0.0).astype(BF16)


def params(limit=VMEM):
    return pltpu.CompilerParams(vmem_limit_bytes=limit)


def cost(flops, moved):
    return pl.CostEstimate(flops=flops, bytes_accessed=moved, transcendentals=0)


def pack_kernel(count, dual, col, lev, vertical, out, tgt_out, rank_out, weights, left_v, left_c, right_v, right_c):
    wide = jnp.concatenate([vertical[...], jnp.zeros((LEV, PAD - LEV), F32)], axis=1)
    high, low = split(jnp.concatenate([wide, jnp.zeros((PAD - LEV, PAD), F32)], axis=0), 2)
    both = jnp.concatenate([low, jnp.zeros_like(low)], axis=1)
    weights[...] = jnp.concatenate([jnp.concatenate([high, high], axis=1), both], axis=0)
    number = count[0]
    lane = iota((DEV, COLS), 1)
    upper = one_hot((lane > iota((DEV, COLS), 0)) | (lane >= HALF))
    rows = iota((DEV, HALF), 0)
    lane = iota((1, HALF), 1)
    carry = jnp.zeros((DEV, HALF), F32)
    for i in range(SLOTS // HALF):
        at = slice(i * HALF, (i + 1) * HALF)
        column = col[i : i + 1, :]
        row = column >> 12
        gcol = column & 4095
        y = gcol & 255
        y = ((y & 3) << 6) + (y >> 2)
        target = ((row >> 4) << 4) + (gcol >> 8)
        target = jnp.where(i * HALF + lane < number, target, -1)
        hit = rows == target
        both = dot(one_hot(hit), upper)
        rank = jnp.sum(jnp.where(hit, both[:, :HALF] + carry, 0.0), axis=0, keepdims=True)
        carry = carry + both[:, HALF:]
        tgt_out[i : i + 1, :] = target
        rank = rank.astype(I32)
        rank_out[i : i + 1, :] = rank
        right_v[:, at] = one_hot(rows == rank)
        right_c[:, at] = one_hot(rows == rank + CAP)
        values = dual[i : i + 1, :]
        for p, piece in enumerate(split(values, 3)):
            left_v[p * DEV : (p + 1) * DEV, at] = jnp.where(hit, piece.astype(F32), 0.0).astype(BF16)
        cells = (lev[i : i + 1, :] << 12, (row & 15) << 8, y)
        for p, piece in enumerate(cells):
            left_c[p * DEV : (p + 1) * DEV, at] = jnp.where(hit, piece.astype(F32), 0.0).astype(BF16)
    a = dot_nt(left_v[...], right_v[...])
    b = dot_nt(left_c[...], right_c[...])
    out[...] = ((a[:DEV] + a[DEV : 2 * DEV]) + a[2 * DEV :]) + ((b[:DEV] + b[DEV : 2 * DEV]) + b[2 * DEV :])


def pack(count, dual, col, lev, vertical):
    spec = pl.BlockSpec(memory_space=pltpu.VMEM)
    return pl.pallas_call(
        pack_kernel,
        name="pack",
        out_shape=(
            jax.ShapeDtypeStruct((DEV, HALF), F32),
            jax.ShapeDtypeStruct((SLOTS // HALF, HALF), I32),
            jax.ShapeDtypeStruct((SLOTS // HALF, HALF), I32),
            jax.ShapeDtypeStruct((2 * PAD, 2 * PAD), BF16),
        ),
        in_specs=[pl.BlockSpec(memory_space=pltpu.SMEM)] + [spec] * 4,
        out_specs=(spec,) * 4,
        scratch_shapes=[pltpu.VMEM((3 * DEV, SLOTS), BF16)] * 2 + [pltpu.VMEM((DEV, SLOTS), BF16)] * 2,
        compiler_params=params(),
        cost_estimate=cost(10**9, 10**6),
    )(count, dual.reshape(-1, HALF), col.reshape(-1, HALF), lev.reshape(-1, HALF), vertical)


def unpack_kernel(back, tgt, rank, out):
    rows = iota((DEV, HALF), 0)
    table = jnp.concatenate(split(back[...], 3), axis=0)
    for i in range(SLOTS // HALF):
        found = dot(table, one_hot(rows == rank[i : i + 1, :]))
        found = (found[:DEV] + found[DEV : 2 * DEV]) + found[2 * DEV :]
        out[i : i + 1, :] = jnp.sum(jnp.where(rows == tgt[i : i + 1, :], found, 0.0), axis=0, keepdims=True)


def unpack(back, tgt, rank):
    spec = pl.BlockSpec(memory_space=pltpu.VMEM)
    return pl.pallas_call(
        unpack_kernel,
        name="unpack",
        out_shape=jax.ShapeDtypeStruct((SLOTS // HALF, HALF), F32),
        in_specs=[spec] * 3,
        out_specs=spec,
        compiler_params=params(),
        cost_estimate=cost(10**8, 10**5),
    )(back, tgt, rank).reshape(SLOTS)


def strip_place(lane):
    j = lane % HALF
    return j // PAIRS, jnp.where(j < MEM * PAIRS, j % PAIRS * 2 + lane // HALF, -1)


def natural(place):
    return ((place & 63) << 2) + (place >> 6)


def duo_place(place):
    return ((place & 63) << 2) + (place >> 7), (place >> 6) & 1


def widen(value):
    low = iota((value.shape[0], HALF), 1) < QUARTER
    phases = []
    for half in (value[:, :HALF], value[:, HALF:]):
        turned = pltpu.roll(half, QUARTER, 1)
        phases += [jnp.where(low, half, turned), jnp.where(low, turned, half)]
    return jnp.concatenate(phases, axis=1)


def fold(value):
    low = iota((value.shape[0], HALF), 1) < QUARTER
    p = [value[:, i * HALF : (i + 1) * HALF] for i in range(4)]
    return jnp.concatenate(
        [jnp.where(low, p[i], p[i + 1]) + pltpu.roll(jnp.where(low, p[i + 1], p[i]), QUARTER, 1) for i in (0, 2)],
        axis=1,
    )


def arrange_kernel(
    ens, out, up, down, strip, side_l, side_r, taken, rows, turned_out, up_out, down_out, strip_acc, perm_y, perm_r, sem, sem_out
):
    def fetch(k):
        return pltpu.make_async_copy(ens.at[k], taken.at[k], sem.at[k])

    def send(duo):
        slot = duo % 2
        return (
            pltpu.make_async_copy(turned_out.at[slot], out.at[duo], sem_out.at[0, slot]),
            pltpu.make_async_copy(up_out.at[slot], up.at[duo], sem_out.at[1, slot]),
            pltpu.make_async_copy(down_out.at[slot], down.at[duo], sem_out.at[2, slot]),
        )

    for k in range(MEM):
        fetch(k).start()
    rows[LEV * ROWS :, :] = jnp.zeros((rows.shape[0] - LEV * ROWS, DUO), BF16)
    strip_acc[...] = jnp.zeros_like(strip_acc)
    y, which = duo_place(iota((1, DUO), 1))
    perm_y[...] = one_hot(iota((DUO, DUO), 0) == which * COLS + y)
    i = iota((256, 1), 0)
    perm_r[...] = one_hot(iota((256, 256), 1) == (i & 15) * 16 + (i >> 4))

    @pl.loop(0, DUOS)
    def _(duo):
        @pl.when(duo >= 2)
        def _():
            for copy in send(duo - 2):
                copy.wait()

        fetch(2 * duo).wait()
        fetch(2 * duo + 1).wait()
        here, there, slot = 2 * duo, 2 * duo + 1, duo % 2
        y, which = duo_place(iota((DUO, COLS), 0))
        member, c = strip_place(iota((1, COLS), 1))
        want = jnp.where(y < 6, 3 + y, jnp.where(y >= 250, y - 241, -2))
        select = one_hot((member == 2 * duo + which) & (c == want))
        block = jnp.concatenate([taken[here], taken[there]], axis=1)
        rows[: LEV * ROWS, :] = dot(block, perm_y[...]).astype(BF16)
        for b in range(6):
            turned = dot(perm_r[...], rows[b * 256 : (b + 1) * 256, :])
            at = slice(b * 16, (b + 1) * 16)
            for x in range(ROWS):
                part = turned[x * 16 : (x + 1) * 16, :]
                turned_out[slot, x, at, :] = part.astype(BF16)
                if x < EDGE:
                    up_out[slot, x, at, :] = part
                if x >= ROWS - EDGE:
                    down_out[slot, x - (ROWS - EDGE), at, :] = part
        for copy in send(duo):
            copy.start()
        for x in range(ROWS):
            strip_acc[x] += dot(turned_out[slot, x], select)

    for duo in (DUOS - 2, DUOS - 1):
        for copy in send(duo):
            copy.wait()
    member, c = strip_place(iota((COLS, COLS), 0))
    left, right = (c >= 3) & (c < 6), (c >= 12) & (c < 15)
    spot = jnp.where(left, 3 * member + c - 3, jnp.where(right, HALF + 3 * member + c - 12, -1000))
    places = [one_hot(iota((COLS, COLS), 1) == spot + 30 * j) for j in range(4)]
    for group in range(4):
        sides = jnp.zeros((PAD, COLS), F32)
        for j in range(4):
            low = strip_acc[group * 4 + j].astype(BF16)
            strip[group * 4 + j] = low
            sides = sides + dot(low, places[j])
        side_l[group] = sides[:, :HALF]
        side_r[group] = sides[:, HALF:]


def arrange(ensemble):
    spec, far = pl.BlockSpec(memory_space=pltpu.VMEM), pl.BlockSpec(memory_space=pltpu.HBM)
    return pl.pallas_call(
        arrange_kernel,
        name="arrange",
        out_shape=(
            jax.ShapeDtypeStruct((DUOS, ROWS, PAD, DUO), BF16),
            jax.ShapeDtypeStruct((DUOS, EDGE, PAD, DUO), F32),
            jax.ShapeDtypeStruct((DUOS, EDGE, PAD, DUO), F32),
            jax.ShapeDtypeStruct((ROWS, PAD, COLS), BF16),
            jax.ShapeDtypeStruct((4, PAD, HALF), F32),
            jax.ShapeDtypeStruct((4, PAD, HALF), F32),
        ),
        in_specs=[far],
        out_specs=(far,) * 3 + (spec,) * 3,
        scratch_shapes=[
            pltpu.VMEM((MEM, LEV * ROWS, COLS), BF16),
            pltpu.VMEM((PAD * ROWS, DUO), BF16),
            pltpu.VMEM((2, ROWS, PAD, DUO), BF16),
            pltpu.VMEM((2, EDGE, PAD, DUO), F32),
            pltpu.VMEM((2, EDGE, PAD, DUO), F32),
            pltpu.VMEM((ROWS, PAD, COLS), F32),
            pltpu.VMEM((DUO, DUO), BF16),
            pltpu.VMEM((256, 256), BF16),
            pltpu.SemaphoreType.DMA((MEM,)),
            pltpu.SemaphoreType.DMA((3, 2)),
        ],
        compiler_params=params(MOST),
        cost_estimate=cost(10**10, 25 * 10**6),
    )(ensemble.reshape(MEM, LEV * ROWS, COLS))


KTILE = 1024


def scatter_kernel(incoming, ens_l, ens_r, out, wide, side_l, side_r, turned, hot1, hot2, acc):
    turned[...] = incoming[...].T
    acc[...] = jnp.zeros_like(acc)
    rows1 = iota((4 * PAD, HALF), 0)
    rows2 = iota((4 * COLS, HALF), 0)

    @pl.loop(0, CAP // 8)
    def _(j):
        first = pl.multiple_of(j * 8, 8)
        values = turned[pl.ds(first, 8), :]
        cells = turned[pl.ds(CAP + first, 8), :].astype(I32)
        for q in range(8):
            at = slice(q * HALF, (q + 1) * HALF)
            cell = cells[q : q + 1, :]
            key1 = ((cell >> 10) & 3) * PAD + (cell >> 12)
            hit = rows1 == key1
            for p, piece in enumerate(split(values[q : q + 1, :], 2)):
                hot1[p * 4 * PAD : (p + 1) * 4 * PAD, at] = jnp.where(hit, piece.astype(F32), 0.0).astype(BF16)
            hot2[:, at] = one_hot(rows2 == (cell & 1023))
        for n in range(4):
            cols = slice(n * COLS, (n + 1) * COLS)
            acc[:, cols] += dot_nt(hot1[...], hot2[cols, :])

    y = natural(iota((COLS, COLS), 0))
    lane = iota((COLS, COLS), 1)
    place = jnp.where(y < 3, y, jnp.where(y >= 253, HALF + y - 253, -1000))
    packed = jnp.zeros((PAD, COLS), F32)
    for x in range(ROWS):
        cols = slice(x % 4 * COLS, (x % 4 + 1) * COLS)
        level = x // 4 * PAD
        value = acc[level : level + PAD, cols] + acc[4 * PAD + level : 4 * PAD + level + PAD, cols]
        out[x] = value
        wide[x] = widen(value)
        select = one_hot(lane == place + 3 * x)
        for piece in split(value, 2):
            packed = packed + dot(piece, select)
    side_l[:4] = ens_l[...]
    side_r[:4] = ens_r[...]
    side_l[4] = packed[:, :HALF]
    side_r[4] = packed[:, HALF:]


def scatter(incoming, ens_l, ens_r):
    spec = pl.BlockSpec(memory_space=pltpu.VMEM)
    return pl.pallas_call(
        scatter_kernel,
        name="scatter",
        out_shape=(
            jax.ShapeDtypeStruct((ROWS, PAD, COLS), F32),
            jax.ShapeDtypeStruct((ROWS, PAD, DUO), F32),
            jax.ShapeDtypeStruct((5, PAD, HALF), F32),
            jax.ShapeDtypeStruct((5, PAD, HALF), F32),
        ),
        in_specs=[spec] * 3,
        out_specs=(spec,) * 4,
        scratch_shapes=[
            pltpu.VMEM((HALF, DEV), F32),
            pltpu.VMEM((8 * PAD, KTILE), BF16),
            pltpu.VMEM((4 * COLS, KTILE), BF16),
            pltpu.VMEM((8 * PAD, 4 * COLS), F32),
        ],
        compiler_params=params(),
        cost_estimate=cost(10**10, 2 * 10**6),
    )(incoming, ens_l, ens_r)


def strips_kernel(strip, adjoint, left, right, ens_out, out, up, down):
    member, member_c = strip_place(iota((COLS, COLS), 1))
    y = natural(iota((COLS, COLS), 0))
    own = one_hot(member_c == jnp.where(y < 6, 3 + y, jnp.where(y >= 250, y - 241, -2)))
    from_lane = iota((HALF, COLS), 0)
    member_c, member = member_c[:HALF], member[:HALF]
    pieces = [split(side[4], 2) for side in (left, right)]
    for x in range(ROWS):
        value = strip[x].astype(F32)
        first = x % 4 * 30 + 3 * member
        for side, shift in ((left, 0), (right, 15)):
            inside = (member_c >= shift) & (member_c < shift + 3)
            spot = one_hot(inside & (from_lane == first + member_c - shift))
            value = value + dot(side[x // 4].astype(BF16), spot)
        ens_out[x] = value.astype(BF16)
        if x < EDGE:
            up[2, x] = value
        if x >= ROWS - EDGE:
            down[2, x - (ROWS - EDGE)] = value
        value = jnp.zeros((PAD, COLS), F32)
        for piece in split(adjoint[x], 2):
            value = value + dot(piece, own)
        for side, shift in ((pieces[0], 0), (pieces[1], 15)):
            inside = (member_c >= shift) & (member_c < shift + 3)
            spot = one_hot(inside & (from_lane == 3 * x + member_c - shift))
            for piece in side:
                value = value + dot(piece, spot)
        out[x] = value
        if x < EDGE:
            up[0, x] = adjoint[x]
            up[1, x] = value
        if x >= ROWS - EDGE:
            down[0, x - (ROWS - EDGE)] = adjoint[x]
            down[1, x - (ROWS - EDGE)] = value


def strips(strip, adjoint, left, right):
    spec = pl.BlockSpec(memory_space=pltpu.VMEM)
    return pl.pallas_call(
        strips_kernel,
        name="strips",
        out_shape=(
            jax.ShapeDtypeStruct((ROWS, PAD, COLS), BF16),
            jax.ShapeDtypeStruct((ROWS, PAD, COLS), F32),
            jax.ShapeDtypeStruct((3, EDGE, PAD, COLS), F32),
            jax.ShapeDtypeStruct((3, EDGE, PAD, COLS), F32),
        ),
        in_specs=[spec] * 4,
        out_specs=(spec,) * 4,
        compiler_params=params(),
        cost_estimate=cost(10**9, 4 * 10**6),
    )(strip, adjoint, left, right)


def beside_permuted(value):
    even, odd = value[:, :HALF], value[:, HALF:]
    return jnp.concatenate([odd + pltpu.roll(odd, 1, 1), even + pltpu.roll(even, HALF - 1, 1)], axis=1)


def beside_duo(value):
    p = [value[:, i * HALF : (i + 1) * HALF] for i in range(4)]
    return jnp.concatenate(
        [pltpu.roll(p[3], 1, 1) + p[1], p[0] + p[2], p[1] + p[3], p[2] + pltpu.roll(p[0], HALF - 1, 1)], axis=1
    )


def total(terms):
    result = None
    for term in terms:
        if term is not None:
            result = term if result is None else result + term
    return result


def diffuse(get, given, wanted, beside, emit, mask=None):
    rows = [{} for _ in range(EDGE + 1)]
    for x in range(min(wanted) - EDGE, max(wanted) + EDGE + 1):
        if x in given:
            rows[0][x] = get(x)
        for step in range(1, EDGE + 1):
            at, reach, older = x - step, EDGE - step, rows[step - 1]
            if not min(wanted) - reach <= at <= max(wanted) + reach:
                continue
            terms = [older.get(at - 1), older.get(at + 1)]
            if at in older:
                terms += [beside(older[at]), older[at] * SELF]
            value = total(terms)
            if value is None:
                continue
            if step == EDGE:
                emit(at, value)
            else:
                rows[step][at] = value if mask is None else mask(at, value)


def put_split(ref, index, at, value):
    top = value.astype(BF16)
    ref[index, at, :] = top
    ref[index, pl.ds(at.start + PAD, 16), :] = (value - top.astype(F32)).astype(BF16)


def mix(weights, field):
    both = dot(weights, field)
    return both[:PAD] + both[PAD:]


INNER = ROWS - 2 * EDGE


def inner_kernel(start, count, ens, adj, weights, place, *refs):
    border, out, field, first, taken, sem = refs[-6:]

    def fetch(step):
        return pltpu.make_async_copy(ens.at[start + step], taken.at[step % 2], sem.at[step % 2])

    fetch(0).start()
    out[...] = refs[0][...] if start else jnp.zeros_like(out)
    top_open = jnp.where(place[0] == 0, 0.0, 1.0)
    bottom_open = jnp.where(place[0] == place[2], 0.0, 1.0)

    def mask(x, value):
        if x < 0:
            return value * top_open
        if x >= ROWS:
            return value * bottom_open
        return value

    @pl.loop(0, count)
    def _(step):
        @pl.when(step < count - 1)
        def _():
            fetch(step + 1).start()

        fetch(step).wait()
        slot = step % 2

        @pl.loop(0, PAD // 16)
        def _(group):
            at = pl.ds(pl.multiple_of(group * 16, 16), 16)

            for part in range(2):
                eight = pl.ds(pl.multiple_of(group * 16 + part * 8, 8), 8)

                def get(x):
                    return taken[slot, x, at, :].astype(F32)[part * 8 : part * 8 + 8, :] * adj[x, eight, :]

                def emit(x, value):
                    if not EDGE <= x < ROWS - EDGE:
                        border[step, x if x < EDGE else x - INNER, eight, :] = value
                    elif part == 0:
                        first[x - EDGE] = value
                    else:
                        put_split(field, x - EDGE, at, jnp.concatenate([first[x - EDGE], value], axis=0))

                diffuse(get, range(ROWS), range(ROWS), beside_duo, emit, mask)

        for x in range(INNER):
            out[x] += taken[slot, x + EDGE].astype(F32) * mix(weights[...], field[x])


def inner(ens, adj, weights, place, start, count, before=()):
    spec, far = pl.BlockSpec(memory_space=pltpu.VMEM), pl.BlockSpec(memory_space=pltpu.HBM)
    return pl.pallas_call(
        lambda *refs: inner_kernel(start, count, *refs),
        name="inner",
        out_shape=(
            jax.ShapeDtypeStruct((count, 2 * EDGE, PAD, DUO), F32),
            jax.ShapeDtypeStruct((INNER, PAD, DUO), F32),
        ),
        in_specs=[far, spec, spec, pl.BlockSpec(memory_space=pltpu.SMEM)] + [spec] * len(before),
        out_specs=(spec,) * 2,
        scratch_shapes=[
            pltpu.VMEM((INNER, 2 * PAD, DUO), BF16),
            pltpu.VMEM((INNER, 8, DUO), F32),
            pltpu.VMEM((2, ROWS, PAD, DUO), BF16),
            pltpu.SemaphoreType.DMA((2,)),
        ],
        compiler_params=params(),
        cost_estimate=cost(count * 2 * 10**9, count * 2 * 10**6),
    )(ens, adj, weights, place, *before)


def outer_kernel(
    ens, halo_t, halo_b, adj_t, adj_b, border0, border1, weights, out, field, first, wide, taken_e, taken_h, sem
):
    def fetch(duo):
        slot = duo % 2
        copies = (
            (ens.at[duo, pl.ds(0, EDGE)], taken_e.at[slot, pl.ds(0, EDGE)]),
            (ens.at[duo, pl.ds(ROWS - EDGE, EDGE)], taken_e.at[slot, pl.ds(EDGE, EDGE)]),
            (halo_t.at[duo], taken_h.at[slot, pl.ds(0, EDGE)]),
            (halo_b.at[duo], taken_h.at[slot, pl.ds(EDGE, EDGE)]),
        )
        return [pltpu.make_async_copy(a, b, sem.at[i, slot]) for i, (a, b) in enumerate(copies)]

    for copy in fetch(0):
        copy.start()
    out[...] = jnp.zeros_like(out)
    for x in range(EDGE):
        wide[x] = widen(adj_t[0, x])
        wide[EDGE + x] = widen(adj_b[0, x])

    for border, start in ((border0, 0), (border1, FIRST)):

        @pl.loop(0, border.shape[0])
        def _(step):
            duo = start + step
            slot = duo % 2

            @pl.when(duo < DUOS - 1)
            def _():
                for copy in fetch(duo + 1):
                    copy.start()

            for copy in fetch(duo):
                copy.wait()

            @pl.loop(0, PAD // 16)
            def _(group):
                at = pl.ds(pl.multiple_of(group * 16, 16), 16)

                for part in range(2):
                    eight = pl.ds(pl.multiple_of(group * 16 + part * 8, 8), 8)

                    def emit(x, value):
                        value = value + border[step, x, eight, :]
                        if part == 0:
                            first[x] = value
                        else:
                            put_split(field, x, at, jnp.concatenate([first[x], value], axis=0))

                    def get_t(x):
                        return taken_h[slot, x + EDGE, eight, :] * wide[x + EDGE, eight, :]

                    def get_b(x):
                        return taken_h[slot, x - EDGE, eight, :] * wide[x - EDGE, eight, :]

                    diffuse(get_t, range(-EDGE, 0), range(EDGE), beside_duo, emit)
                    diffuse(get_b, range(2 * EDGE, 3 * EDGE), range(EDGE, 2 * EDGE), beside_duo, emit)

            for x in range(2 * EDGE):
                out[x] += taken_e[slot, x].astype(F32) * mix(weights[...], field[x])


def outer(ens, halo_t, halo_b, adj_t, adj_b, border0, border1, weights):
    spec, far = pl.BlockSpec(memory_space=pltpu.VMEM), pl.BlockSpec(memory_space=pltpu.HBM)
    return pl.pallas_call(
        outer_kernel,
        name="outer",
        out_shape=jax.ShapeDtypeStruct((2 * EDGE, PAD, DUO), F32),
        in_specs=[far] * 3 + [spec] * 5,
        out_specs=spec,
        scratch_shapes=[
            pltpu.VMEM((2 * EDGE, 2 * PAD, DUO), BF16),
            pltpu.VMEM((2 * EDGE, 8, DUO), F32),
            pltpu.VMEM((2 * EDGE, PAD, DUO), F32),
            pltpu.VMEM((2, 2 * EDGE, PAD, DUO), BF16),
            pltpu.VMEM((2, 2 * EDGE, PAD, DUO), F32),
            pltpu.SemaphoreType.DMA((4, 2)),
        ],
        compiler_params=params(),
        cost_estimate=cost(MEM * 10**9, MEM * 3 * 10**6),
    )(ens, halo_t, halo_b, adj_t, adj_b, border0, border1, weights)


def edge_kernel(strip, adj, halo_t, halo_b, weights, place, inside, border, out, field):
    top_open = jnp.where(place[0] == 0, 0.0, 1.0)
    bottom_open = jnp.where(place[0] == place[2], 0.0, 1.0)
    left_open = jnp.where(place[1] == 0, 0.0, 1.0)
    right_open = jnp.where(place[1] == place[3], 0.0, 1.0)

    @pl.loop(0, PAD // 16)
    def _(group):
        at = pl.ds(pl.multiple_of(group * 16, 16), 16)
        c = strip_place(iota((16, COLS), 1))[1]
        lanes = jnp.where(c < 3, left_open, jnp.where(c >= 15, right_open, 1.0))

        def mask(x, value):
            value = value * lanes
            if x < 0:
                return value * top_open
            if x >= ROWS:
                return value * bottom_open
            return value

        def get(x):
            if x < 0:
                return halo_t[2, x + EDGE, at, :] * halo_t[1, x + EDGE, at, :]
            if x >= ROWS:
                return halo_b[2, x - ROWS, at, :] * halo_b[1, x - ROWS, at, :]
            return strip[x, at, :].astype(F32) * adj[x, at, :]

        def emit(x, value):
            put_split(field, x, at, value)

        diffuse(get, range(-EDGE, ROWS + EDGE), range(ROWS), beside_permuted, emit, mask)

    c = strip_place(iota((COLS, COLS), 0))[1]
    spot = jnp.where((c >= 3) & (c < 6), c - 3, jnp.where((c >= 12) & (c < 15), 241 + c, -1))
    collect = one_hot(spot == natural(iota((COLS, COLS), 1)))
    y = natural(iota((PAD, COLS), 1))
    middle = (y >= EDGE) & (y < COLS - EDGE)
    for x in range(ROWS):
        if EDGE <= x < ROWS - EDGE:
            value = inside[x - EDGE]
        else:
            value = border[x if x < EDGE else x - INNER]
        value = jnp.where(middle, fold(value), 0.0)
        product = strip[x].astype(F32) * mix(weights[...], field[x])
        for piece in split(product, 2):
            value = value + dot(piece, collect)
        out[x] = value * SCALE


def edge(strip, adj, halo_t, halo_b, weights, place, inside, border):
    spec = pl.BlockSpec(memory_space=pltpu.VMEM)
    return pl.pallas_call(
        edge_kernel,
        name="edge",
        out_shape=jax.ShapeDtypeStruct((ROWS, PAD, COLS), F32),
        in_specs=[spec] * 5 + [pl.BlockSpec(memory_space=pltpu.SMEM)] + [spec] * 2,
        out_specs=spec,
        scratch_shapes=[pltpu.VMEM((ROWS, 2 * PAD, COLS), BF16)],
        compiler_params=params(),
        cost_estimate=cost(4 * 10**9, 8 * 10**6),
    )(strip, adj, halo_t, halo_b, weights, place, inside, border)


def gather_kernel(field, incoming, out, turned, table, hot, picked):
    turned[...] = incoming[...].T
    picked[...] = jnp.zeros_like(picked)
    for x in range(ROWS):
        cols = slice(x % 4 * COLS, (x % 4 + 1) * COLS)
        for p, piece in enumerate(split(field[x], 2)):
            first = (p * 4 + x // 4) * PAD
            table[first : first + PAD, cols] = piece
    rows1 = iota((4 * PAD, COLS), 0)
    rows2 = iota((4 * COLS, COLS), 0)

    @pl.loop(0, CAP // 8)
    def _(j):
        first = pl.multiple_of(j * 8, 8)
        cells = turned[pl.ds(CAP + first, 8), :].astype(I32)
        lines = []
        for q in range(0, 8, 2):
            cell = jnp.concatenate([cells[q : q + 1, :], cells[q + 1 : q + 2, :]], axis=1)
            hot[...] = one_hot(rows2 == (cell & 1023))
            found = dot(table[...], hot[...])
            key1 = ((cell >> 10) & 3) * PAD + (cell >> 12)
            found = jnp.where(rows1 == key1, found[: 4 * PAD] + found[4 * PAD :], 0.0)
            found = jnp.sum(found, axis=0, keepdims=True)
            lines += [found[:, :HALF], found[:, HALF:]]
        picked[pl.ds(first, 8), :] = jnp.concatenate(lines, axis=0)

    out[...] = picked[...].T


def gather(field, incoming):
    spec = pl.BlockSpec(memory_space=pltpu.VMEM)
    return pl.pallas_call(
        gather_kernel,
        name="gather",
        out_shape=jax.ShapeDtypeStruct((DEV, HALF), F32),
        in_specs=[spec] * 2,
        out_specs=spec,
        scratch_shapes=[
            pltpu.VMEM((HALF, DEV), F32),
            pltpu.VMEM((8 * PAD, 4 * COLS), BF16),
            pltpu.VMEM((4 * COLS, COLS), BF16),
            pltpu.VMEM((HALF, DEV), F32),
        ],
        compiler_params=params(),
        cost_estimate=cost(10**10, 2 * 10**6),
    )(field, incoming)


def restore_kernel(field, out, rows):
    perm_y = one_hot(natural(iota((COLS, COLS), 0)) == iota((COLS, COLS), 1))
    i = iota((256, 1), 0)
    perm_r = one_hot(iota((256, 256), 1) == (i & 15) * 16 + (i >> 4))
    for x in range(ROWS):
        value = field[x]
        high, low = split(value, 2)
        rows[x] = dot(high, perm_y) + dot(low, perm_y)
    for b in range(6):
        block = jnp.concatenate([rows[x, b * 16 : (b + 1) * 16, :] for x in range(ROWS)], axis=0)
        high, low = split(block, 2)
        value = dot(perm_r, high) + dot(perm_r, low)
        if b < 5:
            out[b * 256 : (b + 1) * 256, :] = value
        else:
            out[1280:1440, :] = value[:160]


def restore(field):
    spec = pl.BlockSpec(memory_space=pltpu.VMEM)
    return pl.pallas_call(
        restore_kernel,
        name="restore",
        out_shape=jax.ShapeDtypeStruct((LEV * ROWS, COLS), F32),
        in_specs=[spec],
        out_specs=spec,
        scratch_shapes=[pltpu.VMEM((ROWS, PAD, COLS), F32)],
        compiler_params=params(),
        cost_estimate=cost(10**9, 3 * 10**6),
    )(field).reshape(LEV, ROWS, COLS)


def forward(value, axis):
    size = lax.axis_size(axis)
    return lax.ppermute(value, axis, [(i, i + 1) for i in range(size - 1)])


def backward(value, axis):
    size = lax.axis_size(axis)
    return lax.ppermute(value, axis, [(i + 1, i) for i in range(size - 1)])


FIRST = 2


def body(ensemble, vertical_weights, dual_vector, observed_column, observed_level, active_count):
    place = jnp.stack(
        [lax.axis_index("gx"), lax.axis_index("gy"), lax.axis_size("gx") - 1, lax.axis_size("gy") - 1]
    ).astype(I32)
    outgoing, target, rank, weights = pack(
        active_count, dual_vector, observed_column, observed_level, vertical_weights
    )
    ensemble, outgoing = lax.optimization_barrier((ensemble, outgoing))
    incoming = lax.all_to_all(outgoing, ("gx", "gy"), split_axis=0, concat_axis=0, tiled=True)
    ens, ens_up, ens_down, strip, ens_l, ens_r = arrange(ensemble)
    incoming, ens_up, ens_down = lax.optimization_barrier((incoming, ens_up, ens_down))
    halo_t = forward(ens_down, "gx")
    halo_b = backward(ens_up, "gx")

    adj, wide, side_l, side_r = scatter(incoming, ens_l, ens_r)
    from_left = forward(side_r, "gy")
    from_right = backward(side_l, "gy")
    border0, inside = inner(ens, wide, weights, place, 0, FIRST)
    from_left, from_right, inside = lax.optimization_barrier((from_left, from_right, inside))
    strip, adj_strip, up, down = strips(strip, adj, from_left, from_right)
    top = forward(down, "gx")
    bottom = backward(up, "gx")
    border1, inside = inner(ens, wide, weights, place, FIRST, DUOS - FIRST, (inside,))

    outside = outer(ens, halo_t, halo_b, top, bottom, border0, border1, weights)
    field = edge(strip, adj_strip, top, bottom, weights, place, inside, outside)
    picked = gather(field, incoming)
    back = lax.all_to_all(picked, ("gx", "gy"), split_axis=0, concat_axis=0, tiled=True)
    increment = restore(field)
    obs_product = unpack(back, target, rank)
    return (increment, obs_product)


def solution(mesh):
    placed = (
        P(None, None, "gx", "gy"),
        P(),
        P(("gx", "gy")),
        P(("gx", "gy")),
        P(("gx", "gy")),
        P(("gx", "gy")),
    )
    return jax.shard_map(
        body,
        mesh=mesh,
        in_specs=placed,
        out_specs=(P(None, "gx", "gy"), P(("gx", "gy"))),
        check_vma=False,
    )
```

```python
import jax
import jax.numpy as jnp
from jax import lax
from jax.experimental import pallas as pl
from jax.experimental.pallas import tpu as pltpu
from jax.sharding import PartitionSpec as P

F32 = jnp.float32
BF16 = jnp.bfloat16
I32 = jnp.int32

MEM, LEV, ROWS, COLS = 10, 90, 16, 256
PAD = 96
DEV = 128
CAP = 48
SLOTS = 2048
HALF = 128
QUARTER = 64
DUO = 2 * COLS
DUOS = MEM // 2
EDGE = 3
STRIP = 18
PAIRS = STRIP // 2
SELF = 1.0 / 6.0
SCALE = 0.24**3 / (MEM - 1)
VMEM = 20 * 1024 * 1024
MOST = 58 * 1024 * 1024
ALL = 63 * 1024 * 1024


def split(value, count):
    parts = []
    for _ in range(count - 1):
        top = value.astype(BF16)
        parts.append(top)
        value = value - top.astype(F32)
    parts.append(value.astype(BF16))
    return parts


def dot(a, b):
    return lax.dot_general(a, b, (((1,), (0,)), ((), ())), preferred_element_type=F32)


def dot_nt(a, b):
    return lax.dot_general(a, b, (((1,), (1,)), ((), ())), preferred_element_type=F32)


def iota(shape, dim):
    return lax.broadcasted_iota(I32, shape, dim)


def one_hot(test):
    return jnp.where(test, 1.0, 0.0).astype(BF16)


def params(limit=VMEM):
    return pltpu.CompilerParams(vmem_limit_bytes=limit)


def cost(flops, moved):
    return pl.CostEstimate(flops=flops, bytes_accessed=moved, transcendentals=0)


def pack_kernel(
    count, dual_far, col_far, lev_far, vertical_far, out, tgt_out, rank_out, weights, left_v, left_c, right_v, right_c, dual, col, lev, vertical, sem
):
    pairs = ((col_far, col), (lev_far, lev), (dual_far, dual), (vertical_far, vertical))
    copies = [pltpu.make_async_copy(a, b, sem.at[i]) for i, (a, b) in enumerate(pairs)]
    for copy in copies:
        copy.start()
    for copy in copies:
        copy.wait()
    wide = jnp.concatenate([vertical[...], jnp.zeros((LEV, PAD - LEV), F32)], axis=1)
    high, low = split(jnp.concatenate([wide, jnp.zeros((PAD - LEV, PAD), F32)], axis=0), 2)
    both = jnp.concatenate([low, jnp.zeros_like(low)], axis=1)
    weights[...] = jnp.concatenate([jnp.concatenate([high, high], axis=1), both], axis=0)
    number = count[0]
    lane = iota((DEV, COLS), 1)
    upper = one_hot((lane > iota((DEV, COLS), 0)) | (lane >= HALF))
    rows = iota((DEV, HALF), 0)
    lane = iota((1, HALF), 1)
    carry = jnp.zeros((DEV, HALF), F32)
    for i in range(SLOTS // HALF):
        at = slice(i * HALF, (i + 1) * HALF)
        column = col[i : i + 1, :]
        row = column >> 12
        gcol = column & 4095
        y = gcol & 255
        y = ((y & 3) << 6) + (y >> 2)
        target = ((row >> 4) << 4) + (gcol >> 8)
        target = jnp.where(i * HALF + lane < number, target, -1)
        hit = rows == target
        both = dot(one_hot(hit), upper)
        rank = jnp.sum(jnp.where(hit, both[:, :HALF] + carry, 0.0), axis=0, keepdims=True)
        carry = carry + both[:, HALF:]
        tgt_out[i : i + 1, :] = target
        rank = rank.astype(I32)
        rank_out[i : i + 1, :] = rank
        right_v[:, at] = one_hot(rows == rank)
        right_c[:, at] = one_hot(rows == rank + CAP)
        values = dual[i : i + 1, :]
        for p, piece in enumerate(split(values, 3)):
            left_v[p * DEV : (p + 1) * DEV, at] = jnp.where(hit, piece.astype(F32), 0.0).astype(BF16)
        cells = (lev[i : i + 1, :] << 12, (row & 15) << 8, y + 1)
        for p, piece in enumerate(cells):
            left_c[p * DEV : (p + 1) * DEV, at] = jnp.where(hit, piece.astype(F32), 0.0).astype(BF16)
    a = dot_nt(left_v[...], right_v[...])
    b = dot_nt(left_c[...], right_c[...])
    out[...] = ((a[:DEV] + a[DEV : 2 * DEV]) + a[2 * DEV :]) + ((b[:DEV] + b[DEV : 2 * DEV]) + b[2 * DEV :])


def pack(count, dual, col, lev, vertical):
    spec = pl.BlockSpec(memory_space=pltpu.VMEM)
    return pl.pallas_call(
        pack_kernel,
        name="pack",
        out_shape=(
            jax.ShapeDtypeStruct((DEV, HALF), F32),
            jax.ShapeDtypeStruct((SLOTS // HALF, HALF), I32),
            jax.ShapeDtypeStruct((SLOTS // HALF, HALF), I32),
            jax.ShapeDtypeStruct((2 * PAD, 2 * PAD), BF16),
        ),
        in_specs=[pl.BlockSpec(memory_space=pltpu.SMEM)] + [pl.BlockSpec(memory_space=pltpu.HBM)] * 4,
        out_specs=(spec,) * 4,
        scratch_shapes=[pltpu.VMEM((3 * DEV, SLOTS), BF16)] * 2
        + [pltpu.VMEM((DEV, SLOTS), BF16)] * 2
        + [pltpu.VMEM((SLOTS // HALF, HALF), kind) for kind in (F32, I32, I32)]
        + [pltpu.VMEM((LEV, LEV), F32), pltpu.SemaphoreType.DMA((4,))],
        compiler_params=params(ALL),
        cost_estimate=cost(10**9, 10**6),
    )(count, dual.reshape(-1, HALF), col.reshape(-1, HALF), lev.reshape(-1, HALF), vertical)


def unpack_kernel(back, tgt, rank, out):
    rows = iota((DEV, HALF), 0)
    table = jnp.concatenate(split(back[...], 3), axis=0)
    for i in range(SLOTS // HALF):
        found = dot(table, one_hot(rows == rank[i : i + 1, :]))
        found = (found[:DEV] + found[DEV : 2 * DEV]) + found[2 * DEV :]
        out[i : i + 1, :] = jnp.sum(jnp.where(rows == tgt[i : i + 1, :], found, 0.0), axis=0, keepdims=True)


def unpack(back, tgt, rank):
    spec = pl.BlockSpec(memory_space=pltpu.VMEM)
    return pl.pallas_call(
        unpack_kernel,
        name="unpack",
        out_shape=jax.ShapeDtypeStruct((SLOTS // HALF, HALF), F32),
        in_specs=[spec] * 3,
        out_specs=spec,
        compiler_params=params(),
        cost_estimate=cost(10**8, 10**5),
    )(back, tgt, rank).reshape(SLOTS)


def strip_place(lane):
    j = lane % HALF
    return j // PAIRS, jnp.where(j < MEM * PAIRS, j % PAIRS * 2 + lane // HALF, -1)


def natural(place):
    return ((place & 63) << 2) + (place >> 6)


def duo_place(place):
    return ((place & 63) << 2) + (place >> 7), (place >> 6) & 1


def widen(value):
    low = iota((value.shape[0], HALF), 1) < QUARTER
    phases = []
    for half in (value[:, :HALF], value[:, HALF:]):
        turned = pltpu.roll(half, QUARTER, 1)
        phases += [jnp.where(low, half, turned), jnp.where(low, turned, half)]
    return jnp.concatenate(phases, axis=1)


def fold(value):
    low = iota((value.shape[0], HALF), 1) < QUARTER
    p = [value[:, i * HALF : (i + 1) * HALF] for i in range(4)]
    return jnp.concatenate(
        [jnp.where(low, p[i], p[i + 1]) + pltpu.roll(jnp.where(low, p[i + 1], p[i]), QUARTER, 1) for i in (0, 2)],
        axis=1,
    )


def arrange_kernel(
    ens, out, up, down, strip, side_l, side_r, taken, rows, turned_out, up_out, down_out, strip_acc, perm_y, perm_r, sides_out, sem, sem_out
):
    def fetch(k):
        return pltpu.make_async_copy(ens.at[k], taken.at[k], sem.at[k])

    def send(duo):
        slot = duo % 2
        return (
            pltpu.make_async_copy(turned_out.at[slot], out.at[duo], sem_out.at[0, slot]),
            pltpu.make_async_copy(up_out.at[slot], up.at[duo], sem_out.at[1, slot]),
            pltpu.make_async_copy(down_out.at[slot], down.at[duo], sem_out.at[2, slot]),
        )

    for k in range(MEM):
        fetch(k).start()
    rows[LEV * ROWS :, :] = jnp.zeros((rows.shape[0] - LEV * ROWS, DUO), BF16)
    strip_acc[...] = jnp.zeros_like(strip_acc)
    y, which = duo_place(iota((1, DUO), 1))
    perm_y[...] = one_hot(iota((DUO, DUO), 0) == which * COLS + y)
    i = iota((256, 1), 0)
    perm_r[...] = one_hot(iota((256, 256), 1) == (i & 15) * 16 + (i >> 4))

    @pl.loop(0, DUOS)
    def _(duo):
        @pl.when(duo >= 2)
        def _():
            for copy in send(duo - 2):
                copy.wait()

        fetch(2 * duo).wait()
        fetch(2 * duo + 1).wait()
        here, there, slot = 2 * duo, 2 * duo + 1, duo % 2
        y, which = duo_place(iota((DUO, COLS), 0))
        member, c = strip_place(iota((1, COLS), 1))
        want = jnp.where(y < 6, 3 + y, jnp.where(y >= 250, y - 241, -2))
        select = one_hot((member == 2 * duo + which) & (c == want))
        block = jnp.concatenate([taken[here], taken[there]], axis=1)
        rows[: LEV * ROWS, :] = dot(block, perm_y[...]).astype(BF16)
        for b in range(6):
            turned = dot(perm_r[...], rows[b * 256 : (b + 1) * 256, :])
            at = slice(b * 16, (b + 1) * 16)
            for x in range(ROWS):
                part = turned[x * 16 : (x + 1) * 16, :]
                turned_out[slot, x, at, :] = part.astype(BF16)
                if x < EDGE:
                    up_out[slot, x, at, :] = part
                if x >= ROWS - EDGE:
                    down_out[slot, x - (ROWS - EDGE), at, :] = part
        for copy in send(duo):
            copy.start()
        for x in range(ROWS):
            strip_acc[x] += dot(turned_out[slot, x], select)

    for duo in (DUOS - 2, DUOS - 1):
        for copy in send(duo):
            copy.wait()
    member, c = strip_place(iota((COLS, COLS), 0))
    left, right = (c >= 3) & (c < 6), (c >= 12) & (c < 15)
    spot = jnp.where(left, 3 * member + c - 3, jnp.where(right, HALF + 3 * member + c - 12, -1000))
    places = [one_hot(iota((COLS, COLS), 1) == spot + 30 * j) for j in range(4)]
    places = [one_hot(iota((COLS, COLS), 1) == spot + 30 * j) for j in range(4)]
    for group in range(4):
        sides = jnp.zeros((PAD, COLS), F32)
        for j in range(4):
            low = strip_acc[group * 4 + j].astype(BF16)
            strip[group * 4 + j] = low
            sides = sides + dot(low, places[j])
        sides_out[0, group] = sides[:, :HALF]
        sides_out[1, group] = sides[:, HALF:]
    copies = [
        pltpu.make_async_copy(sides_out.at[i], side.at[pl.ds(0, 4)], sem_out.at[0, i]) for i, side in enumerate((side_l, side_r))
    ]
    for copy in copies:
        copy.start()
    for copy in copies:
        copy.wait()


def arrange(ensemble):
    spec, far = pl.BlockSpec(memory_space=pltpu.VMEM), pl.BlockSpec(memory_space=pltpu.HBM)
    return pl.pallas_call(
        arrange_kernel,
        name="arrange",
        out_shape=(
            jax.ShapeDtypeStruct((DUOS, ROWS, PAD, DUO), BF16),
            jax.ShapeDtypeStruct((DUOS, EDGE, PAD, DUO), F32),
            jax.ShapeDtypeStruct((DUOS, EDGE, PAD, DUO), F32),
            jax.ShapeDtypeStruct((ROWS, PAD, COLS), BF16),
            jax.ShapeDtypeStruct((5, PAD, HALF), F32),
            jax.ShapeDtypeStruct((5, PAD, HALF), F32),
        ),
        in_specs=[far],
        out_specs=(far, far, far, spec, far, far),
        scratch_shapes=[
            pltpu.VMEM((MEM, LEV * ROWS, COLS), BF16),
            pltpu.VMEM((PAD * ROWS, DUO), BF16),
            pltpu.VMEM((2, ROWS, PAD, DUO), BF16),
            pltpu.VMEM((2, EDGE, PAD, DUO), F32),
            pltpu.VMEM((2, EDGE, PAD, DUO), F32),
            pltpu.VMEM((ROWS, PAD, COLS), F32),
            pltpu.VMEM((DUO, DUO), BF16),
            pltpu.VMEM((256, 256), BF16),
            pltpu.VMEM((2, 4, PAD, HALF), F32),
            pltpu.SemaphoreType.DMA((MEM,)),
            pltpu.SemaphoreType.DMA((3, 2)),
        ],
        compiler_params=params(MOST),
        cost_estimate=cost(10**10, 25 * 10**6),
    )(ensemble.reshape(MEM, LEV * ROWS, COLS))


CHUNKS = CAP // 2
TILES = CHUNKS + ROWS
SPACE = 48


def scatter_kernel(
    incoming, ens_l, ens_r, out, wide, side_l, side_r, level_out, column_out, pos_out, row_out,
    turned, hot, left, right, rows_of, sorted_, sides_out, sem
):
    turned[...] = incoming[...].T
    pairs = [[turned[pl.ds(first + i, CHUNKS, stride=2), :] for i in range(2)] for first in (0, CAP)]
    values = jnp.concatenate(pairs[0], axis=1)
    cells = jnp.concatenate(pairs[1], axis=1).astype(I32) - 1
    full = cells >= 0
    x = jnp.where(full, (cells >> 8) & 15, 99)

    for c in range(CHUNKS):
        hot[c * ROWS : (c + 1) * ROWS, :] = one_hot(iota((ROWS, COLS), 0) == x[c : c + 1, :])
    size = CHUNKS * ROWS
    lane = iota((COLS, COLS + HALF), 1)
    both = dot(hot[...], one_hot((lane > iota((COLS, COLS + HALF), 0)) | (lane >= COLS)))
    count = both[:, COLS:].astype(BF16)
    here, there = iota((size, size), 0), iota((size, size), 1)
    same = (here & 15) == (there & 15)
    earlier = dot(one_hot(same & (there < here)), count)
    needed = (dot(one_hot(same), count).astype(I32) + 255) >> 8
    start = dot(one_hot(((there & 15) < (here & 15)) & (there < ROWS)), needed.astype(F32).astype(BF16))
    base = start * 256.0 + earlier
    place = both[:, :COLS] + jnp.concatenate([base, base], axis=1)
    place = jnp.where(hot[...].astype(F32) > 0.5, place, 0.0)
    pos = jnp.sum(place.reshape(CHUNKS, ROWS, COLS), axis=1).astype(I32)
    pos = jnp.where(full, pos, -1)
    pos_out[...] = pos
    begun = jnp.where(start[:ROWS].astype(I32) <= iota((ROWS, HALF), 1), 1.0, 0.0)
    row_out[...] = jnp.sum(begun, axis=0, keepdims=True).astype(I32) - 1
    copy = pltpu.make_async_copy(row_out, rows_of, sem.at[0])
    copy.start()

    parts = [p.astype(F32) for p in split(values, 2)] + [(cells >> 12).astype(F32), (cells & 255).astype(F32)]
    tile, spot = pos >> 8, pos & 255
    for c in range(CHUNKS):
        at = slice(c * COLS, (c + 1) * COLS)
        hit = iota((SPACE, COLS), 0) == tile[c : c + 1, :]
        for p, part in enumerate(parts):
            left[p * SPACE : (p + 1) * SPACE, at] = jnp.where(hit, part[c : c + 1, :], 0.0).astype(BF16)
        right[:, at] = one_hot(iota((COLS, COLS), 0) == spot[c : c + 1, :])
    sorted_[...] = dot_nt(left[...], right[...])
    level_out[...] = sorted_[2 * SPACE : 3 * SPACE, :]
    column_out[...] = sorted_[3 * SPACE :, :]
    out[...] = jnp.zeros_like(out)
    copy.wait()

    @pl.loop(0, TILES // 8)
    def _(j):
        high, low, level, column = (sorted_[pl.ds(pl.multiple_of(p * SPACE + j * 8, 8), 8), :] for p in range(4))
        level, column = level.astype(I32), column.astype(I32)
        for half in range(2):
            results = []
            for q in range(half * 4, half * 4 + 4):
                at = slice(q, q + 1)
                hit = iota((PAD, COLS), 0) == level[at, :]
                lhs = jnp.concatenate([jnp.where(hit, high[at, :], 0.0), jnp.where(hit, low[at, :], 0.0)], axis=0)
                both = dot_nt(lhs.astype(BF16), one_hot(iota((COLS, COLS), 0) == column[at, :]))
                results.append(both[:PAD] + both[PAD:])
            for i, result in enumerate(results):
                out[rows_of[0, j * 8 + half * 4 + i]] += result

    y = natural(iota((COLS, COLS), 0))
    lane = iota((COLS, COLS), 1)
    place = jnp.where(y < 3, y, jnp.where(y >= 253, HALF + y - 253, -1000))
    packed = jnp.zeros((PAD, COLS), F32)
    for x in range(ROWS):
        value = out[x]
        wide[x] = widen(value)
        select = one_hot(lane == place + 3 * x)
        for piece in split(value, 2):
            packed = packed + dot(piece, select)
    sides_out[0] = packed[:, :HALF]
    sides_out[1] = packed[:, HALF:]
    copies = [pltpu.make_async_copy(sides_out.at[i], side.at[4], sem.at[i]) for i, side in enumerate((side_l, side_r))]
    for copy in copies:
        copy.start()
    for copy in copies:
        copy.wait()


def scatter(incoming, ens_l, ens_r):
    spec, far = pl.BlockSpec(memory_space=pltpu.VMEM), pl.BlockSpec(memory_space=pltpu.HBM)
    return pl.pallas_call(
        scatter_kernel,
        name="scatter",
        out_shape=(
            jax.ShapeDtypeStruct((ROWS, PAD, COLS), F32),
            jax.ShapeDtypeStruct((ROWS, PAD, DUO), F32),
            jax.ShapeDtypeStruct((5, PAD, HALF), F32),
            jax.ShapeDtypeStruct((5, PAD, HALF), F32),
            jax.ShapeDtypeStruct((SPACE, COLS), F32),
            jax.ShapeDtypeStruct((SPACE, COLS), F32),
            jax.ShapeDtypeStruct((CHUNKS, COLS), I32),
            jax.ShapeDtypeStruct((1, HALF), I32),
        ),
        in_specs=[spec, far, far],
        out_specs=(spec, spec, far, far, spec, spec, spec, spec),
        input_output_aliases={1: 2, 2: 3},
        scratch_shapes=[
            pltpu.VMEM((HALF, DEV), F32),
            pltpu.VMEM((CHUNKS * ROWS, COLS), BF16),
            pltpu.VMEM((4 * SPACE, CHUNKS * COLS), BF16),
            pltpu.VMEM((COLS, CHUNKS * COLS), BF16),
            pltpu.SMEM((1, HALF), I32),
            pltpu.VMEM((4 * SPACE, COLS), F32),
            pltpu.VMEM((2, PAD, HALF), F32),
            pltpu.SemaphoreType.DMA((2,)),
        ],
        compiler_params=params(),
        cost_estimate=cost(10**10, 2 * 10**6),
    )(incoming, ens_l, ens_r)


def strips_kernel(strip, adjoint, left, right, ens_out, out, up, down):
    member, member_c = strip_place(iota((COLS, COLS), 1))
    y = natural(iota((COLS, COLS), 0))
    own = one_hot(member_c == jnp.where(y < 6, 3 + y, jnp.where(y >= 250, y - 241, -2)))
    from_lane = iota((HALF, COLS), 0)
    member_c, member = member_c[:HALF], member[:HALF]
    pieces = [split(side[4], 2) for side in (left, right)]
    for x in range(ROWS):
        value = strip[x].astype(F32)
        first = x % 4 * 30 + 3 * member
        for side, shift in ((left, 0), (right, 15)):
            inside = (member_c >= shift) & (member_c < shift + 3)
            spot = one_hot(inside & (from_lane == first + member_c - shift))
            value = value + dot(side[x // 4].astype(BF16), spot)
        ens_out[x] = value.astype(BF16)
        if x < EDGE:
            up[2, x] = value
        if x >= ROWS - EDGE:
            down[2, x - (ROWS - EDGE)] = value
        value = jnp.zeros((PAD, COLS), F32)
        for piece in split(adjoint[x], 2):
            value = value + dot(piece, own)
        for side, shift in ((pieces[0], 0), (pieces[1], 15)):
            inside = (member_c >= shift) & (member_c < shift + 3)
            spot = one_hot(inside & (from_lane == 3 * x + member_c - shift))
            for piece in side:
                value = value + dot(piece, spot)
        out[x] = value
        if x < EDGE:
            up[0, x] = adjoint[x]
            up[1, x] = value
        if x >= ROWS - EDGE:
            down[0, x - (ROWS - EDGE)] = adjoint[x]
            down[1, x - (ROWS - EDGE)] = value


def strips(strip, adjoint, left, right):
    spec = pl.BlockSpec(memory_space=pltpu.VMEM)
    return pl.pallas_call(
        strips_kernel,
        name="strips",
        out_shape=(
            jax.ShapeDtypeStruct((ROWS, PAD, COLS), BF16),
            jax.ShapeDtypeStruct((ROWS, PAD, COLS), F32),
            jax.ShapeDtypeStruct((3, EDGE, PAD, COLS), F32),
            jax.ShapeDtypeStruct((3, EDGE, PAD, COLS), F32),
        ),
        in_specs=[spec] * 4,
        out_specs=(spec,) * 4,
        compiler_params=params(),
        cost_estimate=cost(10**9, 4 * 10**6),
    )(strip, adjoint, left, right)


def beside_permuted(value):
    even, odd = value[:, :HALF], value[:, HALF:]
    return jnp.concatenate([odd + pltpu.roll(odd, 1, 1), even + pltpu.roll(even, HALF - 1, 1)], axis=1)


def beside_duo(value):
    p = [value[:, i * HALF : (i + 1) * HALF] for i in range(4)]
    return jnp.concatenate(
        [pltpu.roll(p[3], 1, 1) + p[1], p[0] + p[2], p[1] + p[3], p[2] + pltpu.roll(p[0], HALF - 1, 1)], axis=1
    )


def total(terms):
    result = None
    for term in terms:
        if term is not None:
            result = term if result is None else result + term
    return result


def diffuse(get, given, wanted, beside, emit, mask=None):
    rows = [{} for _ in range(EDGE + 1)]
    for x in range(min(wanted) - EDGE, max(wanted) + EDGE + 1):
        if x in given:
            rows[0][x] = get(x)
        for step in range(1, EDGE + 1):
            at, reach, older = x - step, EDGE - step, rows[step - 1]
            if not min(wanted) - reach <= at <= max(wanted) + reach:
                continue
            terms = [older.get(at - 1), older.get(at + 1)]
            if at in older:
                terms += [beside(older[at]), older[at] * SELF]
            value = total(terms)
            if value is None:
                continue
            if step == EDGE:
                emit(at, value)
            else:
                rows[step][at] = value if mask is None else mask(at, value)


def put_split(ref, index, at, value):
    top = value.astype(BF16)
    ref[index, at, :] = top
    ref[index, pl.ds(at.start + PAD, 16), :] = (value - top.astype(F32)).astype(BF16)


def mix(weights, field):
    both = dot(weights, field)
    return both[:PAD] + both[PAD:]


INNER = ROWS - 2 * EDGE


def inner_kernel(start, count, ens, adj, weights, place, *refs):
    border, out, field, first, taken, sem = refs[-6:]

    def fetch(step):
        return pltpu.make_async_copy(ens.at[start + step], taken.at[step % 2], sem.at[step % 2])

    fetch(0).start()
    out[...] = refs[0][...] if start else jnp.zeros_like(out)
    top_open = jnp.where(place[0] == 0, 0.0, 1.0)
    bottom_open = jnp.where(place[0] == place[2], 0.0, 1.0)

    def mask(x, value):
        if x < 0:
            return value * top_open
        if x >= ROWS:
            return value * bottom_open
        return value

    @pl.loop(0, count)
    def _(step):
        @pl.when(step < count - 1)
        def _():
            fetch(step + 1).start()

        fetch(step).wait()
        slot = step % 2

        @pl.loop(0, PAD // 16)
        def _(group):
            at = pl.ds(pl.multiple_of(group * 16, 16), 16)

            for part in range(2):
                eight = pl.ds(pl.multiple_of(group * 16 + part * 8, 8), 8)

                def get(x):
                    return taken[slot, x, at, :].astype(F32)[part * 8 : part * 8 + 8, :] * adj[x, eight, :]

                def emit(x, value):
                    if not EDGE <= x < ROWS - EDGE:
                        border[step, x if x < EDGE else x - INNER, eight, :] = value
                    elif part == 0:
                        first[x - EDGE] = value
                    else:
                        put_split(field, x - EDGE, at, jnp.concatenate([first[x - EDGE], value], axis=0))

                diffuse(get, range(ROWS), range(ROWS), beside_duo, emit, mask)

        for x in range(INNER):
            out[x] += taken[slot, x + EDGE].astype(F32) * mix(weights[...], field[x])


def inner(ens, adj, weights, place, start, count, before=()):
    spec, far = pl.BlockSpec(memory_space=pltpu.VMEM), pl.BlockSpec(memory_space=pltpu.HBM)
    return pl.pallas_call(
        lambda *refs: inner_kernel(start, count, *refs),
        name="inner",
        out_shape=(
            jax.ShapeDtypeStruct((count, 2 * EDGE, PAD, DUO), F32),
            jax.ShapeDtypeStruct((INNER, PAD, DUO), F32),
        ),
        in_specs=[far, spec, spec, pl.BlockSpec(memory_space=pltpu.SMEM)] + [spec] * len(before),
        out_specs=(spec,) * 2,
        scratch_shapes=[
            pltpu.VMEM((INNER, 2 * PAD, DUO), BF16),
            pltpu.VMEM((INNER, 8, DUO), F32),
            pltpu.VMEM((2, ROWS, PAD, DUO), BF16),
            pltpu.SemaphoreType.DMA((2,)),
        ],
        compiler_params=params(),
        cost_estimate=cost(count * 2 * 10**9, count * 2 * 10**6),
    )(ens, adj, weights, place, *before)


def outer_kernel(
    ens, halo_t, halo_b, adj_t, adj_b, border0, border1, weights, out, field, first, wide, taken_e, taken_h, sem
):
    def fetch(duo):
        slot = duo % 2
        copies = (
            (ens.at[duo, pl.ds(0, EDGE)], taken_e.at[slot, pl.ds(0, EDGE)]),
            (ens.at[duo, pl.ds(ROWS - EDGE, EDGE)], taken_e.at[slot, pl.ds(EDGE, EDGE)]),
            (halo_t.at[duo], taken_h.at[slot, pl.ds(0, EDGE)]),
            (halo_b.at[duo], taken_h.at[slot, pl.ds(EDGE, EDGE)]),
        )
        return [pltpu.make_async_copy(a, b, sem.at[i, slot]) for i, (a, b) in enumerate(copies)]

    for copy in fetch(0):
        copy.start()
    out[...] = jnp.zeros_like(out)
    for x in range(EDGE):
        wide[x] = widen(adj_t[0, x])
        wide[EDGE + x] = widen(adj_b[0, x])

    for border, start in ((border0, 0), (border1, FIRST)):

        @pl.loop(0, border.shape[0])
        def _(step):
            duo = start + step
            slot = duo % 2

            @pl.when(duo < DUOS - 1)
            def _():
                for copy in fetch(duo + 1):
                    copy.start()

            for copy in fetch(duo):
                copy.wait()

            @pl.loop(0, PAD // 16)
            def _(group):
                at = pl.ds(pl.multiple_of(group * 16, 16), 16)

                for part in range(2):
                    eight = pl.ds(pl.multiple_of(group * 16 + part * 8, 8), 8)

                    def emit(x, value):
                        value = value + border[step, x, eight, :]
                        if part == 0:
                            first[x] = value
                        else:
                            put_split(field, x, at, jnp.concatenate([first[x], value], axis=0))

                    def get_t(x):
                        return taken_h[slot, x + EDGE, eight, :] * wide[x + EDGE, eight, :]

                    def get_b(x):
                        return taken_h[slot, x - EDGE, eight, :] * wide[x - EDGE, eight, :]

                    diffuse(get_t, range(-EDGE, 0), range(EDGE), beside_duo, emit)
                    diffuse(get_b, range(2 * EDGE, 3 * EDGE), range(EDGE, 2 * EDGE), beside_duo, emit)

            for x in range(2 * EDGE):
                out[x] += taken_e[slot, x].astype(F32) * mix(weights[...], field[x])


def outer(ens, halo_t, halo_b, adj_t, adj_b, border0, border1, weights):
    spec, far = pl.BlockSpec(memory_space=pltpu.VMEM), pl.BlockSpec(memory_space=pltpu.HBM)
    return pl.pallas_call(
        outer_kernel,
        name="outer",
        out_shape=jax.ShapeDtypeStruct((2 * EDGE, PAD, DUO), F32),
        in_specs=[far] * 3 + [spec] * 5,
        out_specs=spec,
        scratch_shapes=[
            pltpu.VMEM((2 * EDGE, 2 * PAD, DUO), BF16),
            pltpu.VMEM((2 * EDGE, 8, DUO), F32),
            pltpu.VMEM((2 * EDGE, PAD, DUO), F32),
            pltpu.VMEM((2, 2 * EDGE, PAD, DUO), BF16),
            pltpu.VMEM((2, 2 * EDGE, PAD, DUO), F32),
            pltpu.SemaphoreType.DMA((4, 2)),
        ],
        compiler_params=params(),
        cost_estimate=cost(MEM * 10**9, MEM * 3 * 10**6),
    )(ens, halo_t, halo_b, adj_t, adj_b, border0, border1, weights)


def edge_kernel(strip, adj, halo_t, halo_b, weights, place, inside, border, out, field):
    top_open = jnp.where(place[0] == 0, 0.0, 1.0)
    bottom_open = jnp.where(place[0] == place[2], 0.0, 1.0)
    left_open = jnp.where(place[1] == 0, 0.0, 1.0)
    right_open = jnp.where(place[1] == place[3], 0.0, 1.0)

    @pl.loop(0, PAD // 16)
    def _(group):
        at = pl.ds(pl.multiple_of(group * 16, 16), 16)
        c = strip_place(iota((16, COLS), 1))[1]
        lanes = jnp.where(c < 3, left_open, jnp.where(c >= 15, right_open, 1.0))

        def mask(x, value):
            value = value * lanes
            if x < 0:
                return value * top_open
            if x >= ROWS:
                return value * bottom_open
            return value

        def get(x):
            if x < 0:
                return halo_t[2, x + EDGE, at, :] * halo_t[1, x + EDGE, at, :]
            if x >= ROWS:
                return halo_b[2, x - ROWS, at, :] * halo_b[1, x - ROWS, at, :]
            return strip[x, at, :].astype(F32) * adj[x, at, :]

        def emit(x, value):
            put_split(field, x, at, value)

        diffuse(get, range(-EDGE, ROWS + EDGE), range(ROWS), beside_permuted, emit, mask)

    c = strip_place(iota((COLS, COLS), 0))[1]
    spot = jnp.where((c >= 3) & (c < 6), c - 3, jnp.where((c >= 12) & (c < 15), 241 + c, -1))
    collect = one_hot(spot == natural(iota((COLS, COLS), 1)))
    y = natural(iota((PAD, COLS), 1))
    middle = (y >= EDGE) & (y < COLS - EDGE)
    for x in range(ROWS):
        if EDGE <= x < ROWS - EDGE:
            value = inside[x - EDGE]
        else:
            value = border[x if x < EDGE else x - INNER]
        value = jnp.where(middle, fold(value), 0.0)
        product = strip[x].astype(F32) * mix(weights[...], field[x])
        for piece in split(product, 2):
            value = value + dot(piece, collect)
        out[x] = value * SCALE


def edge(strip, adj, halo_t, halo_b, weights, place, inside, border):
    spec = pl.BlockSpec(memory_space=pltpu.VMEM)
    return pl.pallas_call(
        edge_kernel,
        name="edge",
        out_shape=jax.ShapeDtypeStruct((ROWS, PAD, COLS), F32),
        in_specs=[spec] * 5 + [pl.BlockSpec(memory_space=pltpu.SMEM)] + [spec] * 2,
        out_specs=spec,
        scratch_shapes=[pltpu.VMEM((ROWS, 2 * PAD, COLS), BF16)],
        compiler_params=params(),
        cost_estimate=cost(4 * 10**9, 8 * 10**6),
    )(strip, adj, halo_t, halo_b, weights, place, inside, border)


def gather_kernel(field, level, column, pos, rows_of, out, table, picked):
    for x in range(ROWS):
        table[x, :PAD, :], table[x, PAD:, :] = split(field[x], 2)
    picked[...] = jnp.zeros_like(picked)

    @pl.loop(0, TILES // 8)
    def _(j):
        first = pl.multiple_of(j * 8, 8)
        levels, columns = level[pl.ds(first, 8), :].astype(I32), column[pl.ds(first, 8), :].astype(I32)
        lines = []
        for q in range(8):
            at = slice(q, q + 1)
            found = dot(table[rows_of[0, j * 8 + q]], one_hot(iota((COLS, COLS), 0) == columns[at, :]))
            found = jnp.where(iota((PAD, COLS), 0) == levels[at, :], found[:PAD] + found[PAD:], 0.0)
            lines.append(jnp.sum(found, axis=0, keepdims=True))
        picked[pl.ds(first, 8), :] = jnp.concatenate(lines, axis=0)

    both = jnp.concatenate(split(picked[...], 2), axis=0)
    tile, spot = pos[...] >> 8, pos[...] & 255
    lines = []
    for c in range(CHUNKS):
        found = dot(both, one_hot(iota((COLS, COLS), 0) == spot[c : c + 1, :]))
        found = jnp.where(iota((SPACE, COLS), 0) == tile[c : c + 1, :], found[:SPACE] + found[SPACE:], 0.0)
        found = jnp.sum(found, axis=0, keepdims=True)
        lines += [found[:, :HALF], found[:, HALF:]]
    out[...] = jnp.concatenate(lines + [jnp.zeros((HALF - CAP, DEV), F32)], axis=0).T


def gather(field, level, column, pos, rows_of):
    spec = pl.BlockSpec(memory_space=pltpu.VMEM)
    return pl.pallas_call(
        gather_kernel,
        name="gather",
        out_shape=jax.ShapeDtypeStruct((DEV, HALF), F32),
        in_specs=[spec] * 4 + [pl.BlockSpec(memory_space=pltpu.SMEM)],
        out_specs=spec,
        scratch_shapes=[
            pltpu.VMEM((ROWS, 2 * PAD, COLS), BF16),
            pltpu.VMEM((SPACE, COLS), F32),
        ],
        compiler_params=params(),
        cost_estimate=cost(10**10, 2 * 10**6),
    )(field, level, column, pos, rows_of)


def restore_kernel(field, out, rows):
    perm_y = one_hot(natural(iota((COLS, COLS), 0)) == iota((COLS, COLS), 1))
    i = iota((256, 1), 0)
    perm_r = one_hot(iota((256, 256), 1) == (i & 15) * 16 + (i >> 4))
    for x in range(ROWS):
        value = field[x]
        high, low = split(value, 2)
        rows[x] = dot(high, perm_y) + dot(low, perm_y)
    for b in range(6):
        block = jnp.concatenate([rows[x, b * 16 : (b + 1) * 16, :] for x in range(ROWS)], axis=0)
        high, low = split(block, 2)
        value = dot(perm_r, high) + dot(perm_r, low)
        if b < 5:
            out[b * 256 : (b + 1) * 256, :] = value
        else:
            out[1280:1440, :] = value[:160]


def restore(field):
    spec = pl.BlockSpec(memory_space=pltpu.VMEM)
    return pl.pallas_call(
        restore_kernel,
        name="restore",
        out_shape=jax.ShapeDtypeStruct((LEV * ROWS, COLS), F32),
        in_specs=[spec],
        out_specs=spec,
        scratch_shapes=[pltpu.VMEM((ROWS, PAD, COLS), F32)],
        compiler_params=params(),
        cost_estimate=cost(10**9, 3 * 10**6),
    )(field).reshape(LEV, ROWS, COLS)


def forward(value, axis):
    size = lax.axis_size(axis)
    return lax.ppermute(value, axis, [(i, i + 1) for i in range(size - 1)])


def backward(value, axis):
    size = lax.axis_size(axis)
    return lax.ppermute(value, axis, [(i + 1, i) for i in range(size - 1)])


FIRST = 2


def body(ensemble, vertical_weights, dual_vector, observed_column, observed_level, active_count):
    place = jnp.stack(
        [lax.axis_index("gx"), lax.axis_index("gy"), lax.axis_size("gx") - 1, lax.axis_size("gy") - 1]
    ).astype(I32)
    outgoing, target, rank, weights = pack(
        active_count, dual_vector, observed_column, observed_level, vertical_weights
    )
    ensemble, outgoing = lax.optimization_barrier((ensemble, outgoing))
    incoming = lax.all_to_all(outgoing, ("gx", "gy"), split_axis=0, concat_axis=0, tiled=True)
    ens, ens_up, ens_down, strip, ens_l, ens_r = arrange(ensemble)
    incoming, ens_up, ens_down = lax.optimization_barrier((incoming, ens_up, ens_down))
    halo_t = forward(ens_down, "gx")
    halo_b = backward(ens_up, "gx")

    adj, wide, side_l, side_r, *slots = scatter(incoming, ens_l, ens_r)
    from_left = forward(side_r, "gy")
    from_right = backward(side_l, "gy")
    border0, inside = inner(ens, wide, weights, place, 0, FIRST)
    from_left, from_right, inside = lax.optimization_barrier((from_left, from_right, inside))
    strip, adj_strip, up, down = strips(strip, adj, from_left, from_right)
    top = forward(down, "gx")
    bottom = backward(up, "gx")
    border1, inside = inner(ens, wide, weights, place, FIRST, DUOS - FIRST, (inside,))

    outside = outer(ens, halo_t, halo_b, top, bottom, border0, border1, weights)
    field = edge(strip, adj_strip, top, bottom, weights, place, inside, outside)
    picked = gather(field, *slots)
    back = lax.all_to_all(picked, ("gx", "gy"), split_axis=0, concat_axis=0, tiled=True)
    increment = restore(field)
    obs_product = unpack(back, target, rank)
    return (increment, obs_product)


def solution(mesh):
    placed = (
        P(None, None, "gx", "gy"),
        P(),
        P(("gx", "gy")),
        P(("gx", "gy")),
        P(("gx", "gy")),
        P(("gx", "gy")),
    )
    return jax.shard_map(
        body,
        mesh=mesh,
        in_specs=placed,
        out_specs=(P(None, "gx", "gy"), P(("gx", "gy"))),
        check_vma=False,
    )
```

```python
import jax
import jax.numpy as jnp
from jax import lax
from jax.experimental import pallas as pl
from jax.experimental.pallas import tpu as pltpu
from jax.sharding import PartitionSpec as P

F32 = jnp.float32
BF16 = jnp.bfloat16
I32 = jnp.int32

MEM, LEV, ROWS, COLS = 10, 90, 16, 256
PAD = 96
DEV = 128
CAP = 48
SLOTS = 2048
HALF = 128
QUARTER = 64
DUO = 2 * COLS
DUOS = MEM // 2
EDGE = 3
STRIP = 18
PAIRS = STRIP // 2
SELF = 1.0 / 6.0
SCALE = 0.24**3 / (MEM - 1)
VMEM = 20 * 1024 * 1024
MOST = 58 * 1024 * 1024
ALL = 63 * 1024 * 1024


def split(value, count):
    parts = []
    for _ in range(count - 1):
        top = value.astype(BF16)
        parts.append(top)
        value = value - top.astype(F32)
    parts.append(value.astype(BF16))
    return parts


def dot(a, b):
    return lax.dot_general(a, b, (((1,), (0,)), ((), ())), preferred_element_type=F32)


def dot_nt(a, b):
    return lax.dot_general(a, b, (((1,), (1,)), ((), ())), preferred_element_type=F32)


def iota(shape, dim):
    return lax.broadcasted_iota(I32, shape, dim)


def one_hot(test):
    return jnp.where(test, 1.0, 0.0).astype(BF16)


def params(limit=VMEM):
    return pltpu.CompilerParams(vmem_limit_bytes=limit)


def cost(flops, moved):
    return pl.CostEstimate(flops=flops, bytes_accessed=moved, transcendentals=0)


def pack_kernel(
    count, dual_far, col_far, lev_far, vertical_far, out, tgt_out, rank_out, weights, left_v, left_c, right_v, right_c, dual, col, lev, vertical, sem
):
    pairs = ((col_far, col), (lev_far, lev), (dual_far, dual), (vertical_far, vertical))
    copies = [pltpu.make_async_copy(a, b, sem.at[i]) for i, (a, b) in enumerate(pairs)]
    for copy in copies:
        copy.start()
    for copy in copies:
        copy.wait()
    wide = jnp.concatenate([vertical[...], jnp.zeros((LEV, PAD - LEV), F32)], axis=1)
    high, low = split(jnp.concatenate([wide, jnp.zeros((PAD - LEV, PAD), F32)], axis=0), 2)
    both = jnp.concatenate([low, jnp.zeros_like(low)], axis=1)
    weights[...] = jnp.concatenate([jnp.concatenate([high, high], axis=1), both], axis=0)
    number = count[0]
    lane = iota((DEV, COLS), 1)
    upper = one_hot((lane > iota((DEV, COLS), 0)) | (lane >= HALF))
    rows = iota((DEV, HALF), 0)
    lane = iota((1, HALF), 1)
    carry = jnp.zeros((DEV, HALF), F32)
    for i in range(SLOTS // HALF):
        at = slice(i * HALF, (i + 1) * HALF)
        column = col[i : i + 1, :]
        row = column >> 12
        gcol = column & 4095
        y = gcol & 255
        y = ((y & 3) << 6) + (y >> 2)
        target = ((row >> 4) << 4) + (gcol >> 8)
        target = jnp.where(i * HALF + lane < number, target, -1)
        hit = rows == target
        both = dot(one_hot(hit), upper)
        rank = jnp.sum(jnp.where(hit, both[:, :HALF] + carry, 0.0), axis=0, keepdims=True)
        carry = carry + both[:, HALF:]
        tgt_out[i : i + 1, :] = target
        rank = rank.astype(I32)
        rank_out[i : i + 1, :] = rank
        right_v[:, at] = one_hot(rows == rank)
        right_c[:, at] = one_hot(rows == rank + CAP)
        values = dual[i : i + 1, :]
        for p, piece in enumerate(split(values, 3)):
            left_v[p * DEV : (p + 1) * DEV, at] = jnp.where(hit, piece.astype(F32), 0.0).astype(BF16)
        cells = (lev[i : i + 1, :] << 12, (row & 15) << 8, y + 1)
        for p, piece in enumerate(cells):
            left_c[p * DEV : (p + 1) * DEV, at] = jnp.where(hit, piece.astype(F32), 0.0).astype(BF16)
    a = dot_nt(left_v[...], right_v[...])
    b = dot_nt(left_c[...], right_c[...])
    out[...] = ((a[:DEV] + a[DEV : 2 * DEV]) + a[2 * DEV :]) + ((b[:DEV] + b[DEV : 2 * DEV]) + b[2 * DEV :])


def pack(count, dual, col, lev, vertical):
    spec = pl.BlockSpec(memory_space=pltpu.VMEM)
    return pl.pallas_call(
        pack_kernel,
        name="pack",
        out_shape=(
            jax.ShapeDtypeStruct((DEV, HALF), F32),
            jax.ShapeDtypeStruct((SLOTS // HALF, HALF), I32),
            jax.ShapeDtypeStruct((SLOTS // HALF, HALF), I32),
            jax.ShapeDtypeStruct((2 * PAD, 2 * PAD), BF16),
        ),
        in_specs=[pl.BlockSpec(memory_space=pltpu.SMEM)] + [pl.BlockSpec(memory_space=pltpu.HBM)] * 4,
        out_specs=(spec,) * 4,
        scratch_shapes=[pltpu.VMEM((3 * DEV, SLOTS), BF16)] * 2
        + [pltpu.VMEM((DEV, SLOTS), BF16)] * 2
        + [pltpu.VMEM((SLOTS // HALF, HALF), kind) for kind in (F32, I32, I32)]
        + [pltpu.VMEM((LEV, LEV), F32), pltpu.SemaphoreType.DMA((4,))],
        compiler_params=params(ALL),
        cost_estimate=cost(10**9, 10**6),
    )(count, dual.reshape(-1, HALF), col.reshape(-1, HALF), lev.reshape(-1, HALF), vertical)


def unpack_kernel(back, tgt, rank, out):
    rows = iota((DEV, HALF), 0)
    table = jnp.concatenate(split(back[...], 3), axis=0)
    for i in range(SLOTS // HALF):
        found = dot(table, one_hot(rows == rank[i : i + 1, :]))
        found = (found[:DEV] + found[DEV : 2 * DEV]) + found[2 * DEV :]
        out[i : i + 1, :] = jnp.sum(jnp.where(rows == tgt[i : i + 1, :], found, 0.0), axis=0, keepdims=True)


def unpack(back, tgt, rank):
    spec = pl.BlockSpec(memory_space=pltpu.VMEM)
    return pl.pallas_call(
        unpack_kernel,
        name="unpack",
        out_shape=jax.ShapeDtypeStruct((SLOTS // HALF, HALF), F32),
        in_specs=[spec] * 3,
        out_specs=spec,
        compiler_params=params(),
        cost_estimate=cost(10**8, 10**5),
    )(back, tgt, rank).reshape(SLOTS)


def strip_place(lane, members=MEM):
    j = lane % HALF
    return j // PAIRS, jnp.where(j < members * PAIRS, j % PAIRS * 2 + lane // HALF, -1)


def natural(place):
    return ((place & 63) << 2) + (place >> 6)


def duo_place(place):
    return ((place & 63) << 2) + (place >> 7), (place >> 6) & 1


def widen(value):
    low = iota((value.shape[0], HALF), 1) < QUARTER
    phases = []
    for half in (value[:, :HALF], value[:, HALF:]):
        turned = pltpu.roll(half, QUARTER, 1)
        phases += [jnp.where(low, half, turned), jnp.where(low, turned, half)]
    return jnp.concatenate(phases, axis=1)


def fold(value):
    low = iota((value.shape[0], HALF), 1) < QUARTER
    p = [value[:, i * HALF : (i + 1) * HALF] for i in range(4)]
    return jnp.concatenate(
        [jnp.where(low, p[i], p[i + 1]) + pltpu.roll(jnp.where(low, p[i + 1], p[i]), QUARTER, 1) for i in (0, 2)],
        axis=1,
    )


def arrange_kernel(
    ens, out, up, down, strip, side_l, side_r, taken, rows, turned_out, up_out, down_out, strip_acc, perm_y, perm_r, sides_out, sem, sem_out
):
    def fetch(k):
        return pltpu.make_async_copy(ens.at[k], taken.at[k], sem.at[k])

    def send(duo):
        slot = duo % 2
        return (
            pltpu.make_async_copy(turned_out.at[slot], out.at[duo], sem_out.at[0, slot]),
            pltpu.make_async_copy(up_out.at[slot], up.at[duo], sem_out.at[1, slot]),
            pltpu.make_async_copy(down_out.at[slot], down.at[duo], sem_out.at[2, slot]),
        )

    for k in range(MEM):
        fetch(k).start()
    rows[LEV * ROWS :, :] = jnp.zeros((rows.shape[0] - LEV * ROWS, DUO), BF16)
    strip_acc[...] = jnp.zeros_like(strip_acc)
    y, which = duo_place(iota((1, DUO), 1))
    perm_y[...] = one_hot(iota((DUO, DUO), 0) == which * COLS + y)
    i = iota((256, 1), 0)
    perm_r[...] = one_hot(iota((256, 256), 1) == (i & 15) * 16 + (i >> 4))

    @pl.loop(0, DUOS)
    def _(duo):
        @pl.when(duo >= 2)
        def _():
            for copy in send(duo - 2):
                copy.wait()

        fetch(2 * duo).wait()
        fetch(2 * duo + 1).wait()
        here, there, slot = 2 * duo, 2 * duo + 1, duo % 2
        y, which = duo_place(iota((DUO, COLS), 0))
        member, c = strip_place(iota((1, COLS), 1))
        want = jnp.where(y < 6, 3 + y, jnp.where(y >= 250, y - 241, -2))
        select = one_hot((member == 2 * duo + which) & (c == want))
        block = jnp.concatenate([taken[here], taken[there]], axis=1)
        rows[: LEV * ROWS, :] = dot(block, perm_y[...]).astype(BF16)
        for b in range(6):
            turned = dot(perm_r[...], rows[b * 256 : (b + 1) * 256, :])
            at = slice(b * 16, (b + 1) * 16)
            for x in range(ROWS):
                part = turned[x * 16 : (x + 1) * 16, :]
                turned_out[slot, x, at, :] = part.astype(BF16)
                if x < EDGE:
                    up_out[slot, x, at, :] = part
                if x >= ROWS - EDGE:
                    down_out[slot, x - (ROWS - EDGE), at, :] = part
        for copy in send(duo):
            copy.start()
        for x in range(ROWS):
            strip_acc[x] += dot(turned_out[slot, x], select)

    for duo in (DUOS - 2, DUOS - 1):
        for copy in send(duo):
            copy.wait()
    member, c = strip_place(iota((COLS, COLS), 0))
    left, right = (c >= 3) & (c < 6), (c >= 12) & (c < 15)
    spot = jnp.where(left, 3 * member + c - 3, jnp.where(right, HALF + 3 * member + c - 12, -1000))
    places = [one_hot(iota((COLS, COLS), 1) == spot + 30 * j) for j in range(4)]
    places = [one_hot(iota((COLS, COLS), 1) == spot + 30 * j) for j in range(4)]
    for group in range(4):
        sides = jnp.zeros((PAD, COLS), F32)
        for j in range(4):
            low = strip_acc[group * 4 + j].astype(BF16)
            strip[group * 4 + j] = low
            sides = sides + dot(low, places[j])
        sides_out[0, group] = sides[:, :HALF]
        sides_out[1, group] = sides[:, HALF:]
    copies = [
        pltpu.make_async_copy(sides_out.at[i], side.at[pl.ds(0, 4)], sem_out.at[0, i]) for i, side in enumerate((side_l, side_r))
    ]
    for copy in copies:
        copy.start()
    for copy in copies:
        copy.wait()


def arrange(ensemble):
    spec, far = pl.BlockSpec(memory_space=pltpu.VMEM), pl.BlockSpec(memory_space=pltpu.HBM)
    return pl.pallas_call(
        arrange_kernel,
        name="arrange",
        out_shape=(
            jax.ShapeDtypeStruct((DUOS, ROWS, PAD, DUO), BF16),
            jax.ShapeDtypeStruct((DUOS, EDGE, PAD, DUO), F32),
            jax.ShapeDtypeStruct((DUOS, EDGE, PAD, DUO), F32),
            jax.ShapeDtypeStruct((ROWS, PAD, COLS), BF16),
            jax.ShapeDtypeStruct((5, PAD, HALF), F32),
            jax.ShapeDtypeStruct((5, PAD, HALF), F32),
        ),
        in_specs=[far],
        out_specs=(far, far, far, spec, far, far),
        scratch_shapes=[
            pltpu.VMEM((MEM, LEV * ROWS, COLS), BF16),
            pltpu.VMEM((PAD * ROWS, DUO), BF16),
            pltpu.VMEM((2, ROWS, PAD, DUO), BF16),
            pltpu.VMEM((2, EDGE, PAD, DUO), F32),
            pltpu.VMEM((2, EDGE, PAD, DUO), F32),
            pltpu.VMEM((ROWS, PAD, COLS), F32),
            pltpu.VMEM((DUO, DUO), BF16),
            pltpu.VMEM((256, 256), BF16),
            pltpu.VMEM((2, 4, PAD, HALF), F32),
            pltpu.SemaphoreType.DMA((MEM,)),
            pltpu.SemaphoreType.DMA((3, 2)),
        ],
        compiler_params=params(MOST),
        cost_estimate=cost(10**10, 25 * 10**6),
    )(ensemble.reshape(MEM, LEV * ROWS, COLS))


CHUNKS = CAP // 2
TILES = CHUNKS + ROWS
SPACE = 48


def scatter_kernel(
    incoming, ens_l, ens_r, out, wide, side_l, side_r, level_out, column_out, pos_out, row_out,
    turned, hot, left, right, rows_of, sorted_, sides_out, sem
):
    turned[...] = incoming[...].T
    pairs = [[turned[pl.ds(first + i, CHUNKS, stride=2), :] for i in range(2)] for first in (0, CAP)]
    values = jnp.concatenate(pairs[0], axis=1)
    cells = jnp.concatenate(pairs[1], axis=1).astype(I32) - 1
    full = cells >= 0
    x = jnp.where(full, (cells >> 8) & 15, 99)

    for c in range(CHUNKS):
        hot[c * ROWS : (c + 1) * ROWS, :] = one_hot(iota((ROWS, COLS), 0) == x[c : c + 1, :])
    size = CHUNKS * ROWS
    lane = iota((COLS, COLS + HALF), 1)
    both = dot(hot[...], one_hot((lane > iota((COLS, COLS + HALF), 0)) | (lane >= COLS)))
    count = both[:, COLS:].astype(BF16)
    here, there = iota((size, size), 0), iota((size, size), 1)
    same = (here & 15) == (there & 15)
    earlier = dot(one_hot(same & (there < here)), count)
    needed = (dot(one_hot(same), count).astype(I32) + 255) >> 8
    start = dot(one_hot(((there & 15) < (here & 15)) & (there < ROWS)), needed.astype(F32).astype(BF16))
    base = start * 256.0 + earlier
    place = both[:, :COLS] + jnp.concatenate([base, base], axis=1)
    place = jnp.where(hot[...].astype(F32) > 0.5, place, 0.0)
    pos = jnp.sum(place.reshape(CHUNKS, ROWS, COLS), axis=1).astype(I32)
    pos = jnp.where(full, pos, -1)
    pos_out[...] = pos
    begun = jnp.where(start[:ROWS].astype(I32) <= iota((ROWS, HALF), 1), 1.0, 0.0)
    row_out[...] = jnp.sum(begun, axis=0, keepdims=True).astype(I32) - 1
    copy = pltpu.make_async_copy(row_out, rows_of, sem.at[0])
    copy.start()

    parts = [p.astype(F32) for p in split(values, 2)] + [(cells >> 12).astype(F32), (cells & 255).astype(F32)]
    tile, spot = pos >> 8, pos & 255
    for c in range(CHUNKS):
        at = slice(c * COLS, (c + 1) * COLS)
        hit = iota((SPACE, COLS), 0) == tile[c : c + 1, :]
        for p, part in enumerate(parts):
            left[p * SPACE : (p + 1) * SPACE, at] = jnp.where(hit, part[c : c + 1, :], 0.0).astype(BF16)
        right[:, at] = one_hot(iota((COLS, COLS), 0) == spot[c : c + 1, :])
    sorted_[...] = dot_nt(left[...], right[...])
    level_out[...] = sorted_[2 * SPACE : 3 * SPACE, :]
    column_out[...] = sorted_[3 * SPACE :, :]
    out[...] = jnp.zeros_like(out)
    copy.wait()

    @pl.loop(0, TILES // 8)
    def _(j):
        high, low, level, column = (sorted_[pl.ds(pl.multiple_of(p * SPACE + j * 8, 8), 8), :] for p in range(4))
        level, column = level.astype(I32), column.astype(I32)
        for half in range(2):
            results = []
            for q in range(half * 4, half * 4 + 4):
                at = slice(q, q + 1)
                hit = iota((PAD, COLS), 0) == level[at, :]
                lhs = jnp.concatenate([jnp.where(hit, high[at, :], 0.0), jnp.where(hit, low[at, :], 0.0)], axis=0)
                both = dot_nt(lhs.astype(BF16), one_hot(iota((COLS, COLS), 0) == column[at, :]))
                results.append(both[:PAD] + both[PAD:])
            for i, result in enumerate(results):
                out[rows_of[0, j * 8 + half * 4 + i]] += result

    y = natural(iota((COLS, COLS), 0))
    lane = iota((COLS, COLS), 1)
    place = jnp.where(y < 3, y, jnp.where(y >= 253, HALF + y - 253, -1000))
    packed = jnp.zeros((PAD, COLS), F32)
    for x in range(ROWS):
        value = out[x]
        wide[x] = widen(value)
        select = one_hot(lane == place + 3 * x)
        for piece in split(value, 2):
            packed = packed + dot(piece, select)
    sides_out[0] = packed[:, :HALF]
    sides_out[1] = packed[:, HALF:]
    copies = [pltpu.make_async_copy(sides_out.at[i], side.at[4], sem.at[i]) for i, side in enumerate((side_l, side_r))]
    for copy in copies:
        copy.start()
    for copy in copies:
        copy.wait()


def scatter(incoming, ens_l, ens_r):
    spec, far = pl.BlockSpec(memory_space=pltpu.VMEM), pl.BlockSpec(memory_space=pltpu.HBM)
    return pl.pallas_call(
        scatter_kernel,
        name="scatter",
        out_shape=(
            jax.ShapeDtypeStruct((ROWS, PAD, COLS), F32),
            jax.ShapeDtypeStruct((ROWS, PAD, DUO), F32),
            jax.ShapeDtypeStruct((5, PAD, HALF), F32),
            jax.ShapeDtypeStruct((5, PAD, HALF), F32),
            jax.ShapeDtypeStruct((SPACE, COLS), F32),
            jax.ShapeDtypeStruct((SPACE, COLS), F32),
            jax.ShapeDtypeStruct((CHUNKS, COLS), I32),
            jax.ShapeDtypeStruct((1, HALF), I32),
        ),
        in_specs=[spec, far, far],
        out_specs=(spec, spec, far, far, spec, spec, spec, spec),
        input_output_aliases={1: 2, 2: 3},
        scratch_shapes=[
            pltpu.VMEM((HALF, DEV), F32),
            pltpu.VMEM((CHUNKS * ROWS, COLS), BF16),
            pltpu.VMEM((4 * SPACE, CHUNKS * COLS), BF16),
            pltpu.VMEM((COLS, CHUNKS * COLS), BF16),
            pltpu.SMEM((1, HALF), I32),
            pltpu.VMEM((4 * SPACE, COLS), F32),
            pltpu.VMEM((2, PAD, HALF), F32),
            pltpu.SemaphoreType.DMA((2,)),
        ],
        compiler_params=params(),
        cost_estimate=cost(10**10, 2 * 10**6),
    )(incoming, ens_l, ens_r)


def strips_kernel(strip, adjoint, left, right, ens_out, out, up, down):
    lane = iota((COLS, COLS), 1)
    member, member_c = strip_place(lane, MEM + 1)
    y = natural(iota((COLS, COLS), 0))
    own = one_hot(member_c == jnp.where(y < 6, 3 + y, jnp.where(y >= 250, y - 241, -2)))
    from_lane = iota((HALF, COLS), 0)
    member_c, member = member_c[:HALF], member[:HALF]
    pieces = [split(side[4], 2) for side in (left, right)]
    ens_lanes = iota((PAD, COLS), 1) % HALF < MEM * PAIRS
    for x in range(ROWS):
        ens_value = strip[x].astype(F32)
        first = x % 4 * 30 + 3 * member
        for side, shift in ((left, 0), (right, 15)):
            inside = (member_c >= shift) & (member_c < shift + 3) & (member < MEM)
            spot = one_hot(inside & (from_lane == first + member_c - shift))
            ens_value = ens_value + dot(side[x // 4].astype(BF16), spot)
        ens_out[x] = ens_value.astype(BF16)
        value = jnp.zeros((PAD, COLS), F32)
        for piece in split(adjoint[x], 2):
            value = value + dot(piece, own)
        for side, shift in ((pieces[0], 0), (pieces[1], 15)):
            inside = (member_c >= shift) & (member_c < shift + 3)
            spot = one_hot(inside & (from_lane == 3 * x + member_c - shift))
            for piece in side:
                value = value + dot(piece, spot)
        out[x] = value
        for target, start in ((up, 0), (down, ROWS - EDGE)):
            if start <= x < start + EDGE:
                target[0, x - start] = adjoint[x]
                target[1, x - start] = jnp.where(ens_lanes, ens_value, value)


def strips(strip, adjoint, left, right):
    spec = pl.BlockSpec(memory_space=pltpu.VMEM)
    return pl.pallas_call(
        strips_kernel,
        name="strips",
        out_shape=(
            jax.ShapeDtypeStruct((ROWS, PAD, COLS), BF16),
            jax.ShapeDtypeStruct((ROWS, PAD, COLS), F32),
            jax.ShapeDtypeStruct((2, EDGE, PAD, COLS), F32),
            jax.ShapeDtypeStruct((2, EDGE, PAD, COLS), F32),
        ),
        in_specs=[spec] * 4,
        out_specs=(spec,) * 4,
        compiler_params=params(),
        cost_estimate=cost(10**9, 4 * 10**6),
    )(strip, adjoint, left, right)


def beside_permuted(value):
    even, odd = value[:, :HALF], value[:, HALF:]
    return jnp.concatenate([odd + pltpu.roll(odd, 1, 1), even + pltpu.roll(even, HALF - 1, 1)], axis=1)


def beside_duo(value):
    p = [value[:, i * HALF : (i + 1) * HALF] for i in range(4)]
    return jnp.concatenate(
        [pltpu.roll(p[3], 1, 1) + p[1], p[0] + p[2], p[1] + p[3], p[2] + pltpu.roll(p[0], HALF - 1, 1)], axis=1
    )


def total(terms):
    result = None
    for term in terms:
        if term is not None:
            result = term if result is None else result + term
    return result


def diffuse(get, given, wanted, beside, emit, mask=None):
    rows = [{} for _ in range(EDGE + 1)]
    for x in range(min(wanted) - EDGE, max(wanted) + EDGE + 1):
        if x in given:
            rows[0][x] = get(x)
        for step in range(1, EDGE + 1):
            at, reach, older = x - step, EDGE - step, rows[step - 1]
            if not min(wanted) - reach <= at <= max(wanted) + reach:
                continue
            terms = [older.get(at - 1), older.get(at + 1)]
            if at in older:
                terms += [beside(older[at]), older[at] * SELF]
            value = total(terms)
            if value is None:
                continue
            if step == EDGE:
                emit(at, value)
            else:
                rows[step][at] = value if mask is None else mask(at, value)


def put_split(ref, index, at, value):
    top = value.astype(BF16)
    ref[index, at, :] = top
    ref[index, pl.ds(at.start + PAD, 16), :] = (value - top.astype(F32)).astype(BF16)


def mix(weights, field):
    both = dot(weights, field)
    return both[:PAD] + both[PAD:]


INNER = ROWS - 2 * EDGE


def inner_kernel(start, count, ens, adj, weights, place, *refs):
    border, out, field, first, taken, sem = refs[-6:]

    def fetch(step):
        return pltpu.make_async_copy(ens.at[start + step], taken.at[step % 2], sem.at[step % 2])

    fetch(0).start()
    out[...] = refs[0][...] if start else jnp.zeros_like(out)
    top_open = jnp.where(place[0] == 0, 0.0, 1.0)
    bottom_open = jnp.where(place[0] == place[2], 0.0, 1.0)

    def mask(x, value):
        if x < 0:
            return value * top_open
        if x >= ROWS:
            return value * bottom_open
        return value

    @pl.loop(0, count)
    def _(step):
        @pl.when(step < count - 1)
        def _():
            fetch(step + 1).start()

        fetch(step).wait()
        slot = step % 2

        @pl.loop(0, PAD // 16)
        def _(group):
            at = pl.ds(pl.multiple_of(group * 16, 16), 16)

            for part in range(2):
                eight = pl.ds(pl.multiple_of(group * 16 + part * 8, 8), 8)

                def get(x):
                    return taken[slot, x, at, :].astype(F32)[part * 8 : part * 8 + 8, :] * adj[x, eight, :]

                def emit(x, value):
                    if not EDGE <= x < ROWS - EDGE:
                        border[step, x if x < EDGE else x - INNER, eight, :] = value
                    elif part == 0:
                        first[x - EDGE] = value
                    else:
                        put_split(field, x - EDGE, at, jnp.concatenate([first[x - EDGE], value], axis=0))

                diffuse(get, range(ROWS), range(ROWS), beside_duo, emit, mask)

        for x in range(INNER):
            out[x] += taken[slot, x + EDGE].astype(F32) * mix(weights[...], field[x])


def inner(ens, adj, weights, place, start, count, before=()):
    spec, far = pl.BlockSpec(memory_space=pltpu.VMEM), pl.BlockSpec(memory_space=pltpu.HBM)
    return pl.pallas_call(
        lambda *refs: inner_kernel(start, count, *refs),
        name="inner",
        out_shape=(
            jax.ShapeDtypeStruct((count, 2 * EDGE, PAD, DUO), F32),
            jax.ShapeDtypeStruct((INNER, PAD, DUO), F32),
        ),
        in_specs=[far, spec, spec, pl.BlockSpec(memory_space=pltpu.SMEM)] + [spec] * len(before),
        out_specs=(spec,) * 2,
        scratch_shapes=[
            pltpu.VMEM((INNER, 2 * PAD, DUO), BF16),
            pltpu.VMEM((INNER, 8, DUO), F32),
            pltpu.VMEM((2, ROWS, PAD, DUO), BF16),
            pltpu.SemaphoreType.DMA((2,)),
        ],
        compiler_params=params(),
        cost_estimate=cost(count * 2 * 10**9, count * 2 * 10**6),
    )(ens, adj, weights, place, *before)


def outer_kernel(
    ens, halo_t, halo_b, adj_t, adj_b, border0, border1, weights, out, field, first, wide, taken_e, taken_h, sem
):
    def fetch(duo):
        slot = duo % 2
        copies = (
            (ens.at[duo, pl.ds(0, EDGE)], taken_e.at[slot, pl.ds(0, EDGE)]),
            (ens.at[duo, pl.ds(ROWS - EDGE, EDGE)], taken_e.at[slot, pl.ds(EDGE, EDGE)]),
            (halo_t.at[duo], taken_h.at[slot, pl.ds(0, EDGE)]),
            (halo_b.at[duo], taken_h.at[slot, pl.ds(EDGE, EDGE)]),
        )
        return [pltpu.make_async_copy(a, b, sem.at[i, slot]) for i, (a, b) in enumerate(copies)]

    for copy in fetch(0):
        copy.start()
    out[...] = jnp.zeros_like(out)
    for x in range(EDGE):
        wide[x] = widen(adj_t[0, x])
        wide[EDGE + x] = widen(adj_b[0, x])

    for border, start in ((border0, 0), (border1, FIRST)):

        @pl.loop(0, border.shape[0])
        def _(step):
            duo = start + step
            slot = duo % 2

            @pl.when(duo < DUOS - 1)
            def _():
                for copy in fetch(duo + 1):
                    copy.start()

            for copy in fetch(duo):
                copy.wait()

            @pl.loop(0, PAD // 16, unroll=True)
            def _(group):
                at = pl.ds(pl.multiple_of(group * 16, 16), 16)

                for part in range(2):
                    eight = pl.ds(pl.multiple_of(group * 16 + part * 8, 8), 8)

                    def emit(x, value):
                        value = value + border[step, x, eight, :]
                        if part == 0:
                            first[x] = value
                        else:
                            put_split(field, x, at, jnp.concatenate([first[x], value], axis=0))

                    def get_t(x):
                        return taken_h[slot, x + EDGE, eight, :] * wide[x + EDGE, eight, :]

                    def get_b(x):
                        return taken_h[slot, x - EDGE, eight, :] * wide[x - EDGE, eight, :]

                    diffuse(get_t, range(-EDGE, 0), range(EDGE), beside_duo, emit)
                    diffuse(get_b, range(2 * EDGE, 3 * EDGE), range(EDGE, 2 * EDGE), beside_duo, emit)

            for x in range(2 * EDGE):
                out[x] += taken_e[slot, x].astype(F32) * mix(weights[...], field[x])


def outer(ens, halo_t, halo_b, adj_t, adj_b, border0, border1, weights):
    spec, far = pl.BlockSpec(memory_space=pltpu.VMEM), pl.BlockSpec(memory_space=pltpu.HBM)
    return pl.pallas_call(
        outer_kernel,
        name="outer",
        out_shape=jax.ShapeDtypeStruct((2 * EDGE, PAD, DUO), F32),
        in_specs=[far] * 3 + [spec] * 5,
        out_specs=spec,
        scratch_shapes=[
            pltpu.VMEM((2 * EDGE, 2 * PAD, DUO), BF16),
            pltpu.VMEM((2 * EDGE, 8, DUO), F32),
            pltpu.VMEM((2 * EDGE, PAD, DUO), F32),
            pltpu.VMEM((2, 2 * EDGE, PAD, DUO), BF16),
            pltpu.VMEM((2, 2 * EDGE, PAD, DUO), F32),
            pltpu.SemaphoreType.DMA((4, 2)),
        ],
        compiler_params=params(),
        cost_estimate=cost(MEM * 10**9, MEM * 3 * 10**6),
    )(ens, halo_t, halo_b, adj_t, adj_b, border0, border1, weights)


def edge_kernel(strip, adj, halo_t, halo_b, weights, place, inside, border, out, field, halo_adj):
    top_open = jnp.where(place[0] == 0, 0.0, 1.0)
    bottom_open = jnp.where(place[0] == place[2], 0.0, 1.0)
    left_open = jnp.where(place[1] == 0, 0.0, 1.0)
    right_open = jnp.where(place[1] == place[3], 0.0, 1.0)
    member, source = strip_place(iota((COLS, COLS), 0), MEM + 1)
    target = strip_place(iota((COLS, COLS), 1))[1]
    repeat = one_hot((member == MEM) & (source == target))
    for i, halo in enumerate((halo_t, halo_b)):
        for x in range(EDGE):
            high, low = split(halo[1, x], 2)
            halo_adj[i * EDGE + x] = dot(high, repeat) + dot(low, repeat)

    @pl.loop(0, PAD // 16)
    def _(group):
        at = pl.ds(pl.multiple_of(group * 16, 16), 16)
        c = strip_place(iota((16, COLS), 1))[1]
        lanes = jnp.where(c < 3, left_open, jnp.where(c >= 15, right_open, 1.0))

        def mask(x, value):
            value = value * lanes
            if x < 0:
                return value * top_open
            if x >= ROWS:
                return value * bottom_open
            return value

        def get(x):
            if x < 0:
                return halo_t[1, x + EDGE, at, :] * halo_adj[x + EDGE, at, :]
            if x >= ROWS:
                return halo_b[1, x - ROWS, at, :] * halo_adj[x - ROWS + EDGE, at, :]
            return strip[x, at, :].astype(F32) * adj[x, at, :]

        def emit(x, value):
            put_split(field, x, at, value)

        diffuse(get, range(-EDGE, ROWS + EDGE), range(ROWS), beside_permuted, emit, mask)

    c = strip_place(iota((COLS, COLS), 0))[1]
    spot = jnp.where((c >= 3) & (c < 6), c - 3, jnp.where((c >= 12) & (c < 15), 241 + c, -1))
    collect = one_hot(spot == natural(iota((COLS, COLS), 1)))
    y = natural(iota((PAD, COLS), 1))
    middle = (y >= EDGE) & (y < COLS - EDGE)
    for x in range(ROWS):
        if EDGE <= x < ROWS - EDGE:
            value = inside[x - EDGE]
        else:
            value = border[x if x < EDGE else x - INNER]
        value = jnp.where(middle, fold(value), 0.0)
        product = strip[x].astype(F32) * mix(weights[...], field[x])
        for piece in split(product, 2):
            value = value + dot(piece, collect)
        out[x] = value * SCALE


def edge(strip, adj, halo_t, halo_b, weights, place, inside, border):
    spec = pl.BlockSpec(memory_space=pltpu.VMEM)
    return pl.pallas_call(
        edge_kernel,
        name="edge",
        out_shape=jax.ShapeDtypeStruct((ROWS, PAD, COLS), F32),
        in_specs=[spec] * 5 + [pl.BlockSpec(memory_space=pltpu.SMEM)] + [spec] * 2,
        out_specs=spec,
        scratch_shapes=[pltpu.VMEM((ROWS, 2 * PAD, COLS), BF16), pltpu.VMEM((2 * EDGE, PAD, COLS), F32)],
        compiler_params=params(),
        cost_estimate=cost(4 * 10**9, 8 * 10**6),
    )(strip, adj, halo_t, halo_b, weights, place, inside, border)


def gather_kernel(field, level, column, pos, rows_of, out, table, picked):
    for x in range(ROWS):
        table[x, :PAD, :], table[x, PAD:, :] = split(field[x], 2)
    picked[...] = jnp.zeros_like(picked)

    @pl.loop(0, TILES // 8)
    def _(j):
        first = pl.multiple_of(j * 8, 8)
        levels, columns = level[pl.ds(first, 8), :].astype(I32), column[pl.ds(first, 8), :].astype(I32)
        lines = []
        for q in range(8):
            at = slice(q, q + 1)
            found = dot(table[rows_of[0, j * 8 + q]], one_hot(iota((COLS, COLS), 0) == columns[at, :]))
            found = jnp.where(iota((PAD, COLS), 0) == levels[at, :], found[:PAD] + found[PAD:], 0.0)
            lines.append(jnp.sum(found, axis=0, keepdims=True))
        picked[pl.ds(first, 8), :] = jnp.concatenate(lines, axis=0)

    both = jnp.concatenate(split(picked[...], 2), axis=0)
    tile, spot = pos[...] >> 8, pos[...] & 255
    lines = []
    for c in range(CHUNKS):
        found = dot(both, one_hot(iota((COLS, COLS), 0) == spot[c : c + 1, :]))
        found = jnp.where(iota((SPACE, COLS), 0) == tile[c : c + 1, :], found[:SPACE] + found[SPACE:], 0.0)
        found = jnp.sum(found, axis=0, keepdims=True)
        lines += [found[:, :HALF], found[:, HALF:]]
    out[...] = jnp.concatenate(lines + [jnp.zeros((HALF - CAP, DEV), F32)], axis=0).T


def gather(field, level, column, pos, rows_of):
    spec = pl.BlockSpec(memory_space=pltpu.VMEM)
    return pl.pallas_call(
        gather_kernel,
        name="gather",
        out_shape=jax.ShapeDtypeStruct((DEV, HALF), F32),
        in_specs=[spec] * 4 + [pl.BlockSpec(memory_space=pltpu.SMEM)],
        out_specs=spec,
        scratch_shapes=[
            pltpu.VMEM((ROWS, 2 * PAD, COLS), BF16),
            pltpu.VMEM((SPACE, COLS), F32),
        ],
        compiler_params=params(),
        cost_estimate=cost(10**10, 2 * 10**6),
    )(field, level, column, pos, rows_of)


def restore_kernel(field, out, rows):
    perm_y = one_hot(natural(iota((COLS, COLS), 0)) == iota((COLS, COLS), 1))
    i = iota((256, 1), 0)
    perm_r = one_hot(iota((256, 256), 1) == (i & 15) * 16 + (i >> 4))
    for x in range(ROWS):
        value = field[x]
        high, low = split(value, 2)
        rows[x] = dot(high, perm_y) + dot(low, perm_y)
    for b in range(6):
        block = jnp.concatenate([rows[x, b * 16 : (b + 1) * 16, :] for x in range(ROWS)], axis=0)
        high, low = split(block, 2)
        value = dot(perm_r, high) + dot(perm_r, low)
        if b < 5:
            out[b * 256 : (b + 1) * 256, :] = value
        else:
            out[1280:1440, :] = value[:160]


def restore(field):
    spec = pl.BlockSpec(memory_space=pltpu.VMEM)
    return pl.pallas_call(
        restore_kernel,
        name="restore",
        out_shape=jax.ShapeDtypeStruct((LEV * ROWS, COLS), F32),
        in_specs=[spec],
        out_specs=spec,
        scratch_shapes=[pltpu.VMEM((ROWS, PAD, COLS), F32)],
        compiler_params=params(),
        cost_estimate=cost(10**9, 3 * 10**6),
    )(field).reshape(LEV, ROWS, COLS)


def forward(value, axis):
    size = lax.axis_size(axis)
    return lax.ppermute(value, axis, [(i, i + 1) for i in range(size - 1)])


def backward(value, axis):
    size = lax.axis_size(axis)
    return lax.ppermute(value, axis, [(i + 1, i) for i in range(size - 1)])


FIRST = 2


def body(ensemble, vertical_weights, dual_vector, observed_column, observed_level, active_count):
    place = jnp.stack(
        [lax.axis_index("gx"), lax.axis_index("gy"), lax.axis_size("gx") - 1, lax.axis_size("gy") - 1]
    ).astype(I32)
    outgoing, target, rank, weights = pack(
        active_count, dual_vector, observed_column, observed_level, vertical_weights
    )
    ensemble, outgoing = lax.optimization_barrier((ensemble, outgoing))
    incoming = lax.all_to_all(outgoing, ("gx", "gy"), split_axis=0, concat_axis=0, tiled=True)
    ens, ens_up, ens_down, strip, ens_l, ens_r = arrange(ensemble)
    incoming, ens_up, ens_down = lax.optimization_barrier((incoming, ens_up, ens_down))
    halo_t = forward(ens_down, "gx")
    halo_b = backward(ens_up, "gx")

    adj, wide, side_l, side_r, *slots = scatter(incoming, ens_l, ens_r)
    from_left = forward(side_r, "gy")
    from_right = backward(side_l, "gy")
    border0, inside = inner(ens, wide, weights, place, 0, FIRST)
    from_left, from_right, inside = lax.optimization_barrier((from_left, from_right, inside))
    strip, adj_strip, up, down = strips(strip, adj, from_left, from_right)
    top = forward(down, "gx")
    bottom = backward(up, "gx")
    border1, inside = inner(ens, wide, weights, place, FIRST, DUOS - FIRST, (inside,))

    outside = outer(ens, halo_t, halo_b, top, bottom, border0, border1, weights)
    field = edge(strip, adj_strip, top, bottom, weights, place, inside, outside)
    picked = gather(field, *slots)
    back = lax.all_to_all(picked, ("gx", "gy"), split_axis=0, concat_axis=0, tiled=True)
    increment = restore(field)
    obs_product = unpack(back, target, rank)
    return (increment, obs_product)


def solution(mesh):
    placed = (
        P(None, None, "gx", "gy"),
        P(),
        P(("gx", "gy")),
        P(("gx", "gy")),
        P(("gx", "gy")),
        P(("gx", "gy")),
    )
    return jax.shard_map(
        body,
        mesh=mesh,
        in_specs=placed,
        out_specs=(P(None, "gx", "gy"), P(("gx", "gy"))),
        check_vma=False,
    )
```

```python
import jax
import jax.numpy as jnp
from jax import lax
from jax.experimental import pallas as pl
from jax.experimental.pallas import tpu as pltpu
from jax.sharding import PartitionSpec as P

F32 = jnp.float32
BF16 = jnp.bfloat16
I32 = jnp.int32

MEM, LEV, ROWS, COLS = 10, 90, 16, 256
PAD = 96
DEV = 128
CAP = 48
SLOTS = 2048
HALF = 128
QUARTER = 64
DUO = 2 * COLS
DUOS = MEM // 2
EDGE = 3
STRIP = 18
PAIRS = STRIP // 2
SELF = 1.0 / 6.0
SCALE = 0.24**3 / (MEM - 1)
VMEM = 20 * 1024 * 1024
MOST = 58 * 1024 * 1024
ALL = 63 * 1024 * 1024


def split(value, count):
    parts = []
    for _ in range(count - 1):
        top = value.astype(BF16)
        parts.append(top)
        value = value - top.astype(F32)
    parts.append(value.astype(BF16))
    return parts


def dot(a, b):
    return lax.dot_general(a, b, (((1,), (0,)), ((), ())), preferred_element_type=F32)


def dot_nt(a, b):
    return lax.dot_general(a, b, (((1,), (1,)), ((), ())), preferred_element_type=F32)


def iota(shape, dim):
    return lax.broadcasted_iota(I32, shape, dim)


def one_hot(test):
    return jnp.where(test, 1.0, 0.0).astype(BF16)


def params(limit=VMEM):
    return pltpu.CompilerParams(vmem_limit_bytes=limit)


def cost(flops, moved):
    return pl.CostEstimate(flops=flops, bytes_accessed=moved, transcendentals=0)


def pack_kernel(
    count, dual_far, col_far, lev_far, vertical_far, out, tgt_out, rank_out, weights, left_v, left_c, right_v, right_c, dual, col, lev, vertical, sem
):
    pairs = ((col_far, col), (lev_far, lev), (dual_far, dual), (vertical_far, vertical))
    copies = [pltpu.make_async_copy(a, b, sem.at[i]) for i, (a, b) in enumerate(pairs)]
    for copy in copies:
        copy.start()
    for copy in copies:
        copy.wait()
    wide = jnp.concatenate([vertical[...], jnp.zeros((LEV, PAD - LEV), F32)], axis=1)
    high, low = split(jnp.concatenate([wide, jnp.zeros((PAD - LEV, PAD), F32)], axis=0), 2)
    both = jnp.concatenate([low, jnp.zeros_like(low)], axis=1)
    weights[...] = jnp.concatenate([jnp.concatenate([high, high], axis=1), both], axis=0)
    number = count[0]
    lane = iota((DEV, COLS), 1)
    upper = one_hot((lane > iota((DEV, COLS), 0)) | (lane >= HALF))
    rows = iota((DEV, HALF), 0)
    lane = iota((1, HALF), 1)
    carry = jnp.zeros((DEV, HALF), F32)
    for i in range(SLOTS // HALF):
        at = slice(i * HALF, (i + 1) * HALF)
        column = col[i : i + 1, :]
        row = column >> 12
        gcol = column & 4095
        y = gcol & 255
        y = ((y & 3) << 6) + (y >> 2)
        target = ((row >> 4) << 4) + (gcol >> 8)
        target = jnp.where(i * HALF + lane < number, target, -1)
        hit = rows == target
        both = dot(one_hot(hit), upper)
        rank = jnp.sum(jnp.where(hit, both[:, :HALF] + carry, 0.0), axis=0, keepdims=True)
        carry = carry + both[:, HALF:]
        tgt_out[i : i + 1, :] = target
        rank = rank.astype(I32)
        rank_out[i : i + 1, :] = rank
        right_v[:, at] = one_hot(rows == rank)
        right_c[:, at] = one_hot(rows == rank + CAP)
        values = dual[i : i + 1, :]
        for p, piece in enumerate(split(values, 3)):
            left_v[p * DEV : (p + 1) * DEV, at] = jnp.where(hit, piece.astype(F32), 0.0).astype(BF16)
        cells = (lev[i : i + 1, :] << 12, (row & 15) << 8, y + 1)
        for p, piece in enumerate(cells):
            left_c[p * DEV : (p + 1) * DEV, at] = jnp.where(hit, piece.astype(F32), 0.0).astype(BF16)
    a = dot_nt(left_v[...], right_v[...])
    b = dot_nt(left_c[...], right_c[...])
    out[...] = ((a[:DEV] + a[DEV : 2 * DEV]) + a[2 * DEV :]) + ((b[:DEV] + b[DEV : 2 * DEV]) + b[2 * DEV :])


def pack(count, dual, col, lev, vertical):
    spec = pl.BlockSpec(memory_space=pltpu.VMEM)
    return pl.pallas_call(
        pack_kernel,
        name="pack",
        out_shape=(
            jax.ShapeDtypeStruct((DEV, HALF), F32),
            jax.ShapeDtypeStruct((SLOTS // HALF, HALF), I32),
            jax.ShapeDtypeStruct((SLOTS // HALF, HALF), I32),
            jax.ShapeDtypeStruct((2 * PAD, 2 * PAD), BF16),
        ),
        in_specs=[pl.BlockSpec(memory_space=pltpu.SMEM)] + [pl.BlockSpec(memory_space=pltpu.HBM)] * 4,
        out_specs=(spec,) * 4,
        scratch_shapes=[pltpu.VMEM((3 * DEV, SLOTS), BF16)] * 2
        + [pltpu.VMEM((DEV, SLOTS), BF16)] * 2
        + [pltpu.VMEM((SLOTS // HALF, HALF), kind) for kind in (F32, I32, I32)]
        + [pltpu.VMEM((LEV, LEV), F32), pltpu.SemaphoreType.DMA((4,))],
        compiler_params=params(ALL),
        cost_estimate=cost(10**9, 10**6),
    )(count, dual.reshape(-1, HALF), col.reshape(-1, HALF), lev.reshape(-1, HALF), vertical)


def unpack_kernel(back, tgt, rank, out):
    rows = iota((DEV, HALF), 0)
    table = jnp.concatenate(split(back[...], 3), axis=0)
    for i in range(SLOTS // HALF):
        found = dot(table, one_hot(rows == rank[i : i + 1, :]))
        found = (found[:DEV] + found[DEV : 2 * DEV]) + found[2 * DEV :]
        out[i : i + 1, :] = jnp.sum(jnp.where(rows == tgt[i : i + 1, :], found, 0.0), axis=0, keepdims=True)


def unpack(back, tgt, rank):
    spec = pl.BlockSpec(memory_space=pltpu.VMEM)
    return pl.pallas_call(
        unpack_kernel,
        name="unpack",
        out_shape=jax.ShapeDtypeStruct((SLOTS // HALF, HALF), F32),
        in_specs=[spec] * 3,
        out_specs=spec,
        compiler_params=params(),
        cost_estimate=cost(10**8, 10**5),
    )(back, tgt, rank).reshape(SLOTS)


def strip_place(lane, members=MEM):
    j = lane % HALF
    return j // PAIRS, jnp.where(j < members * PAIRS, j % PAIRS * 2 + lane // HALF, -1)


def natural(place):
    return ((place & 63) << 2) + (place >> 6)


def duo_place(place):
    return ((place & 63) << 2) + (place >> 7), (place >> 6) & 1


def widen(value):
    low = iota((value.shape[0], HALF), 1) < QUARTER
    phases = []
    for half in (value[:, :HALF], value[:, HALF:]):
        turned = pltpu.roll(half, QUARTER, 1)
        phases += [jnp.where(low, half, turned), jnp.where(low, turned, half)]
    return jnp.concatenate(phases, axis=1)


def fold(value):
    low = iota((value.shape[0], HALF), 1) < QUARTER
    p = [value[:, i * HALF : (i + 1) * HALF] for i in range(4)]
    return jnp.concatenate(
        [jnp.where(low, p[i], p[i + 1]) + pltpu.roll(jnp.where(low, p[i + 1], p[i]), QUARTER, 1) for i in (0, 2)],
        axis=1,
    )


def arrange_kernel(
    ens, out, up, down, strip, side_l, side_r, taken, rows, turned_out, up_out, down_out, strip_acc, perm_y, perm_r, sides_out, sem, sem_out
):
    def fetch(k):
        return pltpu.make_async_copy(ens.at[k], taken.at[k], sem.at[k])

    def send(duo):
        slot = duo % 2
        return (
            pltpu.make_async_copy(turned_out.at[slot], out.at[duo], sem_out.at[0, slot]),
            pltpu.make_async_copy(up_out.at[slot], up.at[duo], sem_out.at[1, slot]),
            pltpu.make_async_copy(down_out.at[slot], down.at[duo], sem_out.at[2, slot]),
        )

    for k in range(MEM):
        fetch(k).start()
    rows[LEV * ROWS :, :] = jnp.zeros((rows.shape[0] - LEV * ROWS, DUO), BF16)
    strip_acc[...] = jnp.zeros_like(strip_acc)
    y, which = duo_place(iota((1, DUO), 1))
    perm_y[...] = one_hot(iota((DUO, DUO), 0) == which * COLS + y)
    i = iota((256, 1), 0)
    perm_r[...] = one_hot(iota((256, 256), 1) == (i & 15) * 16 + (i >> 4))

    @pl.loop(0, DUOS)
    def _(duo):
        @pl.when(duo >= 2)
        def _():
            for copy in send(duo - 2):
                copy.wait()

        fetch(2 * duo).wait()
        fetch(2 * duo + 1).wait()
        here, there, slot = 2 * duo, 2 * duo + 1, duo % 2
        lane = iota((COLS, COLS), 0)
        y, which = jnp.where(lane % HALF < QUARTER, lane % HALF, lane % HALF + HALF), lane // HALF
        member, c = strip_place(iota((1, COLS), 1))
        want = jnp.where(y < 6, 3 + y, jnp.where(y >= 250, y - 241, -2))
        select = one_hot((member == 2 * duo + which) & (c == want))
        outside = iota((LEV * ROWS, HALF), 1) < QUARTER
        ends = [jnp.where(outside, taken[k, :, :HALF], taken[k, :, HALF:]) for k in (here, there)]
        block = jnp.concatenate([taken[here], taken[there]], axis=1)
        rows[: LEV * ROWS, :] = dot(block, perm_y[...]).astype(BF16)
        for b in range(6):
            turned = dot(perm_r[...], rows[b * 256 : (b + 1) * 256, :])
            at = slice(b * 16, (b + 1) * 16)
            for x in range(ROWS):
                part = turned[x * 16 : (x + 1) * 16, :]
                turned_out[slot, x, at, :] = part.astype(BF16)
                if x < EDGE:
                    up_out[slot, x, at, :] = part
                if x >= ROWS - EDGE:
                    down_out[slot, x - (ROWS - EDGE), at, :] = part
        for copy in send(duo):
            copy.start()
        strip_acc[: LEV * ROWS, :] += dot(jnp.concatenate(ends, axis=1), select)

    member, c = strip_place(iota((COLS, COLS), 0))
    for b in range(6):
        turned = dot(perm_r[...], strip_acc[b * 256 : (b + 1) * 256, :].astype(BF16)).astype(BF16)
        for x in range(ROWS):
            strip[x, b * 16 : (b + 1) * 16, :] = turned[x * 16 : (x + 1) * 16, :]
    left, right = (c >= 3) & (c < 6), (c >= 12) & (c < 15)
    spot = jnp.where(left, 3 * member + c - 3, jnp.where(right, HALF + 3 * member + c - 12, -1000))
    places = [one_hot(iota((COLS, COLS), 1) == spot + 30 * j) for j in range(4)]
    for group in range(4):
        sides = jnp.zeros((PAD, COLS), F32)
        for j in range(4):
            sides = sides + dot(strip[group * 4 + j], places[j])
        sides_out[0, group] = sides[:, :HALF]
        sides_out[1, group] = sides[:, HALF:]
    copies = [
        pltpu.make_async_copy(sides_out.at[i], side.at[pl.ds(0, 4)], sem_out.at[3, i]) for i, side in enumerate((side_l, side_r))
    ]
    for copy in copies:
        copy.start()
    for duo in (DUOS - 2, DUOS - 1):
        for copy in send(duo):
            copy.wait()
    for copy in copies:
        copy.wait()


def arrange(ensemble):
    spec, far = pl.BlockSpec(memory_space=pltpu.VMEM), pl.BlockSpec(memory_space=pltpu.HBM)
    return pl.pallas_call(
        arrange_kernel,
        name="arrange",
        out_shape=(
            jax.ShapeDtypeStruct((DUOS, ROWS, PAD, DUO), BF16),
            jax.ShapeDtypeStruct((DUOS, EDGE, PAD, DUO), F32),
            jax.ShapeDtypeStruct((DUOS, EDGE, PAD, DUO), F32),
            jax.ShapeDtypeStruct((ROWS, PAD, COLS), BF16),
            jax.ShapeDtypeStruct((5, PAD, HALF), F32),
            jax.ShapeDtypeStruct((5, PAD, HALF), F32),
        ),
        in_specs=[far],
        out_specs=(far, far, far, spec, far, far),
        scratch_shapes=[
            pltpu.VMEM((MEM, LEV * ROWS, COLS), BF16),
            pltpu.VMEM((PAD * ROWS, DUO), BF16),
            pltpu.VMEM((2, ROWS, PAD, DUO), BF16),
            pltpu.VMEM((2, EDGE, PAD, DUO), F32),
            pltpu.VMEM((2, EDGE, PAD, DUO), F32),
            pltpu.VMEM((ROWS * PAD, COLS), F32),
            pltpu.VMEM((DUO, DUO), BF16),
            pltpu.VMEM((256, 256), BF16),
            pltpu.VMEM((2, 4, PAD, HALF), F32),
            pltpu.SemaphoreType.DMA((MEM,)),
            pltpu.SemaphoreType.DMA((4, 2)),
        ],
        compiler_params=params(MOST),
        cost_estimate=cost(10**10, 25 * 10**6),
    )(ensemble.reshape(MEM, LEV * ROWS, COLS))


CHUNKS = CAP // 2
TILES = CHUNKS + ROWS
SPACE = 48


def scatter_kernel(
    incoming, ens_l, ens_r, out, wide, side_l, side_r, level_out, column_out, pos_out, row_out,
    turned, hot, left, right, rows_of, sorted_, sides_out, sem
):
    turned[...] = incoming[...].T
    pairs = [[turned[pl.ds(first + i, CHUNKS, stride=2), :] for i in range(2)] for first in (0, CAP)]
    values = jnp.concatenate(pairs[0], axis=1)
    cells = jnp.concatenate(pairs[1], axis=1).astype(I32) - 1
    full = cells >= 0
    x = jnp.where(full, (cells >> 8) & 15, 99)

    for c in range(CHUNKS):
        hot[c * ROWS : (c + 1) * ROWS, :] = one_hot(iota((ROWS, COLS), 0) == x[c : c + 1, :])
    size = CHUNKS * ROWS
    lane = iota((COLS, COLS + HALF), 1)
    both = dot(hot[...], one_hot((lane > iota((COLS, COLS + HALF), 0)) | (lane >= COLS)))
    count = both[:, COLS:].astype(BF16)
    here, there = iota((size, size), 0), iota((size, size), 1)
    same = (here & 15) == (there & 15)
    earlier = dot(one_hot(same & (there < here)), count)
    needed = (dot(one_hot(same), count).astype(I32) + 255) >> 8
    start = dot(one_hot(((there & 15) < (here & 15)) & (there < ROWS)), needed.astype(F32).astype(BF16))
    base = start * 256.0 + earlier
    place = both[:, :COLS] + jnp.concatenate([base, base], axis=1)
    place = jnp.where(hot[...].astype(F32) > 0.5, place, 0.0)
    pos = jnp.sum(place.reshape(CHUNKS, ROWS, COLS), axis=1).astype(I32)
    pos = jnp.where(full, pos, -1)
    pos_out[...] = pos
    begun = jnp.where(start[:ROWS].astype(I32) <= iota((ROWS, HALF), 1), 1.0, 0.0)
    row_out[...] = jnp.sum(begun, axis=0, keepdims=True).astype(I32) - 1
    copy = pltpu.make_async_copy(row_out, rows_of, sem.at[0])
    copy.start()

    parts = [p.astype(F32) for p in split(values, 2)] + [(cells >> 12).astype(F32), (cells & 255).astype(F32)]
    tile, spot = pos >> 8, pos & 255
    for c in range(CHUNKS):
        at = slice(c * COLS, (c + 1) * COLS)
        hit = iota((SPACE, COLS), 0) == tile[c : c + 1, :]
        for p, part in enumerate(parts):
            left[p * SPACE : (p + 1) * SPACE, at] = jnp.where(hit, part[c : c + 1, :], 0.0).astype(BF16)
        right[:, at] = one_hot(iota((COLS, COLS), 0) == spot[c : c + 1, :])
    sorted_[...] = dot_nt(left[...], right[...])
    level_out[...] = sorted_[2 * SPACE : 3 * SPACE, :]
    column_out[...] = sorted_[3 * SPACE :, :]
    out[...] = jnp.zeros_like(out)
    copy.wait()

    @pl.loop(0, TILES // 8)
    def _(j):
        high, low, level, column = (sorted_[pl.ds(pl.multiple_of(p * SPACE + j * 8, 8), 8), :] for p in range(4))
        level, column = level.astype(I32), column.astype(I32)
        for half in range(2):
            results = []
            for q in range(half * 4, half * 4 + 4):
                at = slice(q, q + 1)
                hit = iota((PAD, COLS), 0) == level[at, :]
                lhs = jnp.concatenate([jnp.where(hit, high[at, :], 0.0), jnp.where(hit, low[at, :], 0.0)], axis=0)
                both = dot_nt(lhs.astype(BF16), one_hot(iota((COLS, COLS), 0) == column[at, :]))
                results.append(both[:PAD] + both[PAD:])
            for i, result in enumerate(results):
                out[rows_of[0, j * 8 + half * 4 + i]] += result

    y = natural(iota((COLS, COLS), 0))
    lane = iota((COLS, COLS), 1)
    place = jnp.where(y < 3, y, jnp.where(y >= 253, HALF + y - 253, -1000))
    packed = jnp.zeros((PAD, COLS), F32)
    for x in range(ROWS):
        select = one_hot(lane == place + 3 * x)
        for piece in split(out[x], 2):
            packed = packed + dot(piece, select)
    sides_out[0] = packed[:, :HALF]
    sides_out[1] = packed[:, HALF:]
    copies = [pltpu.make_async_copy(sides_out.at[i], side.at[4], sem.at[i]) for i, side in enumerate((side_l, side_r))]
    for copy in copies:
        copy.start()
    for x in range(ROWS):
        wide[x] = widen(out[x])
    for copy in copies:
        copy.wait()


def scatter(incoming, ens_l, ens_r):
    spec, far = pl.BlockSpec(memory_space=pltpu.VMEM), pl.BlockSpec(memory_space=pltpu.HBM)
    return pl.pallas_call(
        scatter_kernel,
        name="scatter",
        out_shape=(
            jax.ShapeDtypeStruct((ROWS, PAD, COLS), F32),
            jax.ShapeDtypeStruct((ROWS, PAD, DUO), F32),
            jax.ShapeDtypeStruct((5, PAD, HALF), F32),
            jax.ShapeDtypeStruct((5, PAD, HALF), F32),
            jax.ShapeDtypeStruct((SPACE, COLS), F32),
            jax.ShapeDtypeStruct((SPACE, COLS), F32),
            jax.ShapeDtypeStruct((CHUNKS, COLS), I32),
            jax.ShapeDtypeStruct((1, HALF), I32),
        ),
        in_specs=[spec, far, far],
        out_specs=(spec, spec, far, far, spec, spec, spec, spec),
        input_output_aliases={1: 2, 2: 3},
        scratch_shapes=[
            pltpu.VMEM((HALF, DEV), F32),
            pltpu.VMEM((CHUNKS * ROWS, COLS), BF16),
            pltpu.VMEM((4 * SPACE, CHUNKS * COLS), BF16),
            pltpu.VMEM((COLS, CHUNKS * COLS), BF16),
            pltpu.SMEM((1, HALF), I32),
            pltpu.VMEM((4 * SPACE, COLS), F32),
            pltpu.VMEM((2, PAD, HALF), F32),
            pltpu.SemaphoreType.DMA((2,)),
        ],
        compiler_params=params(),
        cost_estimate=cost(10**10, 2 * 10**6),
    )(incoming, ens_l, ens_r)


def strips_kernel(strip, adjoint, left, right, ens_out, out, up, down):
    lane = iota((COLS, COLS), 1)
    member, member_c = strip_place(lane, MEM + 1)
    y = natural(iota((COLS, COLS), 0))
    own = one_hot(member_c == jnp.where(y < 6, 3 + y, jnp.where(y >= 250, y - 241, -2)))
    from_lane = iota((HALF, COLS), 0)
    member_c, member = member_c[:HALF], member[:HALF]
    pieces = [split(side[4], 2) for side in (left, right)]
    ens_lanes = iota((PAD, COLS), 1) % HALF < MEM * PAIRS
    for x in range(ROWS):
        ens_value = strip[x].astype(F32)
        first = x % 4 * 30 + 3 * member
        for side, shift in ((left, 0), (right, 15)):
            inside = (member_c >= shift) & (member_c < shift + 3) & (member < MEM)
            spot = one_hot(inside & (from_lane == first + member_c - shift))
            ens_value = ens_value + dot(side[x // 4].astype(BF16), spot)
        ens_out[x] = ens_value.astype(BF16)
        value = jnp.zeros((PAD, COLS), F32)
        for piece in split(adjoint[x], 2):
            value = value + dot(piece, own)
        for side, shift in ((pieces[0], 0), (pieces[1], 15)):
            inside = (member_c >= shift) & (member_c < shift + 3)
            spot = one_hot(inside & (from_lane == 3 * x + member_c - shift))
            for piece in side:
                value = value + dot(piece, spot)
        out[x] = value
        for target, start in ((up, 0), (down, ROWS - EDGE)):
            if start <= x < start + EDGE:
                target[0, x - start] = adjoint[x]
                target[1, x - start] = jnp.where(ens_lanes, ens_value, value)


def strips(strip, adjoint, left, right):
    spec = pl.BlockSpec(memory_space=pltpu.VMEM)
    return pl.pallas_call(
        strips_kernel,
        name="strips",
        out_shape=(
            jax.ShapeDtypeStruct((ROWS, PAD, COLS), BF16),
            jax.ShapeDtypeStruct((ROWS, PAD, COLS), F32),
            jax.ShapeDtypeStruct((2, EDGE, PAD, COLS), F32),
            jax.ShapeDtypeStruct((2, EDGE, PAD, COLS), F32),
        ),
        in_specs=[spec] * 4,
        out_specs=(spec,) * 4,
        compiler_params=params(),
        cost_estimate=cost(10**9, 4 * 10**6),
    )(strip, adjoint, left, right)


def beside_permuted(value):
    even, odd = value[:, :HALF], value[:, HALF:]
    return jnp.concatenate([odd + pltpu.roll(odd, 1, 1), even + pltpu.roll(even, HALF - 1, 1)], axis=1)


def beside_duo(value):
    p = [value[:, i * HALF : (i + 1) * HALF] for i in range(4)]
    return jnp.concatenate(
        [pltpu.roll(p[3], 1, 1) + p[1], p[0] + p[2], p[1] + p[3], p[2] + pltpu.roll(p[0], HALF - 1, 1)], axis=1
    )


def total(terms):
    result = None
    for term in terms:
        if term is not None:
            result = term if result is None else result + term
    return result


def diffuse(get, given, wanted, beside, emit, mask=None):
    rows = [{} for _ in range(EDGE + 1)]
    for x in range(min(wanted) - EDGE, max(wanted) + EDGE + 1):
        if x in given:
            rows[0][x] = get(x)
        for step in range(1, EDGE + 1):
            at, reach, older = x - step, EDGE - step, rows[step - 1]
            if not min(wanted) - reach <= at <= max(wanted) + reach:
                continue
            terms = [older.get(at - 1), older.get(at + 1)]
            if at in older:
                terms += [beside(older[at]), older[at] * SELF]
            value = total(terms)
            if value is None:
                continue
            if step == EDGE:
                emit(at, value)
            else:
                rows[step][at] = value if mask is None else mask(at, value)


def put_split(ref, index, at, value):
    top = value.astype(BF16)
    ref[index, at, :] = top
    ref[index, pl.ds(at.start + PAD, 16), :] = (value - top.astype(F32)).astype(BF16)


def mix(weights, field):
    both = dot(weights, field)
    return both[:PAD] + both[PAD:]


INNER = ROWS - 2 * EDGE


def inner_kernel(start, count, ens, adj, weights, place, *refs):
    border, out, field, first, taken, sem = refs[-6:]

    def fetch(step):
        return pltpu.make_async_copy(ens.at[start + step], taken.at[step % 2], sem.at[step % 2])

    fetch(0).start()
    out[...] = refs[0][...] if start else jnp.zeros_like(out)
    top_open = jnp.where(place[0] == 0, 0.0, 1.0)
    bottom_open = jnp.where(place[0] == place[2], 0.0, 1.0)

    def mask(x, value):
        if x < 0:
            return value * top_open
        if x >= ROWS:
            return value * bottom_open
        return value

    @pl.loop(0, count)
    def _(step):
        @pl.when(step < count - 1)
        def _():
            fetch(step + 1).start()

        fetch(step).wait()
        slot = step % 2

        @pl.loop(0, PAD // 16)
        def _(group):
            at = pl.ds(pl.multiple_of(group * 16, 16), 16)

            for part in range(2):
                eight = pl.ds(pl.multiple_of(group * 16 + part * 8, 8), 8)

                def get(x):
                    return taken[slot, x, at, :].astype(F32)[part * 8 : part * 8 + 8, :] * adj[x, eight, :]

                def emit(x, value):
                    if not EDGE <= x < ROWS - EDGE:
                        border[step, x if x < EDGE else x - INNER, eight, :] = value
                    elif part == 0:
                        first[x - EDGE] = value
                    else:
                        put_split(field, x - EDGE, at, jnp.concatenate([first[x - EDGE], value], axis=0))

                diffuse(get, range(ROWS), range(ROWS), beside_duo, emit, mask)

        for x in range(INNER):
            out[x] += taken[slot, x + EDGE].astype(F32) * mix(weights[...], field[x])


def inner(ens, adj, weights, place, start, count, before=()):
    spec, far = pl.BlockSpec(memory_space=pltpu.VMEM), pl.BlockSpec(memory_space=pltpu.HBM)
    return pl.pallas_call(
        lambda *refs: inner_kernel(start, count, *refs),
        name="inner",
        out_shape=(
            jax.ShapeDtypeStruct((count, 2 * EDGE, PAD, DUO), F32),
            jax.ShapeDtypeStruct((INNER, PAD, DUO), F32),
        ),
        in_specs=[far, spec, spec, pl.BlockSpec(memory_space=pltpu.SMEM)] + [spec] * len(before),
        out_specs=(spec,) * 2,
        scratch_shapes=[
            pltpu.VMEM((INNER, 2 * PAD, DUO), BF16),
            pltpu.VMEM((INNER, 8, DUO), F32),
            pltpu.VMEM((2, ROWS, PAD, DUO), BF16),
            pltpu.SemaphoreType.DMA((2,)),
        ],
        compiler_params=params(),
        cost_estimate=cost(count * 2 * 10**9, count * 2 * 10**6),
    )(ens, adj, weights, place, *before)


def outer_kernel(
    ens, halo_t, halo_b, adj_t, adj_b, border0, border1, weights, out, field, first, wide, taken_e, taken_h, sem
):
    def fetch(duo):
        slot = duo % 2
        copies = (
            (ens.at[duo, pl.ds(0, EDGE)], taken_e.at[slot, pl.ds(0, EDGE)]),
            (ens.at[duo, pl.ds(ROWS - EDGE, EDGE)], taken_e.at[slot, pl.ds(EDGE, EDGE)]),
            (halo_t.at[duo], taken_h.at[slot, pl.ds(0, EDGE)]),
            (halo_b.at[duo], taken_h.at[slot, pl.ds(EDGE, EDGE)]),
        )
        return [pltpu.make_async_copy(a, b, sem.at[i, slot]) for i, (a, b) in enumerate(copies)]

    for copy in fetch(0):
        copy.start()
    out[...] = jnp.zeros_like(out)
    for x in range(EDGE):
        wide[x] = widen(adj_t[0, x])
        wide[EDGE + x] = widen(adj_b[0, x])

    for border, start in ((border0, 0), (border1, FIRST)):

        @pl.loop(0, border.shape[0])
        def _(step):
            duo = start + step
            slot = duo % 2

            @pl.when(duo < DUOS - 1)
            def _():
                for copy in fetch(duo + 1):
                    copy.start()

            for copy in fetch(duo):
                copy.wait()

            @pl.loop(0, PAD // 16, unroll=True)
            def _(group):
                at = pl.ds(pl.multiple_of(group * 16, 16), 16)

                for part in range(2):
                    eight = pl.ds(pl.multiple_of(group * 16 + part * 8, 8), 8)

                    def emit(x, value):
                        value = value + border[step, x, eight, :]
                        if part == 0:
                            first[x] = value
                        else:
                            put_split(field, x, at, jnp.concatenate([first[x], value], axis=0))

                    def get_t(x):
                        return taken_h[slot, x + EDGE, eight, :] * wide[x + EDGE, eight, :]

                    def get_b(x):
                        return taken_h[slot, x - EDGE, eight, :] * wide[x - EDGE, eight, :]

                    diffuse(get_t, range(-EDGE, 0), range(EDGE), beside_duo, emit)
                    diffuse(get_b, range(2 * EDGE, 3 * EDGE), range(EDGE, 2 * EDGE), beside_duo, emit)

            for x in range(2 * EDGE):
                out[x] += taken_e[slot, x].astype(F32) * mix(weights[...], field[x])


def outer(ens, halo_t, halo_b, adj_t, adj_b, border0, border1, weights):
    spec, far = pl.BlockSpec(memory_space=pltpu.VMEM), pl.BlockSpec(memory_space=pltpu.HBM)
    return pl.pallas_call(
        outer_kernel,
        name="outer",
        out_shape=jax.ShapeDtypeStruct((2 * EDGE, PAD, DUO), F32),
        in_specs=[far] * 3 + [spec] * 5,
        out_specs=spec,
        scratch_shapes=[
            pltpu.VMEM((2 * EDGE, 2 * PAD, DUO), BF16),
            pltpu.VMEM((2 * EDGE, 8, DUO), F32),
            pltpu.VMEM((2 * EDGE, PAD, DUO), F32),
            pltpu.VMEM((2, 2 * EDGE, PAD, DUO), BF16),
            pltpu.VMEM((2, 2 * EDGE, PAD, DUO), F32),
            pltpu.SemaphoreType.DMA((4, 2)),
        ],
        compiler_params=params(),
        cost_estimate=cost(MEM * 10**9, MEM * 3 * 10**6),
    )(ens, halo_t, halo_b, adj_t, adj_b, border0, border1, weights)


def edge_kernel(strip, adj, halo_t, halo_b, weights, place, inside, border, out, field, halo_adj):
    top_open = jnp.where(place[0] == 0, 0.0, 1.0)
    bottom_open = jnp.where(place[0] == place[2], 0.0, 1.0)
    left_open = jnp.where(place[1] == 0, 0.0, 1.0)
    right_open = jnp.where(place[1] == place[3], 0.0, 1.0)
    member, source = strip_place(iota((COLS, COLS), 0), MEM + 1)
    target = strip_place(iota((COLS, COLS), 1))[1]
    repeat = one_hot((member == MEM) & (source == target))
    for i, halo in enumerate((halo_t, halo_b)):
        for x in range(EDGE):
            high, low = split(halo[1, x], 2)
            halo_adj[i * EDGE + x] = dot(high, repeat) + dot(low, repeat)

    @pl.loop(0, PAD // 16)
    def _(group):
        at = pl.ds(pl.multiple_of(group * 16, 16), 16)
        c = strip_place(iota((16, COLS), 1))[1]
        lanes = jnp.where(c < 3, left_open, jnp.where(c >= 15, right_open, 1.0))

        def mask(x, value):
            value = value * lanes
            if x < 0:
                return value * top_open
            if x >= ROWS:
                return value * bottom_open
            return value

        def get(x):
            if x < 0:
                return halo_t[1, x + EDGE, at, :] * halo_adj[x + EDGE, at, :]
            if x >= ROWS:
                return halo_b[1, x - ROWS, at, :] * halo_adj[x - ROWS + EDGE, at, :]
            return strip[x, at, :].astype(F32) * adj[x, at, :]

        def emit(x, value):
            put_split(field, x, at, value)

        diffuse(get, range(-EDGE, ROWS + EDGE), range(ROWS), beside_permuted, emit, mask)

    c = strip_place(iota((COLS, COLS), 0))[1]
    spot = jnp.where((c >= 3) & (c < 6), c - 3, jnp.where((c >= 12) & (c < 15), 241 + c, -1))
    collect = one_hot(spot == natural(iota((COLS, COLS), 1)))
    y = natural(iota((PAD, COLS), 1))
    middle = (y >= EDGE) & (y < COLS - EDGE)
    for x in range(ROWS):
        if EDGE <= x < ROWS - EDGE:
            value = inside[x - EDGE]
        else:
            value = border[x if x < EDGE else x - INNER]
        value = jnp.where(middle, fold(value), 0.0)
        product = strip[x].astype(F32) * mix(weights[...], field[x])
        for piece in split(product, 2):
            value = value + dot(piece, collect)
        out[x] = value * SCALE


def edge(strip, adj, halo_t, halo_b, weights, place, inside, border):
    spec = pl.BlockSpec(memory_space=pltpu.VMEM)
    return pl.pallas_call(
        edge_kernel,
        name="edge",
        out_shape=jax.ShapeDtypeStruct((ROWS, PAD, COLS), F32),
        in_specs=[spec] * 5 + [pl.BlockSpec(memory_space=pltpu.SMEM)] + [spec] * 2,
        out_specs=spec,
        scratch_shapes=[pltpu.VMEM((ROWS, 2 * PAD, COLS), BF16), pltpu.VMEM((2 * EDGE, PAD, COLS), F32)],
        compiler_params=params(),
        cost_estimate=cost(4 * 10**9, 8 * 10**6),
    )(strip, adj, halo_t, halo_b, weights, place, inside, border)


def gather_kernel(field, level, column, pos, rows_of, out, table, picked):
    for x in range(ROWS):
        table[x, :PAD, :], table[x, PAD:, :] = split(field[x], 2)
    picked[...] = jnp.zeros_like(picked)

    @pl.loop(0, TILES // 8)
    def _(j):
        first = pl.multiple_of(j * 8, 8)
        levels, columns = level[pl.ds(first, 8), :].astype(I32), column[pl.ds(first, 8), :].astype(I32)
        lines = []
        for q in range(8):
            at = slice(q, q + 1)
            found = dot(table[rows_of[0, j * 8 + q]], one_hot(iota((COLS, COLS), 0) == columns[at, :]))
            found = jnp.where(iota((PAD, COLS), 0) == levels[at, :], found[:PAD] + found[PAD:], 0.0)
            lines.append(jnp.sum(found, axis=0, keepdims=True))
        picked[pl.ds(first, 8), :] = jnp.concatenate(lines, axis=0)

    both = jnp.concatenate(split(picked[...], 2), axis=0)
    tile, spot = pos[...] >> 8, pos[...] & 255
    lines = []
    for c in range(CHUNKS):
        found = dot(both, one_hot(iota((COLS, COLS), 0) == spot[c : c + 1, :]))
        found = jnp.where(iota((SPACE, COLS), 0) == tile[c : c + 1, :], found[:SPACE] + found[SPACE:], 0.0)
        found = jnp.sum(found, axis=0, keepdims=True)
        lines += [found[:, :HALF], found[:, HALF:]]
    out[...] = jnp.concatenate(lines + [jnp.zeros((HALF - CAP, DEV), F32)], axis=0).T


def gather(field, level, column, pos, rows_of):
    spec = pl.BlockSpec(memory_space=pltpu.VMEM)
    return pl.pallas_call(
        gather_kernel,
        name="gather",
        out_shape=jax.ShapeDtypeStruct((DEV, HALF), F32),
        in_specs=[spec] * 4 + [pl.BlockSpec(memory_space=pltpu.SMEM)],
        out_specs=spec,
        scratch_shapes=[
            pltpu.VMEM((ROWS, 2 * PAD, COLS), BF16),
            pltpu.VMEM((SPACE, COLS), F32),
        ],
        compiler_params=params(),
        cost_estimate=cost(10**10, 2 * 10**6),
    )(field, level, column, pos, rows_of)


def restore_kernel(field, out, rows):
    perm_y = one_hot(natural(iota((COLS, COLS), 0)) == iota((COLS, COLS), 1))
    i = iota((256, 1), 0)
    perm_r = one_hot(iota((256, 256), 1) == (i & 15) * 16 + (i >> 4))
    for x in range(ROWS):
        value = field[x]
        high, low = split(value, 2)
        rows[x] = dot(high, perm_y) + dot(low, perm_y)
    for b in range(6):
        block = jnp.concatenate([rows[x, b * 16 : (b + 1) * 16, :] for x in range(ROWS)], axis=0)
        high, low = split(block, 2)
        value = dot(perm_r, high) + dot(perm_r, low)
        if b < 5:
            out[b * 256 : (b + 1) * 256, :] = value
        else:
            out[1280:1440, :] = value[:160]


def restore(field):
    spec = pl.BlockSpec(memory_space=pltpu.VMEM)
    return pl.pallas_call(
        restore_kernel,
        name="restore",
        out_shape=jax.ShapeDtypeStruct((LEV * ROWS, COLS), F32),
        in_specs=[spec],
        out_specs=spec,
        scratch_shapes=[pltpu.VMEM((ROWS, PAD, COLS), F32)],
        compiler_params=params(),
        cost_estimate=cost(10**9, 3 * 10**6),
    )(field).reshape(LEV, ROWS, COLS)


def forward(value, axis):
    size = lax.axis_size(axis)
    return lax.ppermute(value, axis, [(i, i + 1) for i in range(size - 1)])


def backward(value, axis):
    size = lax.axis_size(axis)
    return lax.ppermute(value, axis, [(i + 1, i) for i in range(size - 1)])


FIRST = 2


def body(ensemble, vertical_weights, dual_vector, observed_column, observed_level, active_count):
    place = jnp.stack(
        [lax.axis_index("gx"), lax.axis_index("gy"), lax.axis_size("gx") - 1, lax.axis_size("gy") - 1]
    ).astype(I32)
    outgoing, target, rank, weights = pack(
        active_count, dual_vector, observed_column, observed_level, vertical_weights
    )
    ensemble, outgoing = lax.optimization_barrier((ensemble, outgoing))
    incoming = lax.all_to_all(outgoing, ("gx", "gy"), split_axis=0, concat_axis=0, tiled=True)
    ens, ens_up, ens_down, strip, ens_l, ens_r = arrange(ensemble)
    incoming, ens_up, ens_down = lax.optimization_barrier((incoming, ens_up, ens_down))
    halo_t = forward(ens_down, "gx")
    halo_b = backward(ens_up, "gx")

    adj, wide, side_l, side_r, *slots = scatter(incoming, ens_l, ens_r)
    from_left = forward(side_r, "gy")
    from_right = backward(side_l, "gy")
    border0, inside = inner(ens, wide, weights, place, 0, FIRST)
    from_left, from_right, inside = lax.optimization_barrier((from_left, from_right, inside))
    strip, adj_strip, up, down = strips(strip, adj, from_left, from_right)
    top = forward(down, "gx")
    bottom = backward(up, "gx")
    border1, inside = inner(ens, wide, weights, place, FIRST, DUOS - FIRST, (inside,))

    outside = outer(ens, halo_t, halo_b, top, bottom, border0, border1, weights)
    field = edge(strip, adj_strip, top, bottom, weights, place, inside, outside)
    picked = gather(field, *slots)
    back = lax.all_to_all(picked, ("gx", "gy"), split_axis=0, concat_axis=0, tiled=True)
    increment = restore(field)
    obs_product = unpack(back, target, rank)
    return (increment, obs_product)


def solution(mesh):
    placed = (
        P(None, None, "gx", "gy"),
        P(),
        P(("gx", "gy")),
        P(("gx", "gy")),
        P(("gx", "gy")),
        P(("gx", "gy")),
    )
    return jax.shard_map(
        body,
        mesh=mesh,
        in_specs=placed,
        out_specs=(P(None, "gx", "gy"), P(("gx", "gy"))),
        check_vma=False,
    )
```

```python
import jax
import jax.numpy as jnp
from jax import lax
from jax.experimental import pallas as pl
from jax.experimental.pallas import tpu as pltpu
from jax.sharding import PartitionSpec as P

F32 = jnp.float32
BF16 = jnp.bfloat16
I32 = jnp.int32

MEM, LEV, ROWS, COLS = 10, 90, 16, 256
PAD = 96
DEV = 128
CAP = 48
SLOTS = 2048
HALF = 128
QUARTER = 64
DUO = 2 * COLS
DUOS = MEM // 2
EDGE = 3
STRIP = 18
PAIRS = STRIP // 2
SELF = 1.0 / 6.0
SCALE = 0.24**3 / (MEM - 1)
VMEM = 20 * 1024 * 1024
MOST = 58 * 1024 * 1024
ALL = 63 * 1024 * 1024


def split(value, count):
    parts = []
    for _ in range(count - 1):
        top = value.astype(BF16)
        parts.append(top)
        value = value - top.astype(F32)
    parts.append(value.astype(BF16))
    return parts


def dot(a, b):
    return lax.dot_general(a, b, (((1,), (0,)), ((), ())), preferred_element_type=F32)


def dot_nt(a, b):
    return lax.dot_general(a, b, (((1,), (1,)), ((), ())), preferred_element_type=F32)


def iota(shape, dim):
    return lax.broadcasted_iota(I32, shape, dim)


def one_hot(test):
    return jnp.where(test, 1.0, 0.0).astype(BF16)


def params(limit=VMEM):
    return pltpu.CompilerParams(vmem_limit_bytes=limit)


def cost(flops, moved):
    return pl.CostEstimate(flops=flops, bytes_accessed=moved, transcendentals=0)


def pack_kernel(
    count, dual_far, col_far, lev_far, vertical_far, out, tgt_out, rank_out, weights, left_v, left_c, right_v, right_c, dual, col, lev, vertical, sem
):
    pairs = ((col_far, col), (lev_far, lev), (dual_far, dual), (vertical_far, vertical))
    copies = [pltpu.make_async_copy(a, b, sem.at[i]) for i, (a, b) in enumerate(pairs)]
    for copy in copies:
        copy.start()
    for copy in copies:
        copy.wait()
    wide = jnp.concatenate([vertical[...], jnp.zeros((LEV, PAD - LEV), F32)], axis=1)
    high, low = split(jnp.concatenate([wide, jnp.zeros((PAD - LEV, PAD), F32)], axis=0), 2)
    both = jnp.concatenate([low, jnp.zeros_like(low)], axis=1)
    weights[...] = jnp.concatenate([jnp.concatenate([high, high], axis=1), both], axis=0)
    number = count[0]
    lane = iota((DEV, COLS), 1)
    upper = one_hot((lane > iota((DEV, COLS), 0)) | (lane >= HALF))
    rows = iota((DEV, HALF), 0)
    lane = iota((1, HALF), 1)
    carry = jnp.zeros((DEV, HALF), F32)
    for i in range(SLOTS // HALF):
        at = slice(i * HALF, (i + 1) * HALF)
        column = col[i : i + 1, :]
        row = column >> 12
        gcol = column & 4095
        y = gcol & 255
        y = ((y & 3) << 6) + (y >> 2)
        target = ((row >> 4) << 4) + (gcol >> 8)
        target = jnp.where(i * HALF + lane < number, target, -1)
        hit = rows == target
        both = dot(one_hot(hit), upper)
        rank = jnp.sum(jnp.where(hit, both[:, :HALF] + carry, 0.0), axis=0, keepdims=True)
        carry = carry + both[:, HALF:]
        tgt_out[i : i + 1, :] = target
        rank = rank.astype(I32)
        rank_out[i : i + 1, :] = rank
        right_v[:, at] = one_hot(rows == rank)
        right_c[:, at] = one_hot(rows == rank + CAP)
        values = dual[i : i + 1, :]
        for p, piece in enumerate(split(values, 3)):
            left_v[p * DEV : (p + 1) * DEV, at] = jnp.where(hit, piece.astype(F32), 0.0).astype(BF16)
        cells = (lev[i : i + 1, :] << 12, (row & 15) << 8, y + 1)
        for p, piece in enumerate(cells):
            left_c[p * DEV : (p + 1) * DEV, at] = jnp.where(hit, piece.astype(F32), 0.0).astype(BF16)
    a = dot_nt(left_v[...], right_v[...])
    b = dot_nt(left_c[...], right_c[...])
    out[...] = ((a[:DEV] + a[DEV : 2 * DEV]) + a[2 * DEV :]) + ((b[:DEV] + b[DEV : 2 * DEV]) + b[2 * DEV :])


def pack(count, dual, col, lev, vertical):
    spec = pl.BlockSpec(memory_space=pltpu.VMEM)
    return pl.pallas_call(
        pack_kernel,
        name="pack",
        out_shape=(
            jax.ShapeDtypeStruct((DEV, HALF), F32),
            jax.ShapeDtypeStruct((SLOTS // HALF, HALF), I32),
            jax.ShapeDtypeStruct((SLOTS // HALF, HALF), I32),
            jax.ShapeDtypeStruct((2 * PAD, 2 * PAD), BF16),
        ),
        in_specs=[pl.BlockSpec(memory_space=pltpu.SMEM)] + [pl.BlockSpec(memory_space=pltpu.HBM)] * 4,
        out_specs=(spec,) * 4,
        scratch_shapes=[pltpu.VMEM((3 * DEV, SLOTS), BF16)] * 2
        + [pltpu.VMEM((DEV, SLOTS), BF16)] * 2
        + [pltpu.VMEM((SLOTS // HALF, HALF), kind) for kind in (F32, I32, I32)]
        + [pltpu.VMEM((LEV, LEV), F32), pltpu.SemaphoreType.DMA((4,))],
        compiler_params=params(ALL),
        cost_estimate=cost(10**9, 10**6),
    )(count, dual.reshape(-1, HALF), col.reshape(-1, HALF), lev.reshape(-1, HALF), vertical)


def unpack_kernel(back, tgt, rank, out):
    rows = iota((DEV, HALF), 0)
    table = jnp.concatenate(split(back[...], 3), axis=0)
    for i in range(SLOTS // HALF):
        found = dot(table, one_hot(rows == rank[i : i + 1, :]))
        found = (found[:DEV] + found[DEV : 2 * DEV]) + found[2 * DEV :]
        out[i : i + 1, :] = jnp.sum(jnp.where(rows == tgt[i : i + 1, :], found, 0.0), axis=0, keepdims=True)


def unpack(back, tgt, rank):
    spec = pl.BlockSpec(memory_space=pltpu.VMEM)
    return pl.pallas_call(
        unpack_kernel,
        name="unpack",
        out_shape=jax.ShapeDtypeStruct((SLOTS // HALF, HALF), F32),
        in_specs=[spec] * 3,
        out_specs=spec,
        compiler_params=params(),
        cost_estimate=cost(10**8, 10**5),
    )(back, tgt, rank).reshape(SLOTS)


def strip_place(lane, members=MEM):
    j = lane % HALF
    return j // PAIRS, jnp.where(j < members * PAIRS, j % PAIRS * 2 + lane // HALF, -1)


def natural(place):
    return ((place & 63) << 2) + (place >> 6)


def duo_place(place):
    return ((place & 63) << 2) + (place >> 7), (place >> 6) & 1


def widen(value):
    low = iota((value.shape[0], HALF), 1) < QUARTER
    phases = []
    for half in (value[:, :HALF], value[:, HALF:]):
        turned = pltpu.roll(half, QUARTER, 1)
        phases += [jnp.where(low, half, turned), jnp.where(low, turned, half)]
    return jnp.concatenate(phases, axis=1)


def fold(value):
    low = iota((value.shape[0], HALF), 1) < QUARTER
    p = [value[:, i * HALF : (i + 1) * HALF] for i in range(4)]
    return jnp.concatenate(
        [jnp.where(low, p[i], p[i + 1]) + pltpu.roll(jnp.where(low, p[i + 1], p[i]), QUARTER, 1) for i in (0, 2)],
        axis=1,
    )


def arrange_kernel(
    ens, out, up, down, strip, side_l, side_r, taken, rows, turned_out, up_out, down_out, strip_acc, perm_y, perm_r, sides_out, sem, sem_out
):
    def fetch(k):
        return pltpu.make_async_copy(ens.at[k], taken.at[k], sem.at[k])

    def send(duo):
        slot = duo % 2
        return (
            pltpu.make_async_copy(turned_out.at[slot], out.at[duo], sem_out.at[0, slot]),
            pltpu.make_async_copy(up_out.at[slot], up.at[duo], sem_out.at[1, slot]),
            pltpu.make_async_copy(down_out.at[slot], down.at[duo], sem_out.at[2, slot]),
        )

    for k in range(MEM):
        fetch(k).start()
    rows[LEV * ROWS :, :] = jnp.zeros((rows.shape[0] - LEV * ROWS, DUO), BF16)
    strip_acc[...] = jnp.zeros_like(strip_acc)
    y, which = duo_place(iota((1, DUO), 1))
    perm_y[...] = one_hot(iota((DUO, DUO), 0) == which * COLS + y)
    i = iota((256, 1), 0)
    perm_r[...] = one_hot(iota((256, 256), 1) == (i & 15) * 16 + (i >> 4))

    @pl.loop(0, DUOS)
    def _(duo):
        @pl.when(duo >= 2)
        def _():
            for copy in send(duo - 2):
                copy.wait()

        fetch(2 * duo).wait()
        fetch(2 * duo + 1).wait()
        here, there, slot = 2 * duo, 2 * duo + 1, duo % 2
        lane = iota((COLS, COLS), 0)
        y, which = jnp.where(lane % HALF < QUARTER, lane % HALF, lane % HALF + HALF), lane // HALF
        member, c = strip_place(iota((1, COLS), 1))
        want = jnp.where(y < 6, 3 + y, jnp.where(y >= 250, y - 241, -2))
        select = one_hot((member == 2 * duo + which) & (c == want))
        outside = iota((LEV * ROWS, HALF), 1) < QUARTER
        ends = [jnp.where(outside, taken[k, :, :HALF], taken[k, :, HALF:]) for k in (here, there)]
        block = jnp.concatenate([taken[here], taken[there]], axis=1)
        rows[: LEV * ROWS, :] = dot(block, perm_y[...]).astype(BF16)
        for b in range(6):
            turned = dot(perm_r[...], rows[b * 256 : (b + 1) * 256, :])
            at = slice(b * 16, (b + 1) * 16)
            for x in range(ROWS):
                part = turned[x * 16 : (x + 1) * 16, :]
                turned_out[slot, x, at, :] = part.astype(BF16)
                if x < EDGE:
                    up_out[slot, x, at, :] = part
                if x >= ROWS - EDGE:
                    down_out[slot, x - (ROWS - EDGE), at, :] = part
        for copy in send(duo):
            copy.start()
        strip_acc[: LEV * ROWS, :] += dot(jnp.concatenate(ends, axis=1), select)

    member, c = strip_place(iota((COLS, COLS), 0))
    for b in range(6):
        turned = dot(perm_r[...], strip_acc[b * 256 : (b + 1) * 256, :].astype(BF16)).astype(BF16)
        for x in range(ROWS):
            strip[x, b * 16 : (b + 1) * 16, :] = turned[x * 16 : (x + 1) * 16, :]
    left, right = (c >= 3) & (c < 6), (c >= 12) & (c < 15)
    spot = jnp.where(left, 3 * member + c - 3, jnp.where(right, HALF + 3 * member + c - 12, -1000))
    places = [one_hot(iota((COLS, COLS), 1) == spot + 30 * j) for j in range(4)]
    for group in range(4):
        sides = jnp.zeros((PAD, COLS), F32)
        for j in range(4):
            sides = sides + dot(strip[group * 4 + j], places[j])
        sides_out[0, group] = sides[:, :HALF]
        sides_out[1, group] = sides[:, HALF:]
    copies = [
        pltpu.make_async_copy(sides_out.at[i], side.at[pl.ds(0, 4)], sem_out.at[3, i]) for i, side in enumerate((side_l, side_r))
    ]
    for copy in copies:
        copy.start()
    for duo in (DUOS - 2, DUOS - 1):
        for copy in send(duo):
            copy.wait()
    for copy in copies:
        copy.wait()


def arrange(ensemble):
    spec, far = pl.BlockSpec(memory_space=pltpu.VMEM), pl.BlockSpec(memory_space=pltpu.HBM)
    return pl.pallas_call(
        arrange_kernel,
        name="arrange",
        out_shape=(
            jax.ShapeDtypeStruct((DUOS, ROWS, PAD, DUO), BF16),
            jax.ShapeDtypeStruct((DUOS, EDGE, PAD, DUO), F32),
            jax.ShapeDtypeStruct((DUOS, EDGE, PAD, DUO), F32),
            jax.ShapeDtypeStruct((ROWS, PAD, COLS), BF16),
            jax.ShapeDtypeStruct((5, PAD, HALF), F32),
            jax.ShapeDtypeStruct((5, PAD, HALF), F32),
        ),
        in_specs=[far],
        out_specs=(far, far, far, spec, far, far),
        scratch_shapes=[
            pltpu.VMEM((MEM, LEV * ROWS, COLS), BF16),
            pltpu.VMEM((PAD * ROWS, DUO), BF16),
            pltpu.VMEM((2, ROWS, PAD, DUO), BF16),
            pltpu.VMEM((2, EDGE, PAD, DUO), F32),
            pltpu.VMEM((2, EDGE, PAD, DUO), F32),
            pltpu.VMEM((ROWS * PAD, COLS), F32),
            pltpu.VMEM((DUO, DUO), BF16),
            pltpu.VMEM((256, 256), BF16),
            pltpu.VMEM((2, 4, PAD, HALF), F32),
            pltpu.SemaphoreType.DMA((MEM,)),
            pltpu.SemaphoreType.DMA((4, 2)),
        ],
        compiler_params=params(MOST),
        cost_estimate=cost(10**10, 25 * 10**6),
    )(ensemble.reshape(MEM, LEV * ROWS, COLS))


CHUNKS = CAP // 2
TILES = CHUNKS + ROWS
SPACE = 48


def scatter_kernel(
    incoming, ens_l, ens_r, out, wide, side_l, side_r, level_out, column_out, pos_out, row_out,
    turned, hot, left, right, rows_of, sorted_, sides_out, sem
):
    turned[...] = incoming[...].T
    pairs = [[turned[pl.ds(first + i, CHUNKS, stride=2), :] for i in range(2)] for first in (0, CAP)]
    values = jnp.concatenate(pairs[0], axis=1)
    cells = jnp.concatenate(pairs[1], axis=1).astype(I32) - 1
    full = cells >= 0
    x = jnp.where(full, (cells >> 8) & 15, 99)

    for c in range(CHUNKS):
        hot[c * ROWS : (c + 1) * ROWS, :] = one_hot(iota((ROWS, COLS), 0) == x[c : c + 1, :])
    lane = iota((COLS, COLS + HALF), 1)
    both = dot(hot[...], one_hot((lane > iota((COLS, COLS + HALF), 0)) | (lane >= COLS)))
    before = jnp.zeros((ROWS, HALF), F32)
    earlier = []
    for c in range(CHUNKS):
        earlier.append(before)
        before = before + both[c * ROWS : (c + 1) * ROWS, COLS:]
    needed = ((before.astype(I32) + 255) >> 8).astype(F32).astype(BF16)
    start = dot(one_hot(iota((ROWS, ROWS), 1) < iota((ROWS, ROWS), 0)), needed)
    lines = []
    for c in range(CHUNKS):
        base = start * 256.0 + earlier[c]
        spots = both[c * ROWS : (c + 1) * ROWS, :COLS] + jnp.concatenate([base, base], axis=1)
        spots = jnp.where(iota((ROWS, COLS), 0) == x[c : c + 1, :], spots, 0.0)
        lines.append(jnp.sum(spots, axis=0, keepdims=True))
    pos = jnp.concatenate(lines, axis=0).astype(I32)
    pos = jnp.where(full, pos, -1)
    pos_out[...] = pos
    begun = jnp.where(start[:ROWS].astype(I32) <= iota((ROWS, HALF), 1), 1.0, 0.0)
    row_out[...] = jnp.sum(begun, axis=0, keepdims=True).astype(I32) - 1
    copy = pltpu.make_async_copy(row_out, rows_of, sem.at[0])
    copy.start()

    parts = [p.astype(F32) for p in split(values, 2)] + [(cells >> 12).astype(F32), (cells & 255).astype(F32)]
    tile, spot = pos >> 8, pos & 255
    for c in range(CHUNKS):
        at = slice(c * COLS, (c + 1) * COLS)
        hit = iota((SPACE, COLS), 0) == tile[c : c + 1, :]
        for p, part in enumerate(parts):
            left[p * SPACE : (p + 1) * SPACE, at] = jnp.where(hit, part[c : c + 1, :], 0.0).astype(BF16)
        right[:, at] = one_hot(iota((COLS, COLS), 0) == spot[c : c + 1, :])
    sorted_[...] = dot_nt(left[...], right[...])
    level_out[...] = sorted_[2 * SPACE : 3 * SPACE, :]
    column_out[...] = sorted_[3 * SPACE :, :]
    out[...] = jnp.zeros_like(out)
    copy.wait()

    @pl.loop(0, TILES // 8)
    def _(j):
        high, low, level, column = (sorted_[pl.ds(pl.multiple_of(p * SPACE + j * 8, 8), 8), :] for p in range(4))
        level, column = level.astype(I32), column.astype(I32)
        for half in range(2):
            results = []
            for q in range(half * 4, half * 4 + 4):
                at = slice(q, q + 1)
                hit = iota((PAD, COLS), 0) == level[at, :]
                lhs = jnp.concatenate([jnp.where(hit, high[at, :], 0.0), jnp.where(hit, low[at, :], 0.0)], axis=0)
                both = dot_nt(lhs.astype(BF16), one_hot(iota((COLS, COLS), 0) == column[at, :]))
                results.append(both[:PAD] + both[PAD:])
            for i, result in enumerate(results):
                out[rows_of[0, j * 8 + half * 4 + i]] += result

    y = natural(iota((COLS, COLS), 0))
    lane = iota((COLS, COLS), 1)
    place = jnp.where(y < 3, y, jnp.where(y >= 253, HALF + y - 253, -1000))
    packed = jnp.zeros((PAD, COLS), F32)
    for x in range(ROWS):
        select = one_hot(lane == place + 3 * x)
        for piece in split(out[x], 2):
            packed = packed + dot(piece, select)
    sides_out[0] = packed[:, :HALF]
    sides_out[1] = packed[:, HALF:]
    copies = [pltpu.make_async_copy(sides_out.at[i], side.at[4], sem.at[i]) for i, side in enumerate((side_l, side_r))]
    for copy in copies:
        copy.start()
    for x in range(ROWS):
        wide[x] = widen(out[x])
    for copy in copies:
        copy.wait()


def scatter(incoming, ens_l, ens_r):
    spec, far = pl.BlockSpec(memory_space=pltpu.VMEM), pl.BlockSpec(memory_space=pltpu.HBM)
    return pl.pallas_call(
        scatter_kernel,
        name="scatter",
        out_shape=(
            jax.ShapeDtypeStruct((ROWS, PAD, COLS), F32),
            jax.ShapeDtypeStruct((ROWS, PAD, DUO), F32),
            jax.ShapeDtypeStruct((5, PAD, HALF), F32),
            jax.ShapeDtypeStruct((5, PAD, HALF), F32),
            jax.ShapeDtypeStruct((SPACE, COLS), F32),
            jax.ShapeDtypeStruct((SPACE, COLS), F32),
            jax.ShapeDtypeStruct((CHUNKS, COLS), I32),
            jax.ShapeDtypeStruct((1, HALF), I32),
        ),
        in_specs=[spec, far, far],
        out_specs=(spec, spec, far, far, spec, spec, spec, spec),
        input_output_aliases={1: 2, 2: 3},
        scratch_shapes=[
            pltpu.VMEM((HALF, DEV), F32),
            pltpu.VMEM((CHUNKS * ROWS, COLS), BF16),
            pltpu.VMEM((4 * SPACE, CHUNKS * COLS), BF16),
            pltpu.VMEM((COLS, CHUNKS * COLS), BF16),
            pltpu.SMEM((1, HALF), I32),
            pltpu.VMEM((4 * SPACE, COLS), F32),
            pltpu.VMEM((2, PAD, HALF), F32),
            pltpu.SemaphoreType.DMA((2,)),
        ],
        compiler_params=params(),
        cost_estimate=cost(10**10, 2 * 10**6),
    )(incoming, ens_l, ens_r)


def strips_kernel(strip, adjoint, left, right, ens_out, out, up, down):
    lane = iota((COLS, COLS), 1)
    member, member_c = strip_place(lane, MEM + 1)
    y = natural(iota((COLS, COLS), 0))
    own = one_hot(member_c == jnp.where(y < 6, 3 + y, jnp.where(y >= 250, y - 241, -2)))
    from_lane = iota((HALF, COLS), 0)
    member_c, member = member_c[:HALF], member[:HALF]
    pieces = [split(side[4], 2) for side in (left, right)]
    ens_lanes = iota((PAD, COLS), 1) % HALF < MEM * PAIRS
    for x in range(ROWS):
        ens_value = strip[x].astype(F32)
        first = x % 4 * 30 + 3 * member
        for side, shift in ((left, 0), (right, 15)):
            inside = (member_c >= shift) & (member_c < shift + 3) & (member < MEM)
            spot = one_hot(inside & (from_lane == first + member_c - shift))
            ens_value = ens_value + dot(side[x // 4].astype(BF16), spot)
        ens_out[x] = ens_value.astype(BF16)
        value = jnp.zeros((PAD, COLS), F32)
        for piece in split(adjoint[x], 2):
            value = value + dot(piece, own)
        for side, shift in ((pieces[0], 0), (pieces[1], 15)):
            inside = (member_c >= shift) & (member_c < shift + 3)
            spot = one_hot(inside & (from_lane == 3 * x + member_c - shift))
            for piece in side:
                value = value + dot(piece, spot)
        out[x] = value
        for target, start in ((up, 0), (down, ROWS - EDGE)):
            if start <= x < start + EDGE:
                target[0, x - start] = adjoint[x]
                target[1, x - start] = jnp.where(ens_lanes, ens_value, value)


def strips(strip, adjoint, left, right):
    spec = pl.BlockSpec(memory_space=pltpu.VMEM)
    return pl.pallas_call(
        strips_kernel,
        name="strips",
        out_shape=(
            jax.ShapeDtypeStruct((ROWS, PAD, COLS), BF16),
            jax.ShapeDtypeStruct((ROWS, PAD, COLS), F32),
            jax.ShapeDtypeStruct((2, EDGE, PAD, COLS), F32),
            jax.ShapeDtypeStruct((2, EDGE, PAD, COLS), F32),
        ),
        in_specs=[spec] * 4,
        out_specs=(spec,) * 4,
        compiler_params=params(),
        cost_estimate=cost(10**9, 4 * 10**6),
    )(strip, adjoint, left, right)


def beside_permuted(value):
    even, odd = value[:, :HALF], value[:, HALF:]
    return jnp.concatenate([odd + pltpu.roll(odd, 1, 1), even + pltpu.roll(even, HALF - 1, 1)], axis=1)


def beside_duo(value):
    p = [value[:, i * HALF : (i + 1) * HALF] for i in range(4)]
    return jnp.concatenate(
        [pltpu.roll(p[3], 1, 1) + p[1], p[0] + p[2], p[1] + p[3], p[2] + pltpu.roll(p[0], HALF - 1, 1)], axis=1
    )


def total(terms):
    result = None
    for term in terms:
        if term is not None:
            result = term if result is None else result + term
    return result


def diffuse(get, given, wanted, beside, emit, mask=None):
    rows = [{} for _ in range(EDGE + 1)]
    for x in range(min(wanted) - EDGE, max(wanted) + EDGE + 1):
        if x in given:
            rows[0][x] = get(x)
        for step in range(1, EDGE + 1):
            at, reach, older = x - step, EDGE - step, rows[step - 1]
            if not min(wanted) - reach <= at <= max(wanted) + reach:
                continue
            terms = [older.get(at - 1), older.get(at + 1)]
            if at in older:
                terms += [beside(older[at]), older[at] * SELF]
            value = total(terms)
            if value is None:
                continue
            if step == EDGE:
                emit(at, value)
            else:
                rows[step][at] = value if mask is None else mask(at, value)


def put_split(ref, index, at, value):
    top = value.astype(BF16)
    ref[index, at, :] = top
    ref[index, pl.ds(at.start + PAD, 16), :] = (value - top.astype(F32)).astype(BF16)


def mix(weights, field):
    both = dot(weights, field)
    return both[:PAD] + both[PAD:]


INNER = ROWS - 2 * EDGE


def inner_kernel(start, count, ens, adj, weights, place, *refs):
    border, out, field, first, taken, sem = refs[-6:]

    def fetch(step):
        return pltpu.make_async_copy(ens.at[start + step], taken.at[step % 2], sem.at[step % 2])

    fetch(0).start()
    out[...] = refs[0][...] if start else jnp.zeros_like(out)
    top_open = jnp.where(place[0] == 0, 0.0, 1.0)
    bottom_open = jnp.where(place[0] == place[2], 0.0, 1.0)

    def mask(x, value):
        if x < 0:
            return value * top_open
        if x >= ROWS:
            return value * bottom_open
        return value

    @pl.loop(0, count)
    def _(step):
        @pl.when(step < count - 1)
        def _():
            fetch(step + 1).start()

        fetch(step).wait()
        slot = step % 2

        @pl.loop(0, PAD // 16)
        def _(group):
            at = pl.ds(pl.multiple_of(group * 16, 16), 16)

            for part in range(2):
                eight = pl.ds(pl.multiple_of(group * 16 + part * 8, 8), 8)

                def get(x):
                    return taken[slot, x, at, :].astype(F32)[part * 8 : part * 8 + 8, :] * adj[x, eight, :]

                def emit(x, value):
                    if not EDGE <= x < ROWS - EDGE:
                        border[step, x if x < EDGE else x - INNER, eight, :] = value
                    elif part == 0:
                        first[x - EDGE] = value
                    else:
                        put_split(field, x - EDGE, at, jnp.concatenate([first[x - EDGE], value], axis=0))

                diffuse(get, range(ROWS), range(ROWS), beside_duo, emit, mask)

        for x in range(INNER):
            out[x] += taken[slot, x + EDGE].astype(F32) * mix(weights[...], field[x])


def inner(ens, adj, weights, place, start, count, before=()):
    spec, far = pl.BlockSpec(memory_space=pltpu.VMEM), pl.BlockSpec(memory_space=pltpu.HBM)
    return pl.pallas_call(
        lambda *refs: inner_kernel(start, count, *refs),
        name="inner",
        out_shape=(
            jax.ShapeDtypeStruct((count, 2 * EDGE, PAD, DUO), F32),
            jax.ShapeDtypeStruct((INNER, PAD, DUO), F32),
        ),
        in_specs=[far, spec, spec, pl.BlockSpec(memory_space=pltpu.SMEM)] + [spec] * len(before),
        out_specs=(spec,) * 2,
        scratch_shapes=[
            pltpu.VMEM((INNER, 2 * PAD, DUO), BF16),
            pltpu.VMEM((INNER, 8, DUO), F32),
            pltpu.VMEM((2, ROWS, PAD, DUO), BF16),
            pltpu.SemaphoreType.DMA((2,)),
        ],
        compiler_params=params(),
        cost_estimate=cost(count * 2 * 10**9, count * 2 * 10**6),
    )(ens, adj, weights, place, *before)


def outer_kernel(
    ens, halo_t, halo_b, adj_t, adj_b, border0, border1, weights, out, field, first, wide, taken_e, taken_h, sem
):
    def fetch(duo):
        slot = duo % 2
        copies = (
            (ens.at[duo, pl.ds(0, EDGE)], taken_e.at[slot, pl.ds(0, EDGE)]),
            (ens.at[duo, pl.ds(ROWS - EDGE, EDGE)], taken_e.at[slot, pl.ds(EDGE, EDGE)]),
            (halo_t.at[duo], taken_h.at[slot, pl.ds(0, EDGE)]),
            (halo_b.at[duo], taken_h.at[slot, pl.ds(EDGE, EDGE)]),
        )
        return [pltpu.make_async_copy(a, b, sem.at[i, slot]) for i, (a, b) in enumerate(copies)]

    for copy in fetch(0):
        copy.start()
    out[...] = jnp.zeros_like(out)
    for x in range(EDGE):
        wide[x] = widen(adj_t[0, x])
        wide[EDGE + x] = widen(adj_b[0, x])

    for border, start in ((border0, 0), (border1, FIRST)):

        @pl.loop(0, border.shape[0])
        def _(step):
            duo = start + step
            slot = duo % 2

            @pl.when(duo < DUOS - 1)
            def _():
                for copy in fetch(duo + 1):
                    copy.start()

            for copy in fetch(duo):
                copy.wait()

            @pl.loop(0, PAD // 16, unroll=True)
            def _(group):
                at = pl.ds(pl.multiple_of(group * 16, 16), 16)

                for part in range(2):
                    eight = pl.ds(pl.multiple_of(group * 16 + part * 8, 8), 8)

                    def emit(x, value):
                        value = value + border[step, x, eight, :]
                        if part == 0:
                            first[x] = value
                        else:
                            put_split(field, x, at, jnp.concatenate([first[x], value], axis=0))

                    def get_t(x):
                        return taken_h[slot, x + EDGE, eight, :] * wide[x + EDGE, eight, :]

                    def get_b(x):
                        return taken_h[slot, x - EDGE, eight, :] * wide[x - EDGE, eight, :]

                    diffuse(get_t, range(-EDGE, 0), range(EDGE), beside_duo, emit)
                    diffuse(get_b, range(2 * EDGE, 3 * EDGE), range(EDGE, 2 * EDGE), beside_duo, emit)

            for x in range(2 * EDGE):
                out[x] += taken_e[slot, x].astype(F32) * mix(weights[...], field[x])


def outer(ens, halo_t, halo_b, adj_t, adj_b, border0, border1, weights):
    spec, far = pl.BlockSpec(memory_space=pltpu.VMEM), pl.BlockSpec(memory_space=pltpu.HBM)
    return pl.pallas_call(
        outer_kernel,
        name="outer",
        out_shape=jax.ShapeDtypeStruct((2 * EDGE, PAD, DUO), F32),
        in_specs=[far] * 3 + [spec] * 5,
        out_specs=spec,
        scratch_shapes=[
            pltpu.VMEM((2 * EDGE, 2 * PAD, DUO), BF16),
            pltpu.VMEM((2 * EDGE, 8, DUO), F32),
            pltpu.VMEM((2 * EDGE, PAD, DUO), F32),
            pltpu.VMEM((2, 2 * EDGE, PAD, DUO), BF16),
            pltpu.VMEM((2, 2 * EDGE, PAD, DUO), F32),
            pltpu.SemaphoreType.DMA((4, 2)),
        ],
        compiler_params=params(),
        cost_estimate=cost(MEM * 10**9, MEM * 3 * 10**6),
    )(ens, halo_t, halo_b, adj_t, adj_b, border0, border1, weights)


def edge_kernel(strip, adj, halo_t, halo_b, weights, place, inside, border, out, field, halo_adj):
    top_open = jnp.where(place[0] == 0, 0.0, 1.0)
    bottom_open = jnp.where(place[0] == place[2], 0.0, 1.0)
    left_open = jnp.where(place[1] == 0, 0.0, 1.0)
    right_open = jnp.where(place[1] == place[3], 0.0, 1.0)
    member, source = strip_place(iota((COLS, COLS), 0), MEM + 1)
    target = strip_place(iota((COLS, COLS), 1))[1]
    repeat = one_hot((member == MEM) & (source == target))
    for i, halo in enumerate((halo_t, halo_b)):
        for x in range(EDGE):
            high, low = split(halo[1, x], 2)
            halo_adj[i * EDGE + x] = dot(high, repeat) + dot(low, repeat)

    @pl.loop(0, PAD // 16)
    def _(group):
        at = pl.ds(pl.multiple_of(group * 16, 16), 16)
        c = strip_place(iota((16, COLS), 1))[1]
        lanes = jnp.where(c < 3, left_open, jnp.where(c >= 15, right_open, 1.0))

        def mask(x, value):
            value = value * lanes
            if x < 0:
                return value * top_open
            if x >= ROWS:
                return value * bottom_open
            return value

        def get(x):
            if x < 0:
                return halo_t[1, x + EDGE, at, :] * halo_adj[x + EDGE, at, :]
            if x >= ROWS:
                return halo_b[1, x - ROWS, at, :] * halo_adj[x - ROWS + EDGE, at, :]
            return strip[x, at, :].astype(F32) * adj[x, at, :]

        def emit(x, value):
            put_split(field, x, at, value)

        diffuse(get, range(-EDGE, ROWS + EDGE), range(ROWS), beside_permuted, emit, mask)

    c = strip_place(iota((COLS, COLS), 0))[1]
    spot = jnp.where((c >= 3) & (c < 6), c - 3, jnp.where((c >= 12) & (c < 15), 241 + c, -1))
    collect = one_hot(spot == natural(iota((COLS, COLS), 1)))
    y = natural(iota((PAD, COLS), 1))
    middle = (y >= EDGE) & (y < COLS - EDGE)
    for x in range(ROWS):
        if EDGE <= x < ROWS - EDGE:
            value = inside[x - EDGE]
        else:
            value = border[x if x < EDGE else x - INNER]
        value = jnp.where(middle, fold(value), 0.0)
        product = strip[x].astype(F32) * mix(weights[...], field[x])
        for piece in split(product, 2):
            value = value + dot(piece, collect)
        out[x] = value * SCALE


def edge(strip, adj, halo_t, halo_b, weights, place, inside, border):
    spec = pl.BlockSpec(memory_space=pltpu.VMEM)
    return pl.pallas_call(
        edge_kernel,
        name="edge",
        out_shape=jax.ShapeDtypeStruct((ROWS, PAD, COLS), F32),
        in_specs=[spec] * 5 + [pl.BlockSpec(memory_space=pltpu.SMEM)] + [spec] * 2,
        out_specs=spec,
        scratch_shapes=[pltpu.VMEM((ROWS, 2 * PAD, COLS), BF16), pltpu.VMEM((2 * EDGE, PAD, COLS), F32)],
        compiler_params=params(),
        cost_estimate=cost(4 * 10**9, 8 * 10**6),
    )(strip, adj, halo_t, halo_b, weights, place, inside, border)


def gather_kernel(field, level, column, pos, rows_of, out, table, picked):
    for x in range(ROWS):
        table[x, :PAD, :], table[x, PAD:, :] = split(field[x], 2)
    picked[...] = jnp.zeros_like(picked)

    @pl.loop(0, TILES // 8)
    def _(j):
        first = pl.multiple_of(j * 8, 8)
        levels, columns = level[pl.ds(first, 8), :].astype(I32), column[pl.ds(first, 8), :].astype(I32)
        lines = []
        for q in range(8):
            at = slice(q, q + 1)
            found = dot(table[rows_of[0, j * 8 + q]], one_hot(iota((COLS, COLS), 0) == columns[at, :]))
            found = jnp.where(iota((PAD, COLS), 0) == levels[at, :], found[:PAD] + found[PAD:], 0.0)
            lines.append(jnp.sum(found, axis=0, keepdims=True))
        picked[pl.ds(first, 8), :] = jnp.concatenate(lines, axis=0)

    both = jnp.concatenate(split(picked[...], 2), axis=0)
    tile, spot = pos[...] >> 8, pos[...] & 255
    lines = []
    for c in range(CHUNKS):
        found = dot(both, one_hot(iota((COLS, COLS), 0) == spot[c : c + 1, :]))
        found = jnp.where(iota((SPACE, COLS), 0) == tile[c : c + 1, :], found[:SPACE] + found[SPACE:], 0.0)
        found = jnp.sum(found, axis=0, keepdims=True)
        lines += [found[:, :HALF], found[:, HALF:]]
    out[...] = jnp.concatenate(lines + [jnp.zeros((HALF - CAP, DEV), F32)], axis=0).T


def gather(field, level, column, pos, rows_of):
    spec = pl.BlockSpec(memory_space=pltpu.VMEM)
    return pl.pallas_call(
        gather_kernel,
        name="gather",
        out_shape=jax.ShapeDtypeStruct((DEV, HALF), F32),
        in_specs=[spec] * 4 + [pl.BlockSpec(memory_space=pltpu.SMEM)],
        out_specs=spec,
        scratch_shapes=[
            pltpu.VMEM((ROWS, 2 * PAD, COLS), BF16),
            pltpu.VMEM((SPACE, COLS), F32),
        ],
        compiler_params=params(),
        cost_estimate=cost(10**10, 2 * 10**6),
    )(field, level, column, pos, rows_of)


def restore_kernel(field, out, rows):
    perm_y = one_hot(natural(iota((COLS, COLS), 0)) == iota((COLS, COLS), 1))
    i = iota((256, 1), 0)
    perm_r = one_hot(iota((256, 256), 1) == (i & 15) * 16 + (i >> 4))
    for x in range(ROWS):
        value = field[x]
        high, low = split(value, 2)
        rows[x] = dot(high, perm_y) + dot(low, perm_y)
    for b in range(6):
        block = jnp.concatenate([rows[x, b * 16 : (b + 1) * 16, :] for x in range(ROWS)], axis=0)
        high, low = split(block, 2)
        value = dot(perm_r, high) + dot(perm_r, low)
        if b < 5:
            out[b * 256 : (b + 1) * 256, :] = value
        else:
            out[1280:1440, :] = value[:160]


def restore(field):
    spec = pl.BlockSpec(memory_space=pltpu.VMEM)
    return pl.pallas_call(
        restore_kernel,
        name="restore",
        out_shape=jax.ShapeDtypeStruct((LEV * ROWS, COLS), F32),
        in_specs=[spec],
        out_specs=spec,
        scratch_shapes=[pltpu.VMEM((ROWS, PAD, COLS), F32)],
        compiler_params=params(),
        cost_estimate=cost(10**9, 3 * 10**6),
    )(field).reshape(LEV, ROWS, COLS)


def forward(value, axis):
    size = lax.axis_size(axis)
    return lax.ppermute(value, axis, [(i, i + 1) for i in range(size - 1)])


def backward(value, axis):
    size = lax.axis_size(axis)
    return lax.ppermute(value, axis, [(i + 1, i) for i in range(size - 1)])


FIRST = 2


def body(ensemble, vertical_weights, dual_vector, observed_column, observed_level, active_count):
    place = jnp.stack(
        [lax.axis_index("gx"), lax.axis_index("gy"), lax.axis_size("gx") - 1, lax.axis_size("gy") - 1]
    ).astype(I32)
    outgoing, target, rank, weights = pack(
        active_count, dual_vector, observed_column, observed_level, vertical_weights
    )
    ensemble, outgoing = lax.optimization_barrier((ensemble, outgoing))
    incoming = lax.all_to_all(outgoing, ("gx", "gy"), split_axis=0, concat_axis=0, tiled=True)
    ens, ens_up, ens_down, strip, ens_l, ens_r = arrange(ensemble)
    incoming, ens_up, ens_down = lax.optimization_barrier((incoming, ens_up, ens_down))
    halo_t = forward(ens_down, "gx")
    halo_b = backward(ens_up, "gx")

    adj, wide, side_l, side_r, *slots = scatter(incoming, ens_l, ens_r)
    from_left = forward(side_r, "gy")
    from_right = backward(side_l, "gy")
    border0, inside = inner(ens, wide, weights, place, 0, FIRST)
    from_left, from_right, inside = lax.optimization_barrier((from_left, from_right, inside))
    strip, adj_strip, up, down = strips(strip, adj, from_left, from_right)
    top = forward(down, "gx")
    bottom = backward(up, "gx")
    border1, inside = inner(ens, wide, weights, place, FIRST, DUOS - FIRST, (inside,))

    outside = outer(ens, halo_t, halo_b, top, bottom, border0, border1, weights)
    field = edge(strip, adj_strip, top, bottom, weights, place, inside, outside)
    picked = gather(field, *slots)
    back = lax.all_to_all(picked, ("gx", "gy"), split_axis=0, concat_axis=0, tiled=True)
    increment = restore(field)
    obs_product = unpack(back, target, rank)
    return (increment, obs_product)


def solution(mesh):
    placed = (
        P(None, None, "gx", "gy"),
        P(),
        P(("gx", "gy")),
        P(("gx", "gy")),
        P(("gx", "gy")),
        P(("gx", "gy")),
    )
    return jax.shard_map(
        body,
        mesh=mesh,
        in_specs=placed,
        out_specs=(P(None, "gx", "gy"), P(("gx", "gy"))),
        check_vma=False,
    )
```

```python
import jax
import jax.numpy as jnp
from jax import lax
from jax.experimental import pallas as pl
from jax.experimental.pallas import tpu as pltpu
from jax.sharding import PartitionSpec as P

F32 = jnp.float32
BF16 = jnp.bfloat16
I32 = jnp.int32

MEM, LEV, ROWS, COLS = 10, 90, 16, 256
PAD = 96
DEV = 128
CAP = 48
SLOTS = 2048
HALF = 128
QUARTER = 64
DUO = 2 * COLS
DUOS = MEM // 2
EDGE = 3
STRIP = 18
PAIRS = STRIP // 2
SELF = 1.0 / 6.0
SCALE = 0.24**3 / (MEM - 1)
VMEM = 20 * 1024 * 1024
MOST = 58 * 1024 * 1024
ALL = 63 * 1024 * 1024


def split(value, count):
    parts = []
    for _ in range(count - 1):
        top = value.astype(BF16)
        parts.append(top)
        value = value - top.astype(F32)
    parts.append(value.astype(BF16))
    return parts


def dot(a, b):
    return lax.dot_general(a, b, (((1,), (0,)), ((), ())), preferred_element_type=F32)


def dot_nt(a, b):
    return lax.dot_general(a, b, (((1,), (1,)), ((), ())), preferred_element_type=F32)


def iota(shape, dim):
    return lax.broadcasted_iota(I32, shape, dim)


def one_hot(test):
    return jnp.where(test, 1.0, 0.0).astype(BF16)


def params(limit=VMEM):
    return pltpu.CompilerParams(vmem_limit_bytes=limit)


def cost(flops, moved):
    return pl.CostEstimate(flops=flops, bytes_accessed=moved, transcendentals=0)


def pack_kernel(
    count, dual_far, col_far, lev_far, vertical_far, out, tgt_out, rank_out, weights, left, right, dual, col, lev, vertical, sem
):
    pairs = ((col_far, col), (lev_far, lev), (dual_far, dual), (vertical_far, vertical))
    copies = [pltpu.make_async_copy(a, b, sem.at[i]) for i, (a, b) in enumerate(pairs)]
    for copy in copies:
        copy.start()
    for copy in copies:
        copy.wait()
    wide = jnp.concatenate([vertical[...], jnp.zeros((LEV, PAD - LEV), F32)], axis=1)
    high, low = split(jnp.concatenate([wide, jnp.zeros((PAD - LEV, PAD), F32)], axis=0), 2)
    both = jnp.concatenate([low, jnp.zeros_like(low)], axis=1)
    weights[...] = jnp.concatenate([jnp.concatenate([high, high], axis=1), both], axis=0)
    number = count[0]
    lane = iota((DEV, COLS), 1)
    upper = one_hot((lane > iota((DEV, COLS), 0)) | (lane >= HALF))
    rows = iota((DEV, HALF), 0)
    lane = iota((1, HALF), 1)
    carry = jnp.zeros((DEV, HALF), F32)
    for i in range(SLOTS // HALF):
        at = slice(i * HALF, (i + 1) * HALF)
        column = col[i : i + 1, :]
        row = column >> 12
        gcol = column & 4095
        y = gcol & 255
        y = ((y & 3) << 6) + (y >> 2)
        target = ((row >> 4) << 4) + (gcol >> 8)
        target = jnp.where(i * HALF + lane < number, target, -1)
        hit = rows == target
        both = dot(one_hot(hit), upper)
        rank = jnp.sum(jnp.where(hit, both[:, :HALF] + carry, 0.0), axis=0, keepdims=True)
        carry = carry + both[:, HALF:]
        tgt_out[i : i + 1, :] = target
        rank = rank.astype(I32)
        rank_out[i : i + 1, :] = rank
        right[:, at] = one_hot(rows == rank)
        values = dual[i : i + 1, :]
        for p, piece in enumerate(split(values, 3)):
            left[p * DEV : (p + 1) * DEV, at] = jnp.where(hit, piece.astype(F32), 0.0).astype(BF16)
        cells = (lev[i : i + 1, :] << 12, (row & 15) << 8, y + 1)
        for p, piece in enumerate(cells):
            left[(p + 3) * DEV : (p + 4) * DEV, at] = jnp.where(hit, piece.astype(F32), 0.0).astype(BF16)
    both = dot_nt(left[...], right[...])
    part = [both[p * DEV : (p + 1) * DEV] for p in range(6)]
    out[...] = ((part[0] + part[1]) + part[2]) + pltpu.roll((part[3] + part[4]) + part[5], CAP, 1)


def pack(count, dual, col, lev, vertical):
    spec = pl.BlockSpec(memory_space=pltpu.VMEM)
    return pl.pallas_call(
        pack_kernel,
        name="pack",
        out_shape=(
            jax.ShapeDtypeStruct((DEV, HALF), F32),
            jax.ShapeDtypeStruct((SLOTS // HALF, HALF), I32),
            jax.ShapeDtypeStruct((SLOTS // HALF, HALF), I32),
            jax.ShapeDtypeStruct((2 * PAD, 2 * PAD), BF16),
        ),
        in_specs=[pl.BlockSpec(memory_space=pltpu.SMEM)] + [pl.BlockSpec(memory_space=pltpu.HBM)] * 4,
        out_specs=(spec,) * 4,
        scratch_shapes=[pltpu.VMEM((6 * DEV, SLOTS), BF16), pltpu.VMEM((DEV, SLOTS), BF16)]
        + [pltpu.VMEM((SLOTS // HALF, HALF), kind) for kind in (F32, I32, I32)]
        + [pltpu.VMEM((LEV, LEV), F32), pltpu.SemaphoreType.DMA((4,))],
        compiler_params=params(ALL),
        cost_estimate=cost(10**9, 10**6),
    )(count, dual.reshape(-1, HALF), col.reshape(-1, HALF), lev.reshape(-1, HALF), vertical)


def unpack_kernel(back, tgt, rank, out):
    rows = iota((DEV, HALF), 0)
    table = jnp.concatenate(split(back[...], 3), axis=0)
    for i in range(SLOTS // HALF):
        found = dot(table, one_hot(rows == rank[i : i + 1, :]))
        found = (found[:DEV] + found[DEV : 2 * DEV]) + found[2 * DEV :]
        out[i : i + 1, :] = jnp.sum(jnp.where(rows == tgt[i : i + 1, :], found, 0.0), axis=0, keepdims=True)


def unpack(back, tgt, rank):
    spec = pl.BlockSpec(memory_space=pltpu.VMEM)
    return pl.pallas_call(
        unpack_kernel,
        name="unpack",
        out_shape=jax.ShapeDtypeStruct((SLOTS // HALF, HALF), F32),
        in_specs=[spec] * 3,
        out_specs=spec,
        compiler_params=params(),
        cost_estimate=cost(10**8, 10**5),
    )(back, tgt, rank).reshape(SLOTS)


def strip_place(lane, members=MEM):
    j = lane % HALF
    return j // PAIRS, jnp.where(j < members * PAIRS, j % PAIRS * 2 + lane // HALF, -1)


def natural(place):
    return ((place & 63) << 2) + (place >> 6)


def duo_place(place):
    return ((place & 63) << 2) + (place >> 7), (place >> 6) & 1


def widen(value):
    low = iota((value.shape[0], HALF), 1) < QUARTER
    phases = []
    for half in (value[:, :HALF], value[:, HALF:]):
        turned = pltpu.roll(half, QUARTER, 1)
        phases += [jnp.where(low, half, turned), jnp.where(low, turned, half)]
    return jnp.concatenate(phases, axis=1)


def fold(value):
    low = iota((value.shape[0], HALF), 1) < QUARTER
    p = [value[:, i * HALF : (i + 1) * HALF] for i in range(4)]
    return jnp.concatenate(
        [jnp.where(low, p[i], p[i + 1]) + pltpu.roll(jnp.where(low, p[i + 1], p[i]), QUARTER, 1) for i in (0, 2)],
        axis=1,
    )


def arrange_kernel(
    ens, out, up, down, strip, side_l, side_r, taken, rows, turned_out, up_out, down_out, strip_acc, perm_y, perm_r, sides_out, sem, sem_out
):
    def fetch(k):
        return pltpu.make_async_copy(ens.at[k], taken.at[k], sem.at[k])

    def send(duo):
        slot = duo % 2
        return (
            pltpu.make_async_copy(turned_out.at[slot], out.at[duo], sem_out.at[0, slot]),
            pltpu.make_async_copy(up_out.at[slot], up.at[duo], sem_out.at[1, slot]),
            pltpu.make_async_copy(down_out.at[slot], down.at[duo], sem_out.at[2, slot]),
        )

    for k in range(MEM):
        fetch(k).start()
    rows[LEV * ROWS :, :] = jnp.zeros((rows.shape[0] - LEV * ROWS, DUO), BF16)
    strip_acc[...] = jnp.zeros_like(strip_acc)
    y, which = duo_place(iota((1, DUO), 1))
    perm_y[...] = one_hot(iota((DUO, DUO), 0) == which * COLS + y)
    i = iota((256, 1), 0)
    perm_r[...] = one_hot(iota((256, 256), 1) == (i & 15) * 16 + (i >> 4))

    @pl.loop(0, DUOS)
    def _(duo):
        @pl.when(duo >= 2)
        def _():
            for copy in send(duo - 2):
                copy.wait()

        fetch(2 * duo).wait()
        fetch(2 * duo + 1).wait()
        here, there, slot = 2 * duo, 2 * duo + 1, duo % 2
        lane = iota((COLS, COLS), 0)
        y, which = jnp.where(lane % HALF < QUARTER, lane % HALF, lane % HALF + HALF), lane // HALF
        member, c = strip_place(iota((1, COLS), 1))
        want = jnp.where(y < 6, 3 + y, jnp.where(y >= 250, y - 241, -2))
        select = one_hot((member == 2 * duo + which) & (c == want))
        outside = iota((LEV * ROWS, HALF), 1) < QUARTER
        ends = [jnp.where(outside, taken[k, :, :HALF], taken[k, :, HALF:]) for k in (here, there)]
        block = jnp.concatenate([taken[here], taken[there]], axis=1)
        rows[: LEV * ROWS, :] = dot(block, perm_y[...]).astype(BF16)
        for b in range(6):
            turned = dot(perm_r[...], rows[b * 256 : (b + 1) * 256, :])
            at = slice(b * 16, (b + 1) * 16)
            for x in range(ROWS):
                part = turned[x * 16 : (x + 1) * 16, :]
                turned_out[slot, x, at, :] = part.astype(BF16)
                if x < EDGE:
                    up_out[slot, x, at, :] = part
                if x >= ROWS - EDGE:
                    down_out[slot, x - (ROWS - EDGE), at, :] = part
        for copy in send(duo):
            copy.start()
        strip_acc[: LEV * ROWS, :] += dot(jnp.concatenate(ends, axis=1), select)

    member, c = strip_place(iota((COLS, COLS), 0))
    for b in range(6):
        turned = dot(perm_r[...], strip_acc[b * 256 : (b + 1) * 256, :].astype(BF16)).astype(BF16)
        for x in range(ROWS):
            strip[x, b * 16 : (b + 1) * 16, :] = turned[x * 16 : (x + 1) * 16, :]
    left, right = (c >= 3) & (c < 6), (c >= 12) & (c < 15)
    spot = jnp.where(left, 3 * member + c - 3, jnp.where(right, HALF + 3 * member + c - 12, -1000))
    places = [one_hot(iota((COLS, COLS), 1) == spot + 30 * j) for j in range(4)]
    for group in range(4):
        sides = jnp.zeros((PAD, COLS), F32)
        for j in range(4):
            sides = sides + dot(strip[group * 4 + j], places[j])
        sides_out[0, group] = sides[:, :HALF]
        sides_out[1, group] = sides[:, HALF:]
    copies = [
        pltpu.make_async_copy(sides_out.at[i], side.at[pl.ds(0, 4)], sem_out.at[3, i]) for i, side in enumerate((side_l, side_r))
    ]
    for copy in copies:
        copy.start()
    for duo in (DUOS - 2, DUOS - 1):
        for copy in send(duo):
            copy.wait()
    for copy in copies:
        copy.wait()


def arrange(ensemble):
    spec, far = pl.BlockSpec(memory_space=pltpu.VMEM), pl.BlockSpec(memory_space=pltpu.HBM)
    return pl.pallas_call(
        arrange_kernel,
        name="arrange",
        out_shape=(
            jax.ShapeDtypeStruct((DUOS, ROWS, PAD, DUO), BF16),
            jax.ShapeDtypeStruct((DUOS, EDGE, PAD, DUO), F32),
            jax.ShapeDtypeStruct((DUOS, EDGE, PAD, DUO), F32),
            jax.ShapeDtypeStruct((ROWS, PAD, COLS), BF16),
            jax.ShapeDtypeStruct((5, PAD, HALF), F32),
            jax.ShapeDtypeStruct((5, PAD, HALF), F32),
        ),
        in_specs=[far],
        out_specs=(far, far, far, spec, far, far),
        scratch_shapes=[
            pltpu.VMEM((MEM, LEV * ROWS, COLS), BF16),
            pltpu.VMEM((PAD * ROWS, DUO), BF16),
            pltpu.VMEM((2, ROWS, PAD, DUO), BF16),
            pltpu.VMEM((2, EDGE, PAD, DUO), F32),
            pltpu.VMEM((2, EDGE, PAD, DUO), F32),
            pltpu.VMEM((ROWS * PAD, COLS), F32),
            pltpu.VMEM((DUO, DUO), BF16),
            pltpu.VMEM((256, 256), BF16),
            pltpu.VMEM((2, 4, PAD, HALF), F32),
            pltpu.SemaphoreType.DMA((MEM,)),
            pltpu.SemaphoreType.DMA((4, 2)),
        ],
        compiler_params=params(MOST),
        cost_estimate=cost(10**10, 25 * 10**6),
    )(ensemble.reshape(MEM, LEV * ROWS, COLS))


CHUNKS = CAP // 2
TILES = CHUNKS + ROWS
SPACE = 48


def scatter_kernel(
    incoming, ens_l, ens_r, out, wide, side_l, side_r, level_out, column_out, pos_out, row_out,
    turned, hot, left, right, rows_of, sorted_, sides_out, sem
):
    turned[...] = incoming[...].T
    pairs = [[turned[pl.ds(first + i, CHUNKS, stride=2), :] for i in range(2)] for first in (0, CAP)]
    values = jnp.concatenate(pairs[0], axis=1)
    cells = jnp.concatenate(pairs[1], axis=1).astype(I32) - 1
    full = cells >= 0
    x = jnp.where(full, (cells >> 8) & 15, 99)

    for c in range(CHUNKS):
        hot[c * ROWS : (c + 1) * ROWS, :] = one_hot(iota((ROWS, COLS), 0) == x[c : c + 1, :])
    lane = iota((COLS, COLS + HALF), 1)
    both = dot(hot[...], one_hot((lane > iota((COLS, COLS + HALF), 0)) | (lane >= COLS)))
    before = jnp.zeros((ROWS, HALF), F32)
    earlier = []
    for c in range(CHUNKS):
        earlier.append(before)
        before = before + both[c * ROWS : (c + 1) * ROWS, COLS:]
    needed = ((before.astype(I32) + 255) >> 8).astype(F32).astype(BF16)
    start = dot(one_hot(iota((ROWS, ROWS), 1) < iota((ROWS, ROWS), 0)), needed)
    lines = []
    for c in range(CHUNKS):
        base = start * 256.0 + earlier[c]
        spots = both[c * ROWS : (c + 1) * ROWS, :COLS] + jnp.concatenate([base, base], axis=1)
        spots = jnp.where(iota((ROWS, COLS), 0) == x[c : c + 1, :], spots, 0.0)
        lines.append(jnp.sum(spots, axis=0, keepdims=True))
    pos = jnp.concatenate(lines, axis=0).astype(I32)
    pos = jnp.where(full, pos, -1)
    pos_out[...] = pos
    begun = jnp.where(start[:ROWS].astype(I32) <= iota((ROWS, HALF), 1), 1.0, 0.0)
    row_out[...] = jnp.sum(begun, axis=0, keepdims=True).astype(I32) - 1
    copy = pltpu.make_async_copy(row_out, rows_of, sem.at[0])
    copy.start()

    parts = [p.astype(F32) for p in split(values, 2)] + [(cells >> 12).astype(F32), (cells & 255).astype(F32)]
    tile, spot = pos >> 8, pos & 255
    for c in range(CHUNKS):
        at = slice(c * COLS, (c + 1) * COLS)
        hit = iota((SPACE, COLS), 0) == tile[c : c + 1, :]
        for p, part in enumerate(parts):
            left[p * SPACE : (p + 1) * SPACE, at] = jnp.where(hit, part[c : c + 1, :], 0.0).astype(BF16)
        right[:, at] = one_hot(iota((COLS, COLS), 0) == spot[c : c + 1, :])
    sorted_[...] = dot_nt(left[...], right[...])
    level_out[...] = sorted_[2 * SPACE : 3 * SPACE, :]
    column_out[...] = sorted_[3 * SPACE :, :]
    out[...] = jnp.zeros_like(out)
    copy.wait()

    @pl.loop(0, TILES // 8)
    def _(j):
        high, low, level, column = (sorted_[pl.ds(pl.multiple_of(p * SPACE + j * 8, 8), 8), :] for p in range(4))
        level, column = level.astype(I32), column.astype(I32)
        for half in range(2):
            results = []
            for q in range(half * 4, half * 4 + 4):
                at = slice(q, q + 1)
                hit = iota((PAD, COLS), 0) == level[at, :]
                lhs = jnp.concatenate([jnp.where(hit, high[at, :], 0.0), jnp.where(hit, low[at, :], 0.0)], axis=0)
                both = dot_nt(lhs.astype(BF16), one_hot(iota((COLS, COLS), 0) == column[at, :]))
                results.append(both[:PAD] + both[PAD:])
            for i, result in enumerate(results):
                out[rows_of[0, j * 8 + half * 4 + i]] += result

    y = natural(iota((COLS, COLS), 0))
    lane = iota((COLS, COLS), 1)
    place = jnp.where(y < 3, y, jnp.where(y >= 253, HALF + y - 253, -1000))
    packed = jnp.zeros((PAD, COLS), F32)
    for x in range(ROWS):
        select = one_hot(lane == place + 3 * x)
        for piece in split(out[x], 2):
            packed = packed + dot(piece, select)
    sides_out[0] = packed[:, :HALF]
    sides_out[1] = packed[:, HALF:]
    copies = [pltpu.make_async_copy(sides_out.at[i], side.at[4], sem.at[i]) for i, side in enumerate((side_l, side_r))]
    for copy in copies:
        copy.start()
    for x in range(ROWS):
        wide[x] = widen(out[x])
    for copy in copies:
        copy.wait()


def scatter(incoming, ens_l, ens_r):
    spec, far = pl.BlockSpec(memory_space=pltpu.VMEM), pl.BlockSpec(memory_space=pltpu.HBM)
    return pl.pallas_call(
        scatter_kernel,
        name="scatter",
        out_shape=(
            jax.ShapeDtypeStruct((ROWS, PAD, COLS), F32),
            jax.ShapeDtypeStruct((ROWS, PAD, DUO), F32),
            jax.ShapeDtypeStruct((5, PAD, HALF), F32),
            jax.ShapeDtypeStruct((5, PAD, HALF), F32),
            jax.ShapeDtypeStruct((SPACE, COLS), F32),
            jax.ShapeDtypeStruct((SPACE, COLS), F32),
            jax.ShapeDtypeStruct((CHUNKS, COLS), I32),
            jax.ShapeDtypeStruct((1, HALF), I32),
        ),
        in_specs=[spec, far, far],
        out_specs=(spec, spec, far, far, spec, spec, spec, spec),
        input_output_aliases={1: 2, 2: 3},
        scratch_shapes=[
            pltpu.VMEM((HALF, DEV), F32),
            pltpu.VMEM((CHUNKS * ROWS, COLS), BF16),
            pltpu.VMEM((4 * SPACE, CHUNKS * COLS), BF16),
            pltpu.VMEM((COLS, CHUNKS * COLS), BF16),
            pltpu.SMEM((1, HALF), I32),
            pltpu.VMEM((4 * SPACE, COLS), F32),
            pltpu.VMEM((2, PAD, HALF), F32),
            pltpu.SemaphoreType.DMA((2,)),
        ],
        compiler_params=params(),
        cost_estimate=cost(10**10, 2 * 10**6),
    )(incoming, ens_l, ens_r)


def strips_kernel(strip, adjoint, left, right, ens_out, out, up, down):
    lane = iota((COLS, COLS), 1)
    member, member_c = strip_place(lane, MEM + 1)
    y = natural(iota((COLS, COLS), 0))
    own = one_hot(member_c == jnp.where(y < 6, 3 + y, jnp.where(y >= 250, y - 241, -2)))
    from_lane = iota((HALF, COLS), 0)
    member_c, member = member_c[:HALF], member[:HALF]
    pieces = [split(side[4], 2) for side in (left, right)]
    ens_lanes = iota((PAD, COLS), 1) % HALF < MEM * PAIRS
    for x in range(ROWS):
        ens_value = strip[x].astype(F32)
        first = x % 4 * 30 + 3 * member
        for side, shift in ((left, 0), (right, 15)):
            inside = (member_c >= shift) & (member_c < shift + 3) & (member < MEM)
            spot = one_hot(inside & (from_lane == first + member_c - shift))
            ens_value = ens_value + dot(side[x // 4].astype(BF16), spot)
        ens_out[x] = ens_value.astype(BF16)
        value = jnp.zeros((PAD, COLS), F32)
        for piece in split(adjoint[x], 2):
            value = value + dot(piece, own)
        for side, shift in ((pieces[0], 0), (pieces[1], 15)):
            inside = (member_c >= shift) & (member_c < shift + 3)
            spot = one_hot(inside & (from_lane == 3 * x + member_c - shift))
            for piece in side:
                value = value + dot(piece, spot)
        out[x] = value
        for target, start in ((up, 0), (down, ROWS - EDGE)):
            if start <= x < start + EDGE:
                target[0, x - start] = adjoint[x]
                target[1, x - start] = jnp.where(ens_lanes, ens_value, value)


def strips(strip, adjoint, left, right):
    spec = pl.BlockSpec(memory_space=pltpu.VMEM)
    return pl.pallas_call(
        strips_kernel,
        name="strips",
        out_shape=(
            jax.ShapeDtypeStruct((ROWS, PAD, COLS), BF16),
            jax.ShapeDtypeStruct((ROWS, PAD, COLS), F32),
            jax.ShapeDtypeStruct((2, EDGE, PAD, COLS), F32),
            jax.ShapeDtypeStruct((2, EDGE, PAD, COLS), F32),
        ),
        in_specs=[spec] * 4,
        out_specs=(spec,) * 4,
        compiler_params=params(),
        cost_estimate=cost(10**9, 4 * 10**6),
    )(strip, adjoint, left, right)


def beside_permuted(value):
    even, odd = value[:, :HALF], value[:, HALF:]
    return jnp.concatenate([odd + pltpu.roll(odd, 1, 1), even + pltpu.roll(even, HALF - 1, 1)], axis=1)


def beside_duo(value):
    p = [value[:, i * HALF : (i + 1) * HALF] for i in range(4)]
    return jnp.concatenate(
        [pltpu.roll(p[3], 1, 1) + p[1], p[0] + p[2], p[1] + p[3], p[2] + pltpu.roll(p[0], HALF - 1, 1)], axis=1
    )


def total(terms):
    result = None
    for term in terms:
        if term is not None:
            result = term if result is None else result + term
    return result


def diffuse(get, given, wanted, beside, emit, mask=None):
    rows = [{} for _ in range(EDGE + 1)]
    for x in range(min(wanted) - EDGE, max(wanted) + EDGE + 1):
        if x in given:
            rows[0][x] = get(x)
        for step in range(1, EDGE + 1):
            at, reach, older = x - step, EDGE - step, rows[step - 1]
            if not min(wanted) - reach <= at <= max(wanted) + reach:
                continue
            terms = [older.get(at - 1), older.get(at + 1)]
            if at in older:
                terms += [beside(older[at]), older[at] * SELF]
            value = total(terms)
            if value is None:
                continue
            if step == EDGE:
                emit(at, value)
            else:
                rows[step][at] = value if mask is None else mask(at, value)


def put_split(ref, index, at, value):
    top = value.astype(BF16)
    ref[index, at, :] = top
    ref[index, pl.ds(at.start + PAD, 16), :] = (value - top.astype(F32)).astype(BF16)


def mix(weights, field):
    both = dot(weights, field)
    return both[:PAD] + both[PAD:]


INNER = ROWS - 2 * EDGE


def inner_kernel(start, count, ens, adj, weights, place, *refs):
    border, out, field, first, taken, sem = refs[-6:]

    def fetch(step):
        return pltpu.make_async_copy(ens.at[start + step], taken.at[step % 2], sem.at[step % 2])

    fetch(0).start()
    out[...] = refs[0][...] if start else jnp.zeros_like(out)
    top_open = jnp.where(place[0] == 0, 0.0, 1.0)
    bottom_open = jnp.where(place[0] == place[2], 0.0, 1.0)

    def mask(x, value):
        if x < 0:
            return value * top_open
        if x >= ROWS:
            return value * bottom_open
        return value

    @pl.loop(0, count)
    def _(step):
        @pl.when(step < count - 1)
        def _():
            fetch(step + 1).start()

        fetch(step).wait()
        slot = step % 2

        @pl.loop(0, PAD // 16)
        def _(group):
            at = pl.ds(pl.multiple_of(group * 16, 16), 16)

            for part in range(2):
                eight = pl.ds(pl.multiple_of(group * 16 + part * 8, 8), 8)

                def get(x):
                    return taken[slot, x, at, :].astype(F32)[part * 8 : part * 8 + 8, :] * adj[x, eight, :]

                def emit(x, value):
                    if not EDGE <= x < ROWS - EDGE:
                        border[step, x if x < EDGE else x - INNER, eight, :] = value
                    elif part == 0:
                        first[x - EDGE] = value
                    else:
                        put_split(field, x - EDGE, at, jnp.concatenate([first[x - EDGE], value], axis=0))

                diffuse(get, range(ROWS), range(ROWS), beside_duo, emit, mask)

        for x in range(INNER):
            out[x] += taken[slot, x + EDGE].astype(F32) * mix(weights[...], field[x])


def inner(ens, adj, weights, place, start, count, before=()):
    spec, far = pl.BlockSpec(memory_space=pltpu.VMEM), pl.BlockSpec(memory_space=pltpu.HBM)
    return pl.pallas_call(
        lambda *refs: inner_kernel(start, count, *refs),
        name="inner",
        out_shape=(
            jax.ShapeDtypeStruct((count, 2 * EDGE, PAD, DUO), F32),
            jax.ShapeDtypeStruct((INNER, PAD, DUO), F32),
        ),
        in_specs=[far, spec, spec, pl.BlockSpec(memory_space=pltpu.SMEM)] + [spec] * len(before),
        out_specs=(spec,) * 2,
        scratch_shapes=[
            pltpu.VMEM((INNER, 2 * PAD, DUO), BF16),
            pltpu.VMEM((INNER, 8, DUO), F32),
            pltpu.VMEM((2, ROWS, PAD, DUO), BF16),
            pltpu.SemaphoreType.DMA((2,)),
        ],
        compiler_params=params(),
        cost_estimate=cost(count * 2 * 10**9, count * 2 * 10**6),
    )(ens, adj, weights, place, *before)


def outer_kernel(
    ens, halo_t, halo_b, adj_t, adj_b, border0, border1, weights, out, field, first, wide, taken_e, taken_h, sem
):
    def fetch(duo):
        slot = duo % 2
        copies = (
            (ens.at[duo, pl.ds(0, EDGE)], taken_e.at[slot, pl.ds(0, EDGE)]),
            (ens.at[duo, pl.ds(ROWS - EDGE, EDGE)], taken_e.at[slot, pl.ds(EDGE, EDGE)]),
            (halo_t.at[duo], taken_h.at[slot, pl.ds(0, EDGE)]),
            (halo_b.at[duo], taken_h.at[slot, pl.ds(EDGE, EDGE)]),
        )
        return [pltpu.make_async_copy(a, b, sem.at[i, slot]) for i, (a, b) in enumerate(copies)]

    for copy in fetch(0):
        copy.start()
    out[...] = jnp.zeros_like(out)
    for x in range(EDGE):
        wide[x] = widen(adj_t[0, x])
        wide[EDGE + x] = widen(adj_b[0, x])

    for border, start in ((border0, 0), (border1, FIRST)):

        @pl.loop(0, border.shape[0])
        def _(step):
            duo = start + step
            slot = duo % 2

            @pl.when(duo < DUOS - 1)
            def _():
                for copy in fetch(duo + 1):
                    copy.start()

            for copy in fetch(duo):
                copy.wait()

            @pl.loop(0, PAD // 16, unroll=True)
            def _(group):
                at = pl.ds(pl.multiple_of(group * 16, 16), 16)

                for part in range(2):
                    eight = pl.ds(pl.multiple_of(group * 16 + part * 8, 8), 8)

                    def emit(x, value):
                        value = value + border[step, x, eight, :]
                        if part == 0:
                            first[x] = value
                        else:
                            put_split(field, x, at, jnp.concatenate([first[x], value], axis=0))

                    def get_t(x):
                        return taken_h[slot, x + EDGE, eight, :] * wide[x + EDGE, eight, :]

                    def get_b(x):
                        return taken_h[slot, x - EDGE, eight, :] * wide[x - EDGE, eight, :]

                    diffuse(get_t, range(-EDGE, 0), range(EDGE), beside_duo, emit)
                    diffuse(get_b, range(2 * EDGE, 3 * EDGE), range(EDGE, 2 * EDGE), beside_duo, emit)

            for x in range(2 * EDGE):
                out[x] += taken_e[slot, x].astype(F32) * mix(weights[...], field[x])


def outer(ens, halo_t, halo_b, adj_t, adj_b, border0, border1, weights):
    spec, far = pl.BlockSpec(memory_space=pltpu.VMEM), pl.BlockSpec(memory_space=pltpu.HBM)
    return pl.pallas_call(
        outer_kernel,
        name="outer",
        out_shape=jax.ShapeDtypeStruct((2 * EDGE, PAD, DUO), F32),
        in_specs=[far] * 3 + [spec] * 5,
        out_specs=spec,
        scratch_shapes=[
            pltpu.VMEM((2 * EDGE, 2 * PAD, DUO), BF16),
            pltpu.VMEM((2 * EDGE, 8, DUO), F32),
            pltpu.VMEM((2 * EDGE, PAD, DUO), F32),
            pltpu.VMEM((2, 2 * EDGE, PAD, DUO), BF16),
            pltpu.VMEM((2, 2 * EDGE, PAD, DUO), F32),
            pltpu.SemaphoreType.DMA((4, 2)),
        ],
        compiler_params=params(),
        cost_estimate=cost(MEM * 10**9, MEM * 3 * 10**6),
    )(ens, halo_t, halo_b, adj_t, adj_b, border0, border1, weights)


def edge_kernel(strip, adj, halo_t, halo_b, weights, place, inside, border, out, field, halo_adj):
    top_open = jnp.where(place[0] == 0, 0.0, 1.0)
    bottom_open = jnp.where(place[0] == place[2], 0.0, 1.0)
    left_open = jnp.where(place[1] == 0, 0.0, 1.0)
    right_open = jnp.where(place[1] == place[3], 0.0, 1.0)
    member, source = strip_place(iota((COLS, COLS), 0), MEM + 1)
    target = strip_place(iota((COLS, COLS), 1))[1]
    repeat = one_hot((member == MEM) & (source == target))
    for i, halo in enumerate((halo_t, halo_b)):
        for x in range(EDGE):
            high, low = split(halo[1, x], 2)
            halo_adj[i * EDGE + x] = dot(high, repeat) + dot(low, repeat)

    @pl.loop(0, PAD // 16)
    def _(group):
        at = pl.ds(pl.multiple_of(group * 16, 16), 16)
        c = strip_place(iota((16, COLS), 1))[1]
        lanes = jnp.where(c < 3, left_open, jnp.where(c >= 15, right_open, 1.0))

        def mask(x, value):
            value = value * lanes
            if x < 0:
                return value * top_open
            if x >= ROWS:
                return value * bottom_open
            return value

        def get(x):
            if x < 0:
                return halo_t[1, x + EDGE, at, :] * halo_adj[x + EDGE, at, :]
            if x >= ROWS:
                return halo_b[1, x - ROWS, at, :] * halo_adj[x - ROWS + EDGE, at, :]
            return strip[x, at, :].astype(F32) * adj[x, at, :]

        def emit(x, value):
            put_split(field, x, at, value)

        diffuse(get, range(-EDGE, ROWS + EDGE), range(ROWS), beside_permuted, emit, mask)

    c = strip_place(iota((COLS, COLS), 0))[1]
    spot = jnp.where((c >= 3) & (c < 6), c - 3, jnp.where((c >= 12) & (c < 15), 241 + c, -1))
    collect = one_hot(spot == natural(iota((COLS, COLS), 1)))
    y = natural(iota((PAD, COLS), 1))
    middle = (y >= EDGE) & (y < COLS - EDGE)
    for x in range(ROWS):
        if EDGE <= x < ROWS - EDGE:
            value = inside[x - EDGE]
        else:
            value = border[x if x < EDGE else x - INNER]
        value = jnp.where(middle, fold(value), 0.0)
        product = strip[x].astype(F32) * mix(weights[...], field[x])
        for piece in split(product, 2):
            value = value + dot(piece, collect)
        out[x] = value * SCALE


def edge(strip, adj, halo_t, halo_b, weights, place, inside, border):
    spec = pl.BlockSpec(memory_space=pltpu.VMEM)
    return pl.pallas_call(
        edge_kernel,
        name="edge",
        out_shape=jax.ShapeDtypeStruct((ROWS, PAD, COLS), F32),
        in_specs=[spec] * 5 + [pl.BlockSpec(memory_space=pltpu.SMEM)] + [spec] * 2,
        out_specs=spec,
        scratch_shapes=[pltpu.VMEM((ROWS, 2 * PAD, COLS), BF16), pltpu.VMEM((2 * EDGE, PAD, COLS), F32)],
        compiler_params=params(),
        cost_estimate=cost(4 * 10**9, 8 * 10**6),
    )(strip, adj, halo_t, halo_b, weights, place, inside, border)


def gather_kernel(field, level, column, pos, rows_of, out, table, picked):
    for x in range(ROWS):
        table[x, :PAD, :], table[x, PAD:, :] = split(field[x], 2)
    picked[...] = jnp.zeros_like(picked)

    @pl.loop(0, TILES // 8)
    def _(j):
        first = pl.multiple_of(j * 8, 8)
        levels, columns = level[pl.ds(first, 8), :].astype(I32), column[pl.ds(first, 8), :].astype(I32)
        lines = []
        for q in range(8):
            at = slice(q, q + 1)
            found = dot(table[rows_of[0, j * 8 + q]], one_hot(iota((COLS, COLS), 0) == columns[at, :]))
            found = jnp.where(iota((PAD, COLS), 0) == levels[at, :], found[:PAD] + found[PAD:], 0.0)
            lines.append(jnp.sum(found, axis=0, keepdims=True))
        picked[pl.ds(first, 8), :] = jnp.concatenate(lines, axis=0)

    both = jnp.concatenate(split(picked[...], 2), axis=0)
    tile, spot = pos[...] >> 8, pos[...] & 255
    lines = []
    for c in range(CHUNKS):
        found = dot(both, one_hot(iota((COLS, COLS), 0) == spot[c : c + 1, :]))
        found = jnp.where(iota((SPACE, COLS), 0) == tile[c : c + 1, :], found[:SPACE] + found[SPACE:], 0.0)
        found = jnp.sum(found, axis=0, keepdims=True)
        lines += [found[:, :HALF], found[:, HALF:]]
    out[...] = jnp.concatenate(lines + [jnp.zeros((HALF - CAP, DEV), F32)], axis=0).T


def gather(field, level, column, pos, rows_of):
    spec = pl.BlockSpec(memory_space=pltpu.VMEM)
    return pl.pallas_call(
        gather_kernel,
        name="gather",
        out_shape=jax.ShapeDtypeStruct((DEV, HALF), F32),
        in_specs=[spec] * 4 + [pl.BlockSpec(memory_space=pltpu.SMEM)],
        out_specs=spec,
        scratch_shapes=[
            pltpu.VMEM((ROWS, 2 * PAD, COLS), BF16),
            pltpu.VMEM((SPACE, COLS), F32),
        ],
        compiler_params=params(),
        cost_estimate=cost(10**10, 2 * 10**6),
    )(field, level, column, pos, rows_of)


def restore_kernel(field, out, rows):
    perm_y = one_hot(natural(iota((COLS, COLS), 0)) == iota((COLS, COLS), 1))
    i = iota((256, 1), 0)
    perm_r = one_hot(iota((256, 256), 1) == (i & 15) * 16 + (i >> 4))
    for x in range(ROWS):
        value = field[x]
        high, low = split(value, 2)
        rows[x] = dot(high, perm_y) + dot(low, perm_y)
    for b in range(6):
        block = jnp.concatenate([rows[x, b * 16 : (b + 1) * 16, :] for x in range(ROWS)], axis=0)
        high, low = split(block, 2)
        value = dot(perm_r, high) + dot(perm_r, low)
        if b < 5:
            out[b * 256 : (b + 1) * 256, :] = value
        else:
            out[1280:1440, :] = value[:160]


def restore(field):
    spec = pl.BlockSpec(memory_space=pltpu.VMEM)
    return pl.pallas_call(
        restore_kernel,
        name="restore",
        out_shape=jax.ShapeDtypeStruct((LEV * ROWS, COLS), F32),
        in_specs=[spec],
        out_specs=spec,
        scratch_shapes=[pltpu.VMEM((ROWS, PAD, COLS), F32)],
        compiler_params=params(),
        cost_estimate=cost(10**9, 3 * 10**6),
    )(field).reshape(LEV, ROWS, COLS)


def forward(value, axis):
    size = lax.axis_size(axis)
    return lax.ppermute(value, axis, [(i, i + 1) for i in range(size - 1)])


def backward(value, axis):
    size = lax.axis_size(axis)
    return lax.ppermute(value, axis, [(i + 1, i) for i in range(size - 1)])


FIRST = 2


def body(ensemble, vertical_weights, dual_vector, observed_column, observed_level, active_count):
    place = jnp.stack(
        [lax.axis_index("gx"), lax.axis_index("gy"), lax.axis_size("gx") - 1, lax.axis_size("gy") - 1]
    ).astype(I32)
    outgoing, target, rank, weights = pack(
        active_count, dual_vector, observed_column, observed_level, vertical_weights
    )
    ensemble, outgoing = lax.optimization_barrier((ensemble, outgoing))
    incoming = lax.all_to_all(outgoing, ("gx", "gy"), split_axis=0, concat_axis=0, tiled=True)
    ens, ens_up, ens_down, strip, ens_l, ens_r = arrange(ensemble)
    incoming, ens_up, ens_down = lax.optimization_barrier((incoming, ens_up, ens_down))
    halo_t = forward(ens_down, "gx")
    halo_b = backward(ens_up, "gx")

    adj, wide, side_l, side_r, *slots = scatter(incoming, ens_l, ens_r)
    from_left = forward(side_r, "gy")
    from_right = backward(side_l, "gy")
    border0, inside = inner(ens, wide, weights, place, 0, FIRST)
    from_left, from_right, inside = lax.optimization_barrier((from_left, from_right, inside))
    strip, adj_strip, up, down = strips(strip, adj, from_left, from_right)
    top = forward(down, "gx")
    bottom = backward(up, "gx")
    border1, inside = inner(ens, wide, weights, place, FIRST, DUOS - FIRST, (inside,))

    outside = outer(ens, halo_t, halo_b, top, bottom, border0, border1, weights)
    field = edge(strip, adj_strip, top, bottom, weights, place, inside, outside)
    picked = gather(field, *slots)
    back = lax.all_to_all(picked, ("gx", "gy"), split_axis=0, concat_axis=0, tiled=True)
    increment = restore(field)
    obs_product = unpack(back, target, rank)
    return (increment, obs_product)


def solution(mesh):
    placed = (
        P(None, None, "gx", "gy"),
        P(),
        P(("gx", "gy")),
        P(("gx", "gy")),
        P(("gx", "gy")),
        P(("gx", "gy")),
    )
    return jax.shard_map(
        body,
        mesh=mesh,
        in_specs=placed,
        out_specs=(P(None, "gx", "gy"), P(("gx", "gy"))),
        check_vma=False,
    )
```
